32 devices in a mesh: dp: 8 (over y, x, core), narrow: 4 (over z).
Axes of the slice: x: 2, y: 2, z: 4, core: 2. Of those that a mesh axis runs over, the one named last changes fastest.
Arguments:
- inputs: bfloat16 [16, 1152, 1024], P('dp', 'narrow'), may hold values from -6 to 6
- bucket: int32 [16], P('dp'), may hold values from 0 to 1, as said below
- attn_gain: bfloat16 [1024], P('dp'), may hold values from 0.5 to 1.5
- w_query: bfloat16 [1024, 1024], P('dp', 'narrow'), may hold values from -0.1875 to 0.1875
- w_key: bfloat16 [1024, 1024], P('dp', 'narrow'), may hold values from -0.1875 to 0.1875
- w_value: bfloat16 [1024, 1024], P('dp', 'narrow'), may hold values from -0.1875 to 0.1875
- w_out: bfloat16 [1024, 1024], P('narrow', 'dp'), may hold values from -6 to 6
- ffn_gain: bfloat16 [1024], P('dp'), may hold values from 0.5 to 1.5
- w_gate: bfloat16 [1024, 2816], P('dp', 'narrow'), may hold values from -0.1875 to 0.1875
- w_up: bfloat16 [1024, 2816], P('dp', 'narrow'), may hold values from -0.1875 to 0.1875
- w_down: bfloat16 [2816, 1024], P('narrow', 'dp'), may hold values from -0.109375 to 0.109375
- cotangent: bfloat16 [16, 1152, 1024], P('dp', 'narrow'), may hold values from -6 to 6
Outputs:
- outputs: bfloat16 [16, 1152, 1024], P('dp', 'narrow')
- input_grad: float32 [16, 1152, 1024], P('dp', 'narrow')
- attn_gain_grad: float32 [1024], P('dp')
- w_query_grad: float32 [1024, 1024], P('dp', 'narrow')
- w_key_grad: float32 [1024, 1024], P('dp', 'narrow')
- w_value_grad: float32 [1024, 1024], P('dp', 'narrow')
- w_out_grad: float32 [1024, 1024], P('narrow', 'dp')
- ffn_gain_grad: float32 [1024], P('dp')
- w_gate_grad: float32 [1024, 2816], P('dp', 'narrow')
- w_up_grad: float32 [1024, 2816], P('dp', 'narrow')
- w_down_grad: float32 [2816, 1024], P('narrow', 'dp')
The draws below stay inside these ranges and needn't reach their ends.
Inputs may be any that keep to these rules, and one draw needn't show every extreme that they name: `bucket`: 1 marks a group holding one row of 1152 positions (448 px), 0 a group of three rows of 384 positions (224 px); both kinds occur in every draw.
All inputs are finite; a program needn't handle non-finite values.
Results may differ from the reference program's by a relative error of at most 0.017.
Values may be sent and summed in bfloat16 or wider, within the bound.
No kernel may reach another device: no remote copies, remote signals or barrier semaphores. Data moves between devices by JAX's collectives and lax.ppermute only.
A program may use at most 256 MiB of HBM per device.

```python
import math
import jax
import jax.numpy as jnp
from jax import lax

D = 1024
HEADS = 16
HEAD = 64
FF = 2816
LONG = 1152
SHORT = 384
HH = 1024
GROUPS = 16


def draw_bucket(key, part):
    key = jax.random.fold_in(key, 7)
    key_base, key_first, key_step = jax.random.split(key, 3)
    base = jax.random.randint(key_base, (GROUPS,), 0, 2)
    first = jax.random.randint(key_first, (), 0, GROUPS)
    step = jax.random.randint(key_step, (), 1, GROUPS)
    second = (first + step) % GROUPS
    places = jnp.arange(GROUPS)
    chosen = jnp.where(places == first, 1, jnp.where(places == second, 0, base))
    return chosen.astype(jnp.int32)


def levels(own_key, dims, shards, least, high):
    level, own = 1.0, jax.random.fold_in(own_key, 6)
    for position, shards_of in shards:
        steps = jnp.exp(jax.random.uniform(jax.random.fold_in(own, position), (shards_of,), jnp.float32, least / len(shards), high / len(shards)))
        level = level * jnp.repeat(steps, dims[position] // shards_of).reshape([-1 if axis == position else 1 for axis in range(len(dims))])
    return level


def bell_draw(own_key, extent, spread, reach, cuts=(), kind=jnp.bfloat16):
    values = spread * jax.random.normal(own_key, extent, jnp.float32)
    if cuts:
        values = values * levels(own_key, extent, cuts, -0.22, 0.18)
    return jnp.clip(values, -reach, reach).astype(kind)


def setup_inputs(seed: int = 0) -> dict:
    streams_of = jax.random.split(jax.random.key(seed), 13)
    inputs = bell_draw(streams_of[0], (GROUPS, LONG, D), 1.0, 6.0, ((0, 8), (1, 4)))
    bucket = draw_bucket(jax.random.fold_in(streams_of[12], 71), 0)
    attn_gain = jnp.clip(1.0 + 0.1 * jax.random.normal(streams_of[2], (D,), jnp.float32), 0.5, 1.5).astype(jnp.bfloat16)
    w_query = bell_draw(streams_of[3], (D, HH), D ** -0.5, 0.1875, ((0, 8), (1, 4)))
    w_key = bell_draw(streams_of[4], (D, HH), D ** -0.5, 0.1875, ((0, 8), (1, 4)))
    w_value = bell_draw(streams_of[5], (D, HH), D ** -0.5, 0.1875, ((0, 8), (1, 4)))
    w_out = bell_draw(streams_of[6], (HH, D), (max(1, 2 * HH // LONG)) ** -0.5, 6.0, ((0, 4), (1, 8)))
    ffn_gain = jnp.clip(1.0 + 0.1 * jax.random.normal(streams_of[7], (D,), jnp.float32), 0.5, 1.5).astype(jnp.bfloat16)
    w_gate = bell_draw(streams_of[8], (D, FF), D ** -0.5, 0.1875, ((0, 8), (1, 4)))
    w_up = bell_draw(streams_of[9], (D, FF), D ** -0.5, 0.1875, ((0, 8), (1, 4)))
    w_down = bell_draw(streams_of[10], (FF, D), FF ** -0.5, 0.109375, ((0, 4), (1, 8)))
    cotangent = bell_draw(streams_of[11], (GROUPS, LONG, D), 1.0, 6.0, ((0, 8), (1, 4)))
    return dict(inputs=inputs, bucket=bucket, attn_gain=attn_gain, w_query=w_query, w_key=w_key, w_value=w_value, w_out=w_out, ffn_gain=ffn_gain, w_gate=w_gate, w_up=w_up, w_down=w_down, cotangent=cotangent)


highest = lax.Precision.HIGHEST
epsilon = 1e-06

@jax.custom_vjp
def low(v):
    return lax.optimization_barrier(v.astype(jnp.bfloat16)).astype(jnp.float32)

@jax.custom_vjp
def low_back(v):
    return v

def low_keep(v):
    return (low(v), None)

def low_pass(kept, grad):
    return (grad,)

def back_keep(v):
    return (v, None)

def back_low(kept, grad):
    return (low(grad),)
low.defvjp(low_keep, low_pass)
low_back.defvjp(back_keep, back_low)

def matmul(left, right):
    return jnp.dot(left, right, precision=highest)

def norm_apply(stream, gain):
    return stream * lax.rsqrt(lax.optimization_barrier(jnp.mean(stream * stream, axis=-1, keepdims=True)) + epsilon) * gain

def layer(stream, bucket_flag, params):
    attn_gain, w_query, w_key, w_value, w_out, ffn_gain, w_gate, w_up, w_down = params
    length = stream.shape[0]
    hidden = low(norm_apply(stream, attn_gain))
    query_rows = low_back(low(matmul(hidden, w_query))).reshape(length, HEADS, HEAD)
    key_rows = low_back(low(matmul(hidden, w_key))).reshape(length, HEADS, HEAD)
    value_rows = low_back(low(matmul(hidden, w_value))).reshape(length, HEADS, HEAD)
    score_scale = 1.0 / math.sqrt(HEAD)
    scores = low_back(jnp.einsum('qhd,khd->hqk', query_rows, key_rows, precision=highest) * score_scale)
    places = jnp.arange(length, dtype=jnp.int32)
    allowed = (bucket_flag == 1) | (places[:, None] // SHORT == places[None, :] // SHORT)
    scores = jnp.where(allowed[None], scores, -1e+30)
    row_max = lax.optimization_barrier(jnp.max(scores, axis=-1, keepdims=True))
    expo = jnp.exp(scores - row_max)
    probs = low(expo / lax.optimization_barrier(jnp.sum(expo, axis=-1, keepdims=True)))
    attended = jnp.einsum('hqk,khd->qhd', probs, value_rows, precision=highest)
    attended = low_back(low(attended)).reshape(length, HEADS * HEAD)
    middle = stream + low_back(matmul(attended, w_out))
    normed = low(norm_apply(middle, ffn_gain))
    gate_pre = low_back(matmul(normed, w_gate))
    up_pre = low_back(matmul(normed, w_up))
    inner_act = low(jax.nn.gelu(gate_pre, approximate=True) * up_pre)
    return middle + low_back(matmul(inner_act, w_down))

def reference(inputs, bucket, attn_gain, w_query, w_key, w_value, w_out, ffn_gain, w_gate, w_up, w_down, cotangent):
    params = tuple((item.astype(jnp.float32) for item in (attn_gain, w_query, w_key, w_value, w_out, ffn_gain, w_gate, w_up, w_down)))
    stream = inputs.astype(jnp.float32)

    def forward(stream_all, params_all):

        def one_group(item):
            return jax.checkpoint(layer)(item[0], item[1], params_all)
        return lax.map(one_group, (stream_all, bucket))
    result, pull = jax.vjp(forward, stream, params)
    input_grad, grads = pull(cotangent.astype(jnp.float32))
    return (result.astype(jnp.bfloat16), input_grad, grads[0], grads[1], grads[2], grads[3], grads[4], grads[5], grads[6], grads[7], grads[8])
```

```python
import functools

import jax
import jax.numpy as jnp
from jax import lax
from jax.experimental import pallas as pl
from jax.experimental.pallas import tpu as pltpu
from jax.sharding import PartitionSpec as P

HEAD = 64
SHORT = 384
EPS = 1e-06
BLOCKS = 4
f32 = jnp.float32
bf16 = jnp.bfloat16


def dot_nn(left, right):
    return jnp.dot(left, right, preferred_element_type=f32)


def dot_nt(left, right):
    return lax.dot_general(left, right, (((1,), (1,)), ((), ())), preferred_element_type=f32)


def call(kernel, grid, prefetch, in_specs, out_specs, out_shape, scratch, flops, moved, vmem):
    return pl.pallas_call(
        kernel,
        grid_spec=pltpu.PrefetchScalarGridSpec(
            num_scalar_prefetch=prefetch,
            grid=grid,
            in_specs=in_specs,
            out_specs=out_specs,
            scratch_shapes=scratch,
        ),
        out_shape=out_shape,
        compiler_params=pltpu.CompilerParams(vmem_limit_bytes=vmem << 20),
        cost_estimate=pl.CostEstimate(flops=flops, bytes_accessed=moved, transcendentals=0),
    )


def shaped(shape, dtype):
    return jax.ShapeDtypeStruct(shape, dtype)


def rms_of(rows):
    return lax.rsqrt(jnp.mean(rows * rows, axis=-1, keepdims=True) + EPS)


def qkv_kernel(me_ref, x_ref, gain_ref, w_ref, hidden_ref, q_ref, k_ref, v_ref):
    rows = x_ref[...].astype(f32)
    hidden_ref[...] = (rows * rms_of(rows) * gain_ref[...]).astype(bf16)
    wide = w_ref.shape[3]
    half = w_ref.shape[1] * 128
    for part, ref in enumerate((q_ref, k_ref, v_ref)):
        total = None
        for step in range(BLOCKS):
            start = pl.multiple_of((me_ref[0] ^ step) * wide, wide)
            weight = w_ref[step, :, part * 128 : (part + 1) * 128, :].reshape(half, wide)
            piece = dot_nt(hidden_ref[:, pl.ds(start, wide)], weight)
            total = piece if total is None else total + piece
        if part == 0:
            total = total * (HEAD**-0.5)
        ref[...] = total.astype(bf16)


def qkv_call(me, rows, gain, weights):
    count, width = rows.shape
    half = weights.shape[1] * 128
    tile = count // 4
    row_spec = pl.BlockSpec((tile, width), lambda i, me: (i, 0))
    half_spec = pl.BlockSpec((tile, half), lambda i, me: (i, 0))
    return call(
        qkv_kernel,
        (count // tile,),
        1,
        [
            row_spec,
            pl.BlockSpec((1, width), lambda i, me: (0, 0)),
            pl.BlockSpec(weights.shape, lambda i, me: (0, 0, 0, 0)),
        ],
        [row_spec, half_spec, half_spec, half_spec],
        [shaped(rows.shape, bf16)] + [shaped((count, half), bf16)] * 3,
        [],
        2 * count * width * half * 3,
        12 << 20,
        40,
    )(me, rows, gain, weights)


def two_heads(rows):
    low = lax.broadcasted_iota(jnp.int32, rows.shape, 1) < HEAD
    zero = jnp.zeros_like(rows)
    return jnp.concatenate([jnp.where(low, rows, zero), jnp.where(low, zero, rows)], axis=0)


def one_pair(both):
    half = both.shape[1] // 2
    return jnp.concatenate([both[:HEAD, :half], both[HEAD:, half:]], axis=0)


def attend_kernel(flag_ref, q_ref, k_ref, v_ref, out_ref, probs_ref, v_turned):
    block = pl.program_id(1)

    @pl.when(block == 0)
    def _():
        v_turned[...] = v_ref[...].T

    queries = two_heads(q_ref[...])

    def attend(keys, values):
        scores = dot_nt(keys, queries)
        expo = jnp.exp(scores - jnp.max(scores, axis=0, keepdims=True))
        probs = (expo * (1.0 / jnp.sum(expo, axis=0, keepdims=True))).astype(bf16)
        probs_ref[0, 0, : keys.shape[0], :] = probs
        out_ref[...] = one_pair(dot_nn(values, probs)).T.astype(bf16)

    @pl.when(flag_ref[0] == 1)
    def _():
        attend(k_ref[...], v_turned[...])

    @pl.when(flag_ref[0] != 1)
    def _():
        start = pl.multiple_of(block * SHORT, SHORT)
        attend(k_ref[pl.ds(start, SHORT), :], v_turned[:, pl.ds(start, SHORT)])


def attend_call(flag, q, k, v):
    count, half = q.shape
    pairs, blocks = half // 128, count // SHORT
    some = pl.BlockSpec((SHORT, 128), lambda j, i, flag: (i, j))
    every = pl.BlockSpec((count, 128), lambda j, i, flag: (0, j))
    return call(
        attend_kernel,
        (pairs, blocks),
        1,
        [some, every, every],
        [some, pl.BlockSpec((1, 1, count, 2 * SHORT), lambda j, i, flag: (j, i, 0, 0))],
        [shaped(q.shape, bf16), shaped((pairs, blocks, count, 2 * SHORT), bf16)],
        [pltpu.VMEM((128, count), bf16)],
        4 * 4 * count * count * half,
        28 << 20,
        48,
    )(flag, q, k, v)


def branch_kernel(me_ref, att_ref, w_ref, out_ref):
    wide = w_ref.shape[3]
    for step in range(BLOCKS):
        start = pl.multiple_of((me_ref[0] ^ step) * wide, wide)
        weight = w_ref[step].reshape(att_ref.shape[1], wide)
        out_ref[:, pl.ds(start, wide)] = dot_nn(att_ref[...], weight).astype(bf16)


def branch_call(me, attended, weights):
    count, half = attended.shape
    width = weights.shape[0] * weights.shape[3]
    tile = count // 4
    block = weights.shape[:2] + (128,) + weights.shape[3:]
    return call(
        branch_kernel,
        (count // tile,),
        1,
        [
            pl.BlockSpec((tile, half), lambda i, me: (i, 0)),
            pl.BlockSpec(block, lambda i, me: (0, 0, 3, 0)),
        ],
        pl.BlockSpec((tile, width), lambda i, me: (i, 0)),
        shaped((count, width), bf16),
        [],
        2 * count * width * half,
        5 << 20,
        24,
    )(me, attended, weights)


def middle_kernel(x_ref, one_ref, two_ref, gain_ref, middle_ref, normed_ref):
    middle = x_ref[...].astype(f32) + (one_ref[...].astype(f32) + two_ref[...].astype(f32))
    middle_ref[...] = middle
    normed_ref[...] = (middle * rms_of(middle) * gain_ref[...]).astype(bf16)


def middle_call(rows, one, two, gain):
    count, width = rows.shape
    tile = count // 4
    spec = pl.BlockSpec((tile, width), lambda i: (i, 0))
    return call(
        middle_kernel,
        (count // tile,),
        0,
        [spec, spec, spec, pl.BlockSpec((1, width), lambda i: (0, 0))],
        [spec, spec],
        [shaped(rows.shape, f32), shaped(rows.shape, bf16)],
        [],
        0,
        14 << 20,
        32,
    )(rows, one, two, gain)


def ffn_kernel(
    normed_ref, d_out_ref, w_ref, result_ref, d_normed_ref, grads_ref, result, d_normed, inner_t, gate_t, up_t
):
    chunk, chunks = pl.program_id(0), pl.num_programs(0)
    parts, pieces, kinds, depth, wide = w_ref.shape
    units = pieces * depth
    tile = SHORT

    def weight(step, kind):
        return w_ref[step, :, kind].reshape(units, wide)

    def columns(step):
        return slice(step * wide, (step + 1) * wide)

    def rows_step(index, carry):
        rows = pl.ds(pl.multiple_of(index * tile, tile), tile)

        def project(ref, kind):
            total = None
            for step in range(parts):
                piece = dot_nt(ref[rows, columns(step)], weight(step, kind))
                total = piece if total is None else total + piece
            return total

        gate, up, d_inner = project(normed_ref, 0), project(normed_ref, 1), project(d_out_ref, 2)
        square = gate * gate
        bent = jnp.tanh(0.7978845608 * gate * (1.0 + 0.044715 * square))
        half = 0.5 * (1.0 + bent)
        gelu = gate * half
        slope = half + 0.5 * gate * (1.0 - bent * bent) * (
            0.7978845608 * (1.0 + 3 * 0.044715 * square)
        )
        inner = (gelu * up).astype(bf16)
        d_gate = (d_inner * up * slope).astype(bf16)
        d_up = (d_inner * gelu).astype(bf16)
        inner_t[:, rows] = inner.T
        gate_t[:, rows] = d_gate.T
        up_t[:, rows] = d_up.T
        for step in range(parts):
            forward = dot_nn(inner, weight(step, 2))
            backward = dot_nn(d_gate, weight(step, 0)) + dot_nn(d_up, weight(step, 1))

            @pl.when(chunk == 0)
            def _():
                result[rows, columns(step)] = forward
                d_normed[rows, columns(step)] = backward

            @pl.when(chunk > 0)
            def _():
                result[rows, columns(step)] += forward
                d_normed[rows, columns(step)] += backward

        return carry

    lax.fori_loop(0, normed_ref.shape[0] // tile, rows_step, 0)
    for step in range(parts):
        block = (pieces, depth, wide)
        here = normed_ref[:, columns(step)]
        grads_ref[step, :, 0] = dot_nn(gate_t[...], here).reshape(block).astype(bf16)
        grads_ref[step, :, 1] = dot_nn(up_t[...], here).reshape(block).astype(bf16)
        there = d_out_ref[:, columns(step)]
        grads_ref[step, :, 2] = dot_nn(inner_t[...], there).reshape(block).astype(bf16)

    @pl.when(chunk == chunks - 1)
    def _():
        result_ref[...] = result[...].astype(bf16)
        d_normed_ref[...] = d_normed[...].astype(bf16)


def ffn_call(normed, d_out, weights):
    count, width = normed.shape
    parts, pieces, kinds, depth, wide = weights.shape
    chunks = 2
    part = depth // chunks
    units = pieces * part
    whole = pl.BlockSpec((count, width), lambda f: (0, 0))
    weight_spec = pl.BlockSpec((parts, pieces, kinds, part, wide), lambda f: (0, 0, 0, f, 0))
    return call(
        ffn_kernel,
        (chunks,),
        0,
        [whole, whole, weight_spec],
        [whole, whole, weight_spec],
        [shaped(normed.shape, bf16), shaped(normed.shape, bf16), shaped(weights.shape, bf16)],
        [pltpu.VMEM((count, width), f32)] * 2 + [pltpu.VMEM((units, count), bf16)] * 3,
        18 * count * width * pieces * depth,
        28 << 20,
        60,
    )(normed, d_out, weights)


def turn_kernel(
    me_ref, middle_ref, one_ref, two_ref, cot_ref, gain_ref, w_ref, d_middle_ref, d_branch_ref, d_att_ref, gain_grad_ref
):
    middle = middle_ref[...]
    rms = rms_of(middle)
    scaled = middle * rms
    d_normed = one_ref[...].astype(f32) + two_ref[...].astype(f32)
    pulled = d_normed * gain_ref[...]
    d_middle = cot_ref[...].astype(f32) + rms * (
        pulled - scaled * jnp.mean(pulled * scaled, axis=-1, keepdims=True)
    )
    d_middle_ref[...] = d_middle
    d_branch_ref[...] = d_middle.astype(bf16)

    @pl.when(pl.program_id(0) == 0)
    def _():
        gain_grad_ref[...] = jnp.zeros_like(gain_grad_ref)

    gain_grad_ref[...] += jnp.sum(d_normed * scaled, axis=0, keepdims=True)
    wide = w_ref.shape[3]
    total = None
    for step in range(BLOCKS):
        start = pl.multiple_of((me_ref[0] ^ step) * wide, wide)
        piece = dot_nt(d_branch_ref[:, pl.ds(start, wide)], w_ref[step].reshape(d_att_ref.shape[1], wide))
        total = piece if total is None else total + piece
    d_att_ref[...] = total.astype(bf16)


def turn_call(me, middle, one, two, cot, gain, weights):
    count, width = middle.shape
    half = weights.shape[1] * 128
    tile = count // 4
    spec = pl.BlockSpec((tile, width), lambda i, me: (i, 0))
    line = pl.BlockSpec((1, width), lambda i, me: (0, 0))
    block = weights.shape[:2] + (128,) + weights.shape[3:]
    return call(
        turn_kernel,
        (count // tile,),
        1,
        [spec, spec, spec, spec, line, pl.BlockSpec(block, lambda i, me: (0, 0, 3, 0))],
        [spec, spec, pl.BlockSpec((tile, half), lambda i, me: (i, 0)), line],
        [
            shaped(middle.shape, f32),
            shaped(middle.shape, bf16),
            shaped((count, half), bf16),
            shaped((1, width), f32),
        ],
        [],
        2 * count * width * half,
        22 << 20,
        40,
    )(me, middle, one, two, cot, gain, weights)


def attend_back_kernel(
    flag_ref, q_ref, k_ref, v_ref, out_ref, d_out_ref, probs_ref, dq_ref, dk_ref, dv_ref, k_turned, dk_sum, dv_sum
):
    block, blocks = pl.program_id(1), pl.num_programs(1)

    @pl.when(block == 0)
    def _():
        k_turned[...] = k_ref[...].T

    queries, grads = two_heads(q_ref[...]), two_heads(d_out_ref[...])
    turned = (d_out_ref[...].astype(f32) * out_ref[...].astype(f32)).T
    delta = jnp.concatenate(
        [
            jnp.sum(turned[:HEAD], axis=0, keepdims=True),
            jnp.sum(turned[HEAD:], axis=0, keepdims=True),
        ],
        axis=1,
    )

    def back(values, keys_turned):
        probs = probs_ref[0, 0, : values.shape[0], :]
        d_probs = dot_nt(values, grads)
        d_scores = (probs.astype(f32) * (d_probs - delta)).astype(bf16)
        d_query = one_pair(dot_nn(keys_turned, d_scores)).T * (HEAD**-0.5)
        dq_ref[...] = d_query.astype(bf16)
        return dot_nn(d_scores, queries), dot_nn(probs, grads)

    @pl.when(flag_ref[0] == 1)
    def _():
        d_key, d_value = back(v_ref[...], k_turned[...])

        @pl.when(block == 0)
        def _():
            dk_sum[...] = d_key
            dv_sum[...] = d_value

        @pl.when(block > 0)
        def _():
            dk_sum[...] += d_key
            dv_sum[...] += d_value

    @pl.when(flag_ref[0] != 1)
    def _():
        rows = pl.ds(pl.multiple_of(block * SHORT, SHORT), SHORT)
        d_key, d_value = back(v_ref[rows, :], k_turned[:, rows])
        dk_sum[rows, :] = d_key
        dv_sum[rows, :] = d_value

    @pl.when(block == blocks - 1)
    def _():
        dk_ref[...] = dk_sum[...].astype(bf16)
        dv_ref[...] = dv_sum[...].astype(bf16)


def attend_back_call(flag, q, k, v, out, d_out, probs):
    count, half = q.shape
    pairs, blocks = half // 128, count // SHORT
    some = pl.BlockSpec((SHORT, 128), lambda j, i, flag: (i, j))
    every = pl.BlockSpec((count, 128), lambda j, i, flag: (0, j))
    return call(
        attend_back_kernel,
        (pairs, blocks),
        1,
        [
            some,
            every,
            every,
            some,
            some,
            pl.BlockSpec((1, 1, count, 2 * SHORT), lambda j, i, flag: (j, i, 0, 0)),
        ],
        [some, every, every],
        [shaped(q.shape, bf16)] * 3,
        [pltpu.VMEM((128, count), bf16)] + [pltpu.VMEM((count, 128), f32)] * 2,
        4 * 8 * count * count * half,
        30 << 20,
        48,
    )(flag, q, k, v, out, d_out, probs)


def square_kernel(
    me_ref, dq_ref, dk_ref, dv_ref, att_ref, hidden_ref, d_branch_ref, w_ref, d_hidden_ref, grads_ref, turned
):
    lefts = (dq_ref, dk_ref, dv_ref, att_ref)

    @pl.when(pl.program_id(0) == 0)
    def _():
        for part, ref in enumerate(lefts):
            turned[part] = ref[...].T

    pieces, wide = w_ref.shape[1], w_ref.shape[3]
    total = None
    for part, ref in enumerate(lefts):
        rows = slice(part * 128, (part + 1) * 128)
        right = d_branch_ref if part == 3 else hidden_ref
        grad = dot_nn(turned[part], right[...])
        grads_ref[0, :, rows, :] = grad.reshape(pieces, 128, wide).astype(bf16)
        if part < 3:
            piece = dot_nn(ref[...], w_ref[0, :, rows, :].reshape(pieces * 128, wide))
            total = piece if total is None else total + piece
    d_hidden_ref[...] = total.astype(bf16)


def square_call(me, dq, dk, dv, attended, hidden, d_branch, weights):
    count, half = dq.shape
    width = hidden.shape[1]
    parts, pieces, depth, wide = weights.shape
    every = pl.BlockSpec((count, half), lambda d, me: (0, 0))
    column = pl.BlockSpec((count, wide), lambda d, me: (0, me[0] ^ d))
    return call(
        square_kernel,
        (parts,),
        1,
        [every] * 4
        + [column, column, pl.BlockSpec((1, pieces, depth, wide), lambda d, me: (d, 0, 0, 0))],
        [column, pl.BlockSpec((1, pieces, depth, wide), lambda d, me: (me[0] ^ d, 0, 0, 0))],
        [shaped(hidden.shape, bf16), shaped(weights.shape, bf16)],
        [pltpu.VMEM((4, half, count), bf16)],
        14 * count * width * half,
        24 << 20,
        40,
    )(me, dq, dk, dv, attended, hidden, d_branch, weights)


def output_kernel(core_ref, middle_ref, own_ref, other_ref, out_ref):
    out_ref[0] = (
        middle_ref[0, 0] + (own_ref[0, 0].astype(f32) + other_ref[0].astype(f32))
    ).astype(bf16)


def output_call(core, middle, own, other):
    slots, halves, tile, width = own.shape
    mine = pl.BlockSpec((1, 1, tile, width), lambda i, core: (i, core[0], 0, 0))
    plain = pl.BlockSpec((1, tile, width), lambda i, core: (i, 0, 0))
    return call(
        output_kernel,
        (slots,),
        1,
        [mine, mine, plain],
        plain,
        shaped((slots, tile, width), bf16),
        [],
        0,
        6 << 20,
        16,
    )(core, middle.reshape(own.shape), own, other)


def input_kernel(core_ref, x_ref, d_middle_ref, own_ref, other_ref, gain_ref, out_ref, gain_grad_ref):
    rows = x_ref[0, 0].astype(f32)
    rms = rms_of(rows)
    scaled = rows * rms
    d_hidden = own_ref[0, 0].astype(f32) + other_ref[0].astype(f32)
    pulled = d_hidden * gain_ref[...]
    out_ref[0] = (
        d_middle_ref[0, 0]
        + rms * (pulled - scaled * jnp.mean(pulled * scaled, axis=-1, keepdims=True))
    ).astype(bf16)

    @pl.when(pl.program_id(0) == 0)
    def _():
        gain_grad_ref[...] = jnp.zeros_like(gain_grad_ref)

    gain_grad_ref[...] += jnp.sum(d_hidden * scaled, axis=0, keepdims=True)


def input_call(core, rows, d_middle, own, other, gain):
    slots, halves, tile, width = own.shape
    mine = pl.BlockSpec((1, 1, tile, width), lambda i, core: (i, core[0], 0, 0))
    plain = pl.BlockSpec((1, tile, width), lambda i, core: (i, 0, 0))
    line = pl.BlockSpec((1, width), lambda i, core: (0, 0))
    return call(
        input_kernel,
        (slots,),
        1,
        [mine, mine, mine, plain, line],
        [plain, line],
        [shaped((slots, tile, width), bf16), shaped((1, width), f32)],
        [],
        0,
        8 << 20,
        16,
    )(core, rows.reshape(own.shape), d_middle.reshape(own.shape), own, other, gain)


def per_device(
    inputs,
    bucket,
    attn_gain,
    w_query,
    w_key,
    w_value,
    w_out,
    ffn_gain,
    w_gate,
    w_up,
    w_down,
    cotangent,
):
    dp, narrow = lax.axis_size("dp"), lax.axis_size("narrow")
    chips = dp // 2
    core, chip = lax.axis_index("dp") % 2, lax.axis_index("dp") // 2
    place = lax.axis_index("narrow")
    same_core = [[2 * m + c for m in range(chips)] for c in range(2)]
    by_core = core == 0
    bundle, row_count, width = inputs.shape
    tile = row_count // 2
    own_width = w_query.shape[0]

    def to_core(value):
        return lax.ppermute(value, "dp", [(i, i ^ 1) for i in range(dp)])

    def along(value, shift):
        return lax.ppermute(
            value, "narrow", [(i, (i + shift) % narrow) for i in range(narrow)]
        )

    def to_chip(value, flip):
        return lax.ppermute(value, "dp", [(i, i ^ (2 * flip)) for i in range(dp)])

    def ordered(mine, theirs, axis):
        join = functools.partial(jnp.concatenate, axis=axis)
        return jnp.where(by_core, join([mine, theirs]), join([theirs, mine]))

    def pick(value, index, axis):
        return lax.dynamic_index_in_dim(value, index, axis, keepdims=False)

    def across(value):
        moved = [pick(value, place, 0)] + [
            along(pick(value, (place + k) % narrow, 0), k) for k in range(1, narrow)
        ]
        stacked = jnp.stack(moved)
        order = (place - jnp.arange(narrow)) % narrow
        return jnp.stack([pick(stacked, order[i], 0) for i in range(narrow)])

    def group_in(value):
        halves = value.reshape(bundle, 2, tile, width)
        theirs = to_core(pick(halves, 1 - core, 1))
        groups = ordered(pick(halves, core, 1), theirs, 0)
        mine = across(groups)
        other = to_core(mine)
        return ordered(mine[:, None], other[:, None], 1).reshape(-1, width)

    def group_out(value):
        groups = across(value).reshape(2, bundle, tile, width)
        theirs = to_core(pick(groups, 1 - core, 0))
        mine = pick(groups, core, 0)
        return ordered(mine[:, None], theirs[:, None], 1).reshape(bundle, row_count, width)

    def halves_of(*parts):
        both = jnp.concatenate(
            [part.reshape(2, part.shape[0] // 2, own_width) for part in parts], axis=1
        )
        return ordered(pick(both, core, 0), to_core(pick(both, 1 - core, 0)), 1)

    square = halves_of(w_query.T, w_key.T, w_value.T, w_out)
    ffn = halves_of(w_gate.T, w_up.T, w_down)
    gains = ordered(*(lambda g: (g, to_core(g)))(jnp.stack([attn_gain, ffn_gain])), 1)

    def canonical(value):
        if chips == BLOCKS:
            return value
        parts = value.reshape((BLOCKS, chips // BLOCKS) + value.shape[1:])
        return jnp.moveaxis(parts, 1, -2).reshape(
            (BLOCKS,) + value.shape[1:-1] + (width // BLOCKS,)
        )

    def scattered(value):
        if chips == BLOCKS:
            return value
        parts = value.reshape(
            value.shape[:-1] + (chips // BLOCKS, width // chips)
        )
        return jnp.moveaxis(parts, -2, 1).reshape(
            (chips,) + value.shape[1:-1] + (width // chips,)
        )

    stacked = jnp.stack([square] + [along(square, k) for k in range(1, narrow)])
    x_rows = group_in(inputs)
    if chips == 4:
        first, second = to_chip(stacked, 1), to_chip(stacked, 2)
        third = jnp.concatenate(
            [to_chip(first[: narrow // 2], 2), to_chip(second[narrow // 2 :], 1)]
        )
        square_full = jnp.stack([stacked, first, second, third])
        me = chip.astype(jnp.int32)[None]
        gain_first, gain_second = to_chip(gains, 1), to_chip(gains, 2)
        relative = jnp.stack([gains, gain_first, gain_second, to_chip(gain_first, 2)])
        full_gains = jnp.stack([pick(relative, chip ^ d, 0) for d in range(4)], axis=1)
    else:
        gathered = lax.all_gather(stacked, "dp", axis_index_groups=same_core)
        square_full = canonical(gathered)
        me = jnp.zeros((1,), jnp.int32)
        full_gains = jnp.moveaxis(
            lax.all_gather(gains, "dp", axis_index_groups=same_core), 0, 1
        )
    full_gains = full_gains.reshape(2, 1, width).astype(f32)

    everyone = [
        [(2 * m + c) * narrow + j for m in range(chips) for j in range(narrow)] for c in range(2)
    ]
    gathered = lax.all_gather(ffn, ("dp", "narrow"), axis_index_groups=everyone)
    ffn_full = canonical(gathered.reshape(chips, narrow, ffn.shape[0], ffn.shape[1]))
    ffn_full = ffn_full.reshape(BLOCKS, narrow, 3, ffn.shape[0] // 3, width // BLOCKS)
    cot_rows = group_in(cotangent)

    flags = ordered(bucket, lax.ppermute(bucket.astype(f32), "dp", [(i, i ^ 1) for i in range(dp)]).astype(jnp.int32), 0)
    flag = pick(flags, place, 0)[None]
    core_index = core.astype(jnp.int32)[None]

    hidden, q, k, v = qkv_call(me, x_rows, full_gains[0], square_full)
    attended, probs = attend_call(flag, q, k, v)
    branch = branch_call(me, attended, square_full)
    middle, normed = middle_call(x_rows, branch, to_core(branch), full_gains[1])
    result, d_normed, ffn_grads = ffn_call(normed, cot_rows, ffn_full)

    d_middle, d_branch, d_att, ffn_gain_grad = turn_call(
        me, middle, d_normed, to_core(d_normed), cot_rows, full_gains[1], square_full
    )

    def reduce_chips(value):
        value = scattered(value)
        flat = value.reshape(-1, value.shape[-1])
        got = lax.psum_scatter(
            flat, "dp", scatter_dimension=0, tiled=True, axis_index_groups=same_core
        )
        return got.reshape(value.shape[1:])

    ffn_part = reduce_chips(ffn_grads.reshape(BLOCKS, narrow, ffn.shape[0], width // BLOCKS))

    by_rows = (narrow, 2, tile, width)
    result = result.reshape(by_rows)
    result_other = to_core(pick(result, 1 - core, 1))
    outputs = group_out(output_call(core_index, middle, result, result_other))

    dq, dk, dv = attend_back_call(flag, q, k, v, attended, d_att, probs)
    d_hidden, square_grads = square_call(
        me, dq, dk, dv, attended, hidden, d_branch, square_full
    )
    d_hidden = d_hidden.reshape(by_rows)
    d_hidden_other = to_core(pick(d_hidden, 1 - core, 1))
    input_rows, attn_gain_grad = input_call(
        core_index, x_rows, d_middle, d_hidden, d_hidden_other, full_gains[0]
    )
    input_grad = group_out(input_rows).astype(f32)

    square_part = reduce_chips(square_grads)

    gain_line = jnp.concatenate([attn_gain_grad, 0.5 * ffn_gain_grad], axis=0)
    gain_sum = lax.psum(gain_line, ("dp", "narrow"))
    gain_own = lax.dynamic_slice_in_dim(
        gain_sum, lax.axis_index("dp") * own_width, own_width, axis=1
    )

    def finish(mine, received):
        total = mine.astype(f32)
        for piece in received:
            total = total + piece.astype(f32)
        both = total.reshape(total.shape[0], 2, own_width)
        keep = pick(both, core, 1)
        theirs = to_core(pick(both, 1 - core, 1).astype(bf16)).astype(f32)
        return jnp.where(by_core, jnp.stack([keep, theirs]), jnp.stack([theirs, keep]))

    square_done = finish(
        square_part[0], [along(square_part[k], -k) for k in range(1, narrow)]
    )
    ffn_done = finish(
        pick(ffn_part, place, 0),
        [along(pick(ffn_part, (place + k) % narrow, 0), k) for k in range(1, narrow)],
    )

    def unpack(done, parts):
        size = done.shape[1] // parts
        return [
            done[:, i * size : (i + 1) * size].reshape(2 * size, own_width) for i in range(parts)
        ]

    g_query, g_key, g_value, g_out = unpack(square_done, 4)
    g_gate, g_up, g_down = unpack(ffn_done, 3)
    return (
        outputs,
        input_grad,
        gain_own[0],
        g_query.T,
        g_key.T,
        g_value.T,
        g_out,
        gain_own[1],
        g_gate.T,
        g_up.T,
        g_down,
    )


def solution(mesh):
    rows = P("dp", "narrow", None)
    tall, flat = P("dp", "narrow"), P("narrow", "dp")
    return jax.shard_map(
        per_device,
        mesh=mesh,
        in_specs=(rows, P("dp"), P("dp"), tall, tall, tall, flat, P("dp"), tall, tall, flat, rows),
        out_specs=(rows, rows, P("dp"), tall, tall, tall, flat, P("dp"), tall, tall, flat),
        check_vma=False,
    )
```

```python
import functools

import jax
import jax.numpy as jnp
from jax import lax
from jax.experimental import pallas as pl
from jax.experimental.pallas import tpu as pltpu
from jax.sharding import PartitionSpec as P

HEAD = 64
SHORT = 384
EPS = 1e-06
BLOCKS = 4
f32 = jnp.float32
bf16 = jnp.bfloat16


def dot_nn(left, right):
    return jnp.dot(left, right, preferred_element_type=f32)


def dot_nt(left, right):
    return lax.dot_general(left, right, (((1,), (1,)), ((), ())), preferred_element_type=f32)


def call(kernel, grid, prefetch, in_specs, out_specs, out_shape, scratch, flops, moved, vmem):
    return pl.pallas_call(
        kernel,
        grid_spec=pltpu.PrefetchScalarGridSpec(
            num_scalar_prefetch=prefetch,
            grid=grid,
            in_specs=in_specs,
            out_specs=out_specs,
            scratch_shapes=scratch,
        ),
        out_shape=out_shape,
        compiler_params=pltpu.CompilerParams(vmem_limit_bytes=vmem << 20),
        cost_estimate=pl.CostEstimate(flops=flops, bytes_accessed=moved, transcendentals=0),
    )


def shaped(shape, dtype):
    return jax.ShapeDtypeStruct(shape, dtype)


def rms_of(rows):
    return lax.rsqrt(jnp.mean(rows * rows, axis=-1, keepdims=True) + EPS)


def store_grad(refs, step, grad, first):
    x_keep, x_send, y_keep, y_send = refs
    half, rows = grad.shape[0] // 2, slice(first, first + grad.shape[1])
    (x_send if step % 2 else x_keep)[step // 2, :, rows] = grad[:half]
    (y_send if step // 2 else y_keep)[step % 2, :, rows] = grad[half:]


def grad_shapes(pieces, rows, wide):
    return [shaped((2, pieces // 2, rows, wide), bf16)] * 4


def qkv_kernel(me_ref, x_ref, w_ref, hidden_ref, rms_ref, gains_ref, q_ref, k_ref, v_ref):
    rows = x_ref[...].astype(f32)
    rms = rms_of(rows)
    rms_ref[...] = jnp.broadcast_to(rms, rms_ref.shape)
    wide = w_ref.shape[3]
    half = w_ref.shape[1] * 128
    for step in range(BLOCKS):
        columns = pl.ds(pl.multiple_of((me_ref[0] ^ step) * wide, wide), wide)
        gains = w_ref[step, 0, 4 * 128 :, :].astype(f32)
        gains_ref[:, columns] = gains[:8]
        hidden_ref[:, columns] = (x_ref[:, columns].astype(f32) * rms * gains[:1]).astype(bf16)
    for part, ref in enumerate((q_ref, k_ref, v_ref)):
        total = None
        for step in range(BLOCKS):
            start = pl.multiple_of((me_ref[0] ^ step) * wide, wide)
            weight = w_ref[step, :, part * 128 : (part + 1) * 128, :].reshape(half, wide)
            piece = dot_nt(hidden_ref[:, pl.ds(start, wide)], weight)
            total = piece if total is None else total + piece
        if part == 0:
            total = total * (HEAD**-0.5)
        ref[...] = total.astype(bf16)


def qkv_call(me, rows, weights):
    count, width = rows.shape
    half = weights.shape[1] * 128
    tile = count // 4
    row_spec = pl.BlockSpec((tile, width), lambda i, me: (i, 0))
    half_spec = pl.BlockSpec((tile, half), lambda i, me: (i, 0))
    return call(
        qkv_kernel,
        (count // tile,),
        1,
        [row_spec, pl.BlockSpec(weights.shape, lambda i, me: (0, 0, 0, 0))],
        [
            row_spec,
            pl.BlockSpec((tile, 128), lambda i, me: (i, 0)),
            pl.BlockSpec((8, width), lambda i, me: (0, 0)),
            half_spec,
            half_spec,
            half_spec,
        ],
        [shaped(rows.shape, bf16), shaped((count, 128), f32), shaped((8, width), f32)]
        + [shaped((count, half), bf16)] * 3,
        [],
        2 * count * width * half * 3,
        12 << 20,
        40,
    )(me, rows, weights)


def two_heads(rows):
    low = lax.broadcasted_iota(jnp.int32, rows.shape, 1) < HEAD
    zero = jnp.zeros_like(rows)
    return jnp.concatenate([jnp.where(low, rows, zero), jnp.where(low, zero, rows)], axis=0)


def one_pair(both):
    half = both.shape[1] // 2
    return jnp.concatenate([both[:HEAD, :half], both[HEAD:, half:]], axis=0)


def attend_kernel(flag_ref, q_ref, k_ref, v_ref, out_ref, probs_ref, v_turned):
    block = pl.program_id(1)

    @pl.when(block == 0)
    def _():
        v_turned[...] = v_ref[...].T

    queries = two_heads(q_ref[...])

    def attend(keys, values):
        scores = dot_nt(keys, queries)
        expo = jnp.exp(scores - jnp.max(scores, axis=0, keepdims=True))
        probs = (expo * (1.0 / jnp.sum(expo, axis=0, keepdims=True))).astype(bf16)
        probs_ref[0, 0, : keys.shape[0], :] = probs
        out_ref[...] = one_pair(dot_nn(values, probs)).T.astype(bf16)

    @pl.when(flag_ref[0] == 1)
    def _():
        attend(k_ref[...], v_turned[...])

    @pl.when(flag_ref[0] != 1)
    def _():
        start = pl.multiple_of(block * SHORT, SHORT)
        attend(k_ref[pl.ds(start, SHORT), :], v_turned[:, pl.ds(start, SHORT)])


def attend_call(flag, q, k, v):
    count, half = q.shape
    pairs, blocks = half // 128, count // SHORT
    some = pl.BlockSpec((SHORT, 128), lambda j, i, flag: (i, j))
    every = pl.BlockSpec((count, 128), lambda j, i, flag: (0, j))
    return call(
        attend_kernel,
        (pairs, blocks),
        1,
        [some, every, every],
        [some, pl.BlockSpec((1, 1, count, 2 * SHORT), lambda j, i, flag: (j, i, 0, 0))],
        [shaped(q.shape, bf16), shaped((pairs, blocks, count, 2 * SHORT), bf16)],
        [pltpu.VMEM((128, count), bf16)],
        4 * 4 * count * count * half,
        28 << 20,
        48,
    )(flag, q, k, v)


def branch_kernel(me_ref, att_ref, w_ref, out_ref):
    wide = w_ref.shape[3]
    for step in range(BLOCKS):
        start = pl.multiple_of((me_ref[0] ^ step) * wide, wide)
        weight = w_ref[step].reshape(att_ref.shape[1], wide)
        out_ref[:, pl.ds(start, wide)] = dot_nn(att_ref[...], weight).astype(bf16)


def branch_call(me, attended, weights):
    count, half = attended.shape
    width = weights.shape[0] * weights.shape[3]
    tile = count // 4
    block = weights.shape[:2] + (128,) + weights.shape[3:]
    return call(
        branch_kernel,
        (count // tile,),
        1,
        [
            pl.BlockSpec((tile, half), lambda i, me: (i, 0)),
            pl.BlockSpec(block, lambda i, me: (0, 0, 3, 0)),
        ],
        pl.BlockSpec((tile, width), lambda i, me: (i, 0)),
        shaped((count, width), bf16),
        [],
        2 * count * width * half,
        5 << 20,
        24,
    )(me, attended, weights)


def middle_kernel(x_ref, one_ref, two_ref, gain_ref, middle_ref, normed_ref):
    middle = x_ref[...].astype(f32) + (one_ref[...].astype(f32) + two_ref[...].astype(f32))
    middle_ref[...] = middle
    normed_ref[...] = (middle * rms_of(middle) * gain_ref[1:2, :]).astype(bf16)


def middle_call(rows, one, two, gain):
    count, width = rows.shape
    tile = count // 4
    spec = pl.BlockSpec((tile, width), lambda i: (i, 0))
    return call(
        middle_kernel,
        (count // tile,),
        0,
        [spec, spec, spec, pl.BlockSpec((8, width), lambda i: (0, 0))],
        [spec, spec],
        [shaped(rows.shape, f32), shaped(rows.shape, bf16)],
        [],
        0,
        14 << 20,
        32,
    )(rows, one, two, gain)


def ffn_kernel(prior, me_ref, normed_ref, d_out_ref, *refs):
    pieces_of, refs = refs[:5], refs[5:]
    before = refs[:2] if prior else None
    refs = refs[2 if prior else 0 :]
    result_ref, d_normed_ref = refs[:2]
    grad_refs = refs[2:6]
    weights, inner_t, gate_t, up_t = refs[6:]
    pieces, rows_all, wide = pieces_of[0].shape
    parts, kinds, depth = BLOCKS, 3, rows_all // 3
    units = pieces * depth
    tile = SHORT

    def columns(step):
        return pl.ds(pl.multiple_of((me_ref[0] ^ step) * wide, wide), wide)

    for kind in range(kinds):
        rows = slice(kind * depth, (kind + 1) * depth)
        for step in range(parts - 1):
            piece = pieces_of[step][:, rows, :]
            weights[kind, :, columns(step)] = piece.reshape(units, wide)
        for side in range(2):
            piece = pieces_of[parts - 1 + side][:, rows, :].reshape(units // 2, wide)
            weights[kind, side * units // 2 : (side + 1) * units // 2, columns(parts - 1)] = piece

    def rows_step(index, carry):
        rows = pl.ds(pl.multiple_of(index * tile, tile), tile)
        normed = normed_ref[rows, :]
        gate, up = dot_nt(normed, weights[0]), dot_nt(normed, weights[1])
        d_inner = dot_nt(d_out_ref[rows, :], weights[2])
        square = gate * gate
        bent = jnp.tanh(gate * (0.7978845608 + 0.7978845608 * 0.044715 * square))
        half = 0.5 + 0.5 * bent
        gelu = gate * half
        slope = half + gate * (0.5 - 0.5 * bent * bent) * (
            0.7978845608 + 0.7978845608 * 3 * 0.044715 * square
        )
        inner = (gelu * up).astype(bf16)
        d_gate = (d_inner * up * slope).astype(bf16)
        d_up = (d_inner * gelu).astype(bf16)
        inner_t[:, rows] = inner.T
        gate_t[:, rows] = d_gate.T
        up_t[:, rows] = d_up.T
        forward = dot_nn(inner, weights[2])
        backward = dot_nn(d_gate, weights[0]) + dot_nn(d_up, weights[1])
        if prior:
            forward += before[0][rows, :].astype(f32)
            backward += before[1][rows, :].astype(f32)
        result_ref[rows, :] = forward.astype(bf16)
        d_normed_ref[rows, :] = backward.astype(bf16)
        return carry

    lax.fori_loop(0, normed_ref.shape[0] // tile, rows_step, 0)
    for step in range(parts):
        here, there = normed_ref[:, columns(step)], d_out_ref[:, columns(step)]
        for kind, (left, right) in enumerate(((gate_t, here), (up_t, here), (inner_t, there))):
            grad = dot_nn(left[...], right).astype(bf16)
            store_grad(grad_refs, step, grad.reshape(pieces, depth, wide), kind * depth)


def ffn_call(me, normed, d_out, weights, *before):
    count, width = normed.shape
    pieces, rows_all, wide = weights[0].shape
    units = pieces * rows_all // 3
    whole = pl.BlockSpec(memory_space=pltpu.VMEM)
    return call(
        functools.partial(ffn_kernel, bool(before)),
        (),
        1,
        [whole] * (2 + len(weights) + len(before)),
        [whole] * 6,
        [shaped(normed.shape, bf16)] * 2 + grad_shapes(pieces, rows_all, wide),
        [pltpu.VMEM((3, units, width), bf16)] + [pltpu.VMEM((units, count), bf16)] * 3,
        18 * count * width * units,
        20 << 20,
        56,
    )(me, normed, d_out, *weights, *before)


def turn_kernel(
    me_ref, middle_ref, one_ref, two_ref, cot_ref, gain_ref, w_ref, d_middle_ref, d_branch_ref, d_att_ref, gain_grad_ref
):
    middle = middle_ref[...]
    rms = rms_of(middle)
    scaled = middle * rms
    d_normed = one_ref[...].astype(f32) + two_ref[...].astype(f32)
    pulled = d_normed * gain_ref[1:2, :]
    d_middle = cot_ref[...].astype(f32) + rms * (
        pulled - scaled * jnp.mean(pulled * scaled, axis=-1, keepdims=True)
    )
    d_middle_ref[...] = d_middle
    d_branch_ref[...] = d_middle.astype(bf16)

    @pl.when(pl.program_id(0) == 0)
    def _():
        gain_grad_ref[...] = jnp.zeros_like(gain_grad_ref)

    gain_grad_ref[...] += jnp.sum(d_normed * scaled, axis=0, keepdims=True)
    wide = w_ref.shape[3]
    total = None
    for step in range(BLOCKS):
        start = pl.multiple_of((me_ref[0] ^ step) * wide, wide)
        piece = dot_nt(d_branch_ref[:, pl.ds(start, wide)], w_ref[step].reshape(d_att_ref.shape[1], wide))
        total = piece if total is None else total + piece
    d_att_ref[...] = total.astype(bf16)


def turn_call(me, middle, one, two, cot, gain, weights):
    count, width = middle.shape
    half = weights.shape[1] * 128
    tile = count // 4
    spec = pl.BlockSpec((tile, width), lambda i, me: (i, 0))
    line = pl.BlockSpec((1, width), lambda i, me: (0, 0))
    gain_spec = pl.BlockSpec((8, width), lambda i, me: (0, 0))
    block = weights.shape[:2] + (128,) + weights.shape[3:]
    return call(
        turn_kernel,
        (count // tile,),
        1,
        [spec, spec, spec, spec, gain_spec, pl.BlockSpec(block, lambda i, me: (0, 0, 3, 0))],
        [spec, spec, pl.BlockSpec((tile, half), lambda i, me: (i, 0)), line],
        [
            shaped(middle.shape, f32),
            shaped(middle.shape, bf16),
            shaped((count, half), bf16),
            shaped((1, width), f32),
        ],
        [],
        2 * count * width * half,
        22 << 20,
        40,
    )(me, middle, one, two, cot, gain, weights)


def attend_back_kernel(
    flag_ref, q_ref, k_ref, v_ref, out_ref, d_out_ref, probs_ref, dq_ref, dk_ref, dv_ref, k_turned, dk_sum, dv_sum
):
    block, blocks = pl.program_id(1), pl.num_programs(1)

    @pl.when(block == 0)
    def _():
        k_turned[...] = k_ref[...].T

    queries, grads = two_heads(q_ref[...]), two_heads(d_out_ref[...])
    turned = (d_out_ref[...].astype(f32) * out_ref[...].astype(f32)).T
    delta = jnp.concatenate(
        [
            jnp.sum(turned[:HEAD], axis=0, keepdims=True),
            jnp.sum(turned[HEAD:], axis=0, keepdims=True),
        ],
        axis=1,
    )

    def back(values, keys_turned):
        probs = probs_ref[0, 0, : values.shape[0], :]
        d_probs = dot_nt(values, grads)
        d_scores = (probs.astype(f32) * (d_probs - delta)).astype(bf16)
        d_query = one_pair(dot_nn(keys_turned, d_scores)).T * (HEAD**-0.5)
        dq_ref[...] = d_query.astype(bf16)
        return dot_nn(d_scores, queries), dot_nn(probs, grads)

    @pl.when(flag_ref[0] == 1)
    def _():
        d_key, d_value = back(v_ref[...], k_turned[...])

        @pl.when(block == 0)
        def _():
            dk_sum[...] = d_key
            dv_sum[...] = d_value

        @pl.when(block > 0)
        def _():
            dk_sum[...] += d_key
            dv_sum[...] += d_value

    @pl.when(flag_ref[0] != 1)
    def _():
        rows = pl.ds(pl.multiple_of(block * SHORT, SHORT), SHORT)
        d_key, d_value = back(v_ref[rows, :], k_turned[:, rows])
        dk_sum[rows, :] = d_key
        dv_sum[rows, :] = d_value

    @pl.when(block == blocks - 1)
    def _():
        dk_ref[...] = dk_sum[...].astype(bf16)
        dv_ref[...] = dv_sum[...].astype(bf16)


def attend_back_call(flag, q, k, v, out, d_out, probs):
    count, half = q.shape
    pairs, blocks = half // 128, count // SHORT
    some = pl.BlockSpec((SHORT, 128), lambda j, i, flag: (i, j))
    every = pl.BlockSpec((count, 128), lambda j, i, flag: (0, j))
    return call(
        attend_back_kernel,
        (pairs, blocks),
        1,
        [
            some,
            every,
            every,
            some,
            some,
            pl.BlockSpec((1, 1, count, 2 * SHORT), lambda j, i, flag: (j, i, 0, 0)),
        ],
        [some, every, every],
        [shaped(q.shape, bf16)] * 3,
        [pltpu.VMEM((128, count), bf16)] + [pltpu.VMEM((count, 128), f32)] * 2,
        4 * 8 * count * count * half,
        30 << 20,
        48,
    )(flag, q, k, v, out, d_out, probs)


def square_kernel(
    me_ref, dq_ref, dk_ref, dv_ref, att_ref, hidden_ref, d_branch_ref, w_ref, x_ref, rms_ref, line_ref, d_hidden_ref, *refs
):
    grad_refs, turned = refs[:4], refs[4]
    lefts = (dq_ref, dk_ref, dv_ref, att_ref)

    @pl.when(pl.program_id(0) == 0)
    def _():
        for part, ref in enumerate(lefts):
            turned[part] = ref[...].T

    pieces, wide = w_ref.shape[1], w_ref.shape[3]

    def put(grad, first):
        for step in range(BLOCKS):

            @pl.when(pl.program_id(0) == step)
            def _():
                store_grad(grad_refs, step, grad, first)

    total = None
    for part, ref in enumerate(lefts):
        rows = slice(part * 128, (part + 1) * 128)
        right = d_branch_ref if part == 3 else hidden_ref
        grad = dot_nn(turned[part], right[...])
        put(grad.reshape(pieces, 128, wide).astype(bf16), part * 128)
        if part < 3:
            piece = dot_nn(ref[...], w_ref[0, :, rows, :].reshape(pieces * 128, wide))
            total = piece if total is None else total + piece
    d_hidden_ref[...] = total.astype(bf16)
    scaled = x_ref[...].astype(f32) * rms_ref[:, :1]
    attn = jnp.sum(total * scaled, axis=0, keepdims=True)
    lines = jnp.concatenate([attn, line_ref[...], jnp.zeros((14, wide), f32)], axis=0).astype(bf16)
    put(jnp.broadcast_to(lines[None], (pieces, 16, wide)), 4 * 128)


def square_call(me, dq, dk, dv, attended, hidden, d_branch, weights, x_rows, rms, line):
    count, half = dq.shape
    width = hidden.shape[1]
    parts, pieces, depth, wide = weights.shape
    every = pl.BlockSpec((count, half), lambda d, me: (0, 0))
    column = pl.BlockSpec((count, wide), lambda d, me: (0, me[0] ^ d))
    return call(
        square_kernel,
        (parts,),
        1,
        [every] * 4
        + [column, column, pl.BlockSpec((1, pieces, depth, wide), lambda d, me: (d, 0, 0, 0))]
        + [column, pl.BlockSpec(rms.shape, lambda d, me: (0, 0))]
        + [pl.BlockSpec((1, wide), lambda d, me: (0, me[0] ^ d))],
        [column] + [pl.BlockSpec((2, pieces // 2, depth, wide), lambda d, me: (0, 0, 0, 0))] * 4,
        [shaped(hidden.shape, bf16)] + grad_shapes(pieces, depth, wide),
        [pltpu.VMEM((4, half, count), bf16)],
        14 * count * width * half,
        24 << 20,
        40,
    )(me, dq, dk, dv, attended, hidden, d_branch, weights, x_rows, rms, line)


def output_kernel(core_ref, middle_ref, own_ref, other_ref, out_ref):
    out_ref[0] = (
        middle_ref[0, 0] + (own_ref[0, 0].astype(f32) + other_ref[0].astype(f32))
    ).astype(bf16)


def output_call(core, middle, own, other):
    slots, halves, tile, width = own.shape
    mine = pl.BlockSpec((1, 1, tile, width), lambda i, core: (i, core[0], 0, 0))
    plain = pl.BlockSpec((1, tile, width), lambda i, core: (i, 0, 0))
    return call(
        output_kernel,
        (slots,),
        1,
        [mine, mine, plain],
        plain,
        shaped((slots, tile, width), bf16),
        [],
        0,
        6 << 20,
        16,
    )(core, middle.reshape(own.shape), own, other)


def input_kernel(core_ref, x_ref, d_middle_ref, own_ref, other_ref, gain_ref, out_ref):
    rows = x_ref[0, 0].astype(f32)
    rms = rms_of(rows)
    scaled = rows * rms
    d_hidden = own_ref[0, 0].astype(f32) + other_ref[0].astype(f32)
    pulled = d_hidden * gain_ref[:1, :]
    out_ref[0] = (
        d_middle_ref[0, 0]
        + rms * (pulled - scaled * jnp.mean(pulled * scaled, axis=-1, keepdims=True))
    ).astype(bf16)


def input_call(core, rows, d_middle, own, other, gains):
    slots, halves, tile, width = own.shape
    mine = pl.BlockSpec((1, 1, tile, width), lambda i, core: (i, core[0], 0, 0))
    plain = pl.BlockSpec((1, tile, width), lambda i, core: (i, 0, 0))
    return call(
        input_kernel,
        (slots,),
        1,
        [mine, mine, mine, plain, pl.BlockSpec((8, width), lambda i, core: (0, 0))],
        plain,
        shaped((slots, tile, width), bf16),
        [],
        0,
        8 << 20,
        16,
    )(core, rows.reshape(own.shape), d_middle.reshape(own.shape), own, other, gains)


def per_device(
    inputs,
    bucket,
    attn_gain,
    w_query,
    w_key,
    w_value,
    w_out,
    ffn_gain,
    w_gate,
    w_up,
    w_down,
    cotangent,
):
    dp, narrow = lax.axis_size("dp"), lax.axis_size("narrow")
    chips = dp // 2
    core, chip = lax.axis_index("dp") % 2, lax.axis_index("dp") // 2
    place = lax.axis_index("narrow")
    same_core = [[2 * m + c for m in range(chips)] for c in range(2)]
    by_core = core == 0
    bundle, row_count, width = inputs.shape
    tile = row_count // 2
    own_width = w_query.shape[0]
    wide = width // BLOCKS

    def to_core(value):
        return lax.ppermute(value, "dp", [(i, i ^ 1) for i in range(dp)])

    def to_chip(value, flip):
        return lax.ppermute(value, "dp", [(i, i ^ (2 * flip)) for i in range(dp)])

    def along(value, shift):
        return lax.ppermute(
            value, "narrow", [(i, (i + shift) % narrow) for i in range(narrow)]
        )

    def stage(values, *done):
        return lax.optimization_barrier((values, done))[0]

    def ordered(mine, theirs, axis):
        join = functools.partial(jnp.concatenate, axis=axis)
        return jnp.where(by_core, join([mine, theirs]), join([theirs, mine]))

    def pick(value, index, axis):
        return lax.dynamic_index_in_dim(value, index, axis, keepdims=False)

    def mine_of(value, axis):
        low, high = (lax.index_in_dim(value, i, axis, keepdims=False) for i in range(2))
        return jnp.where(by_core, low, high), jnp.where(by_core, high, low)

    def blocks_for(value):
        return [pick(value, (place + k) % narrow, 0) for k in range(narrow)]

    def across(blocks):
        return [blocks[0]] + [along(blocks[k], k) for k in range(1, narrow)]

    def in_order(moved):
        stacked = jnp.stack(moved)
        order = (place - jnp.arange(narrow)) % narrow
        return jnp.stack([pick(stacked, order[i], 0) for i in range(narrow)])

    def group_start(value):
        keep, give = mine_of(value.reshape(bundle, 2, tile, width), 1)
        return ordered(keep, to_core(give), 0)

    def group_end(moved):
        mine = in_order(moved)
        other = to_core(mine)
        return ordered(mine[:, None], other[:, None], 1).reshape(-1, width)

    def group_back(moved):
        mine, give = mine_of(in_order(moved).reshape(2, bundle, tile, width), 0)
        theirs = to_core(give)
        return ordered(mine[:, None], theirs[:, None], 1).reshape(bundle, row_count, width)

    def halves_of(*parts):
        keep, give = mine_of(jnp.concatenate(parts, axis=1), 0)
        return ordered(keep, to_core(give), 1)

    def two(part):
        return part.reshape(2, part.shape[0] // 2, own_width)

    def canonical(value):
        if chips == BLOCKS:
            return value
        parts = value.reshape((BLOCKS, chips // BLOCKS) + value.shape[1:])
        return jnp.moveaxis(parts, 1, -2).reshape((BLOCKS,) + value.shape[1:-1] + (wide,))

    def scattered(value):
        if chips == BLOCKS:
            return value
        parts = value.reshape(value.shape[:-1] + (chips // BLOCKS, width // chips))
        return jnp.moveaxis(parts, -2, 1).reshape(
            (chips,) + value.shape[1:-1] + (width // chips,)
        )

    def spread(value):
        return [value] + [along(value, k) for k in range(1, narrow)]

    near = chips == BLOCKS

    def chips_first(value):
        return (to_chip(value, 1), to_chip(value, 2)) if near else ()

    def chips_second(first, second):
        return to_chip(first[: narrow // 2], 2), to_chip(second[narrow // 2 :], 1)

    def chips_full(value, firsts, seconds):
        if near:
            return jnp.stack([value, *firsts, jnp.concatenate(seconds)])
        return canonical(lax.all_gather(value, "dp", axis_index_groups=same_core))

    def chips_pieces(value, firsts, seconds):
        if near:
            return (value, *firsts, *seconds)
        full = chips_full(value, firsts, seconds)
        return full[0], full[1], full[2], full[3, : narrow // 2], full[3, narrow // 2 :]

    def sum_first(grads):
        x_keep, x_send, y_keep, y_send = grads
        return to_chip(x_send, 1), to_chip(y_send, 2)

    def sum_ready(grads, got):
        x_keep, _, y_keep, _ = grads
        return (
            (x_keep[1].astype(f32) + got[0][1].astype(f32)).astype(bf16),
            (y_keep[1].astype(f32) + got[1][1].astype(f32)).astype(bf16),
        )

    def sum_second(ready):
        return to_chip(ready[0], 2), to_chip(ready[1], 1)

    def sum_done(grads, got, last):
        x_keep, _, y_keep, _ = grads
        x_sum = x_keep[0].astype(f32) + got[0][0].astype(f32) + last[0].astype(f32)
        y_sum = y_keep[0].astype(f32) + got[1][0].astype(f32) + last[1].astype(f32)
        sent = [x_sum[k] for k in range(1, narrow // 2)] + [y_sum[k] for k in range(narrow // 2)]
        return x_sum[0], [block.astype(bf16) for block in sent]

    def sum_far(grads):
        x_keep, x_send, y_keep, y_send = grads
        x_all = jnp.stack([x_keep, x_send], axis=1).reshape((BLOCKS,) + x_keep.shape[1:])
        y_all = jnp.concatenate([y_keep, y_send])
        value = scattered(
            jnp.concatenate([x_all, y_all], axis=1).reshape(BLOCKS, narrow, -1, wide)
        )
        got = lax.psum_scatter(
            value.reshape(-1, value.shape[-1]),
            "dp",
            scatter_dimension=0,
            tiled=True,
            axis_index_groups=same_core,
        ).reshape(value.shape[1:])
        return got[0].astype(f32), [got[k] for k in range(1, narrow)]

    def sum_places(sent):
        return [along(block, -k) for k, block in enumerate(sent, 1)]

    def swap_ready(own, got):
        total = own
        for piece in got:
            total = total + piece.astype(f32)
        low, high = total[:, :own_width], total[:, own_width:]
        return jnp.where(by_core, low, high), jnp.where(by_core, high, low).astype(bf16)

    def finish(keep, theirs, parts, size):
        theirs = theirs.astype(f32)
        both = jnp.where(by_core, jnp.stack([keep, theirs]), jnp.stack([theirs, keep]))
        return [both[:, i * size : (i + 1) * size] for i in range(parts)]

    extra = jnp.concatenate(
        [
            attn_gain[None],
            ffn_gain[None],
            jnp.pad(bucket.astype(bf16), (0, own_width - bundle))[None],
            jnp.zeros((13, own_width), bf16),
        ]
    )
    square = halves_of(
        two(w_query.T), two(w_key.T), two(w_value.T), two(w_out), jnp.stack([extra, extra])
    )
    kinds = [two(w_gate.T), two(w_up.T), two(w_down)]
    depth = kinds[0].shape[1]
    cut = -(-depth // 32 // 2) * 32
    me = (chip if near else 0 * chip).astype(jnp.int32)[None]
    core_index = core.astype(jnp.int32)[None]

    square_z = spread(square)
    x_blocks = blocks_for(group_start(inputs))

    square_z, x_blocks = stage((square_z, x_blocks))
    square_z = jnp.stack(square_z)
    square_first = chips_first(square_z)
    x_moved = across(x_blocks)
    ffn_one = halves_of(*[kind[:, :cut] for kind in kinds])

    square_first, x_moved, ffn_one = stage((square_first, x_moved, ffn_one))
    square_second = chips_second(*square_first) if near else ()
    one_z = spread(ffn_one)
    x_rows = group_end(x_moved)
    square_full = chips_full(square_z, square_first, square_second)
    hidden, rms, gains, q, k, v = qkv_call(me, x_rows, square_full)
    flags = square[4 * 128 + 2].reshape(2, own_width)[:, :bundle].reshape(-1)
    flag = pick(flags.astype(jnp.int32), place, 0)[None]
    ffn_two = halves_of(*[kind[:, cut:] for kind in kinds])

    q, one_z, ffn_two = stage((q, one_z, ffn_two))
    one_z = jnp.stack(one_z)
    one_first = chips_first(one_z)
    two_z = spread(ffn_two)
    attended, probs = attend_call(flag, q, k, v)
    cot_blocks = blocks_for(group_start(cotangent))

    attended, two_z, one_first, cot_blocks = stage((attended, two_z, one_first, cot_blocks))
    one_second = chips_second(*one_first) if near else ()
    cot_moved = across(cot_blocks)
    branch = branch_call(me, attended, square_full)
    branch, one_second = stage((branch, one_second))
    branch_other = to_core(branch)

    two_z, branch_other = stage((two_z, branch_other))
    two_z = jnp.stack(two_z)
    two_first = chips_first(two_z)
    middle, normed = middle_call(x_rows, branch, branch_other, gains)

    cot_moved, normed, two_first = stage((cot_moved, normed, two_first))
    two_second = chips_second(*two_first) if near else ()
    cot_rows = group_end(cot_moved)
    part_result, part_d_normed, *one_grads = ffn_call(
        me, normed, cot_rows, chips_pieces(one_z, one_first, one_second)
    )

    part_result, part_d_normed, one_grads, two_second = stage(
        (part_result, part_d_normed, one_grads, two_second)
    )
    one_got = sum_first(one_grads) if near else ()
    result, d_normed, *two_grads = ffn_call(
        me,
        normed,
        cot_rows,
        chips_pieces(two_z, two_first, two_second),
        part_result,
        part_d_normed,
    )

    result, d_normed, two_grads, one_got = stage((result, d_normed, two_grads, one_got))
    by_rows = (narrow, 2, tile, width)
    d_normed_other = to_core(d_normed)
    one_last = sum_second(sum_ready(one_grads, one_got)) if near else ()
    d_middle, d_branch, d_att, ffn_gain_grad = turn_call(
        me, middle, d_normed, d_normed_other, cot_rows, gains, square_full
    )
    result = result.reshape(by_rows)
    result_other = to_core(mine_of(result, 1)[1])
    out_blocks = blocks_for(output_call(core_index, middle, result, result_other))

    d_att, out_blocks, one_last, two_grads = stage((d_att, out_blocks, one_last, two_grads))
    two_got = sum_first(two_grads) if near else ()
    out_moved = across(out_blocks)
    dq, dk, dv = attend_back_call(flag, q, k, v, attended, d_att, probs)
    one_own, one_sent = sum_done(one_grads, one_got, one_last) if near else sum_far(one_grads)

    dq, one_sent, two_got, out_moved = stage((dq, one_sent, two_got, out_moved))
    two_last = sum_second(sum_ready(two_grads, two_got)) if near else ()
    one_places = sum_places(one_sent)
    d_hidden, *square_grads = square_call(
        me, dq, dk, dv, attended, hidden, d_branch, square_full, x_rows, rms, 0.5 * ffn_gain_grad
    )
    outputs = group_back(out_moved)

    d_hidden, square_grads, two_last, one_places = stage(
        (d_hidden, square_grads, two_last, one_places)
    )
    square_got = sum_first(square_grads) if near else ()
    d_hidden = d_hidden.reshape(by_rows)
    d_hidden_other = to_core(mine_of(d_hidden, 1)[1])
    two_own, two_sent = sum_done(two_grads, two_got, two_last) if near else sum_far(two_grads)
    two_sent, d_hidden_other = stage((two_sent, d_hidden_other))
    two_places = sum_places(two_sent)
    input_blocks = blocks_for(
        input_call(core_index, x_rows, d_middle, d_hidden, d_hidden_other, gains)
    )
    one_keep, one_swap = swap_ready(one_own, one_places)

    input_blocks, square_got, two_places, one_swap = stage(
        (input_blocks, square_got, two_places, one_swap)
    )
    square_last = sum_second(sum_ready(square_grads, square_got)) if near else ()
    input_moved = across(input_blocks)
    one_theirs = to_core(one_swap)
    two_keep, two_swap = swap_ready(two_own, two_places)
    two_theirs = to_core(two_swap)

    square_last, input_moved = stage((square_last, input_moved))
    square_own, square_sent = (
        sum_done(square_grads, square_got, square_last) if near else sum_far(square_grads)
    )
    square_places = sum_places(square_sent)
    input_grad = group_back(input_moved).astype(f32)
    one_parts = finish(one_keep, one_theirs, 3, cut)
    two_parts = finish(two_keep, two_theirs, 3, depth - cut)
    g_gate, g_up, g_down = [
        jnp.concatenate(parts, axis=1).reshape(2 * depth, own_width)
        for parts in zip(one_parts, two_parts)
    ]
    square_keep, square_swap = swap_ready(square_own, square_places)
    square_theirs = to_core(square_swap)
    g_query, g_key, g_value, g_out = [
        part.reshape(-1, own_width) for part in finish(square_keep, square_theirs, 4, 128)
    ]
    gain_own = square_keep[4 * 128 :] + square_theirs[4 * 128 :].astype(f32)
    return (
        outputs,
        input_grad,
        gain_own[0],
        g_query.T,
        g_key.T,
        g_value.T,
        g_out,
        gain_own[1],
        g_gate.T,
        g_up.T,
        g_down,
    )


def solution(mesh):
    rows = P("dp", "narrow", None)
    tall, flat = P("dp", "narrow"), P("narrow", "dp")
    return jax.shard_map(
        per_device,
        mesh=mesh,
        in_specs=(rows, P("dp"), P("dp"), tall, tall, tall, flat, P("dp"), tall, tall, flat, rows),
        out_specs=(rows, rows, P("dp"), tall, tall, tall, flat, P("dp"), tall, tall, flat),
        check_vma=False,
    )
```

```python
import functools

import jax
import jax.numpy as jnp
from jax import lax
from jax.experimental import pallas as pl
from jax.experimental.pallas import tpu as pltpu
from jax.sharding import PartitionSpec as P

HEAD = 64
SHORT = 384
EPS = 1e-06
BLOCKS = 4
f32 = jnp.float32
bf16 = jnp.bfloat16


def dot_nn(left, right):
    return jnp.dot(left, right, preferred_element_type=f32)


def dot_nt(left, right):
    return lax.dot_general(left, right, (((1,), (1,)), ((), ())), preferred_element_type=f32)


def call(kernel, grid, prefetch, in_specs, out_specs, out_shape, scratch, flops, moved, vmem):
    return pl.pallas_call(
        kernel,
        grid_spec=pltpu.PrefetchScalarGridSpec(
            num_scalar_prefetch=prefetch,
            grid=grid,
            in_specs=in_specs,
            out_specs=out_specs,
            scratch_shapes=scratch,
        ),
        out_shape=out_shape,
        compiler_params=pltpu.CompilerParams(vmem_limit_bytes=vmem << 20),
        cost_estimate=pl.CostEstimate(flops=flops, bytes_accessed=moved, transcendentals=0),
    )


def shaped(shape, dtype):
    return jax.ShapeDtypeStruct(shape, dtype)


def rms_of(rows):
    return lax.rsqrt(jnp.mean(rows * rows, axis=-1, keepdims=True) + EPS)


def store_grad(refs, step, grad, first):
    x_keep, x_send, y_keep, y_send = refs
    half, rows = grad.shape[0] // 2, slice(first, first + grad.shape[1])
    (x_send if step % 2 else x_keep)[step // 2, :, rows] = grad[:half]
    (y_send if step // 2 else y_keep)[step % 2, :, rows] = grad[half:]


def grad_shapes(pieces, rows, wide):
    return [shaped((2, pieces // 2, rows, wide), bf16)] * 4


def square_split_kernel(
    core_ref, bucket_ref, q_ref, k_ref, v_ref, o_ref, attn_ref, ffn_ref, keep_ref, give_ref
):
    halves = [ref[...].T for ref in (q_ref, k_ref, v_ref)] + [o_ref[...]]
    shape = (16, keep_ref.shape[1])
    row, lane = (lax.broadcasted_iota(jnp.int32, shape, axis) for axis in range(2))
    flags = jnp.zeros(shape, f32)
    for i in range(bucket_ref.shape[0]):
        flags = jnp.where(lane == i, bucket_ref[i].astype(f32), flags)
    flags = jnp.where(row == 2, flags, 0.0)
    flags = jnp.where(row == 1, ffn_ref[...].astype(f32), flags)
    extra = jnp.where(row == 0, attn_ref[...].astype(f32), flags).astype(bf16)

    def store(low_ref, high_ref):
        start = 0
        for half in halves:
            count = half.shape[0] // 2
            low_ref[start : start + count] = half[:count]
            high_ref[start : start + count] = half[count:]
            start += count
        low_ref[start:] = extra
        high_ref[start:] = extra

    @pl.when(core_ref[0] == 0)
    def _():
        store(keep_ref, give_ref)

    @pl.when(core_ref[0] != 0)
    def _():
        store(give_ref, keep_ref)


def square_split_call(core, bucket, q, k, v, o, attn, ffn):
    rows, cols = q.shape[1] // 2 * 4 + 16, o.shape[1]
    whole = pl.BlockSpec(memory_space=pltpu.VMEM)
    return call(
        square_split_kernel,
        (),
        2,
        [whole] * 6,
        [whole] * 2,
        [shaped((rows, cols), bf16)] * 2,
        [],
        0,
        1 << 20,
        16,
    )(core, bucket, q, k, v, o, attn[None], ffn[None])


def ffn_split_kernel(cut, core_ref, *refs):
    parts, (keep_ref, give_ref) = refs[:3], refs[3:]

    def store(low_ref, high_ref):
        start = 0
        half = parts[0].shape[0] // 2
        for first, last in ((0, cut), (cut, half)):
            for part in parts:
                count = last - first
                low_ref[start : start + count] = part[first:last]
                high_ref[start : start + count] = part[half + first : half + last]
                start += count

    @pl.when(core_ref[0] == 0)
    def _():
        store(keep_ref, give_ref)

    @pl.when(core_ref[0] != 0)
    def _():
        store(give_ref, keep_ref)


def ffn_split_call(core, cut, gate, up, down):
    rows, cols = gate.shape[0] // 2 * 3, gate.shape[1]
    whole = pl.BlockSpec(memory_space=pltpu.VMEM)
    return call(
        functools.partial(ffn_split_kernel, cut),
        (),
        1,
        [whole] * 3,
        [whole] * 2,
        [shaped((rows, cols), bf16)] * 2,
        [],
        0,
        1 << 20,
        16,
    )(core, gate, up, down)


def join_rows(core_ref, own_ref, other_ref, out_ref):
    count = own_ref.shape[1]

    @pl.when(core_ref[0] == 0)
    def _():
        out_ref[:count] = own_ref[0]
        out_ref[count:] = other_ref[0]

    @pl.when(core_ref[0] != 0)
    def _():
        out_ref[:count] = other_ref[0]
        out_ref[count:] = own_ref[0]


def qkv_kernel(
    me_ref, core_ref, place_ref, own_ref, other_ref, w_ref, x_ref, hidden_ref, rms_ref, gains_ref, q_ref, k_ref, v_ref
):
    join_rows(core_ref, own_ref, other_ref, x_ref)
    rows = x_ref[...].astype(f32)
    rms = rms_of(rows)
    rms_ref[...] = jnp.broadcast_to(rms, rms_ref.shape)
    wide = w_ref.shape[3]
    half = w_ref.shape[1] * 128
    for step in range(BLOCKS):
        columns = pl.ds(pl.multiple_of((me_ref[0] ^ step) * wide, wide), wide)
        gains = w_ref[step, 0, 4 * 128 :, :].astype(f32)
        gains_ref[:, columns] = gains[:8]
        hidden_ref[:, columns] = (x_ref[:, columns].astype(f32) * rms * gains[:1]).astype(bf16)
    for part, ref in enumerate((q_ref, k_ref, v_ref)):
        total = None
        for step in range(BLOCKS):
            start = pl.multiple_of((me_ref[0] ^ step) * wide, wide)
            weight = w_ref[step, :, part * 128 : (part + 1) * 128, :].reshape(half, wide)
            piece = dot_nt(hidden_ref[:, pl.ds(start, wide)], weight)
            total = piece if total is None else total + piece
        if part == 0:
            total = total * (HEAD**-0.5)
        ref[...] = total.astype(bf16)


def qkv_call(me, core, place, own, other, weights):
    places, half_tile, width = own.shape
    half = weights.shape[1] * 128
    tile, count = 2 * half_tile, 2 * half_tile * places
    row_spec = pl.BlockSpec((tile, width), lambda i, me, core, place: (i, 0))
    half_spec = pl.BlockSpec((tile, half), lambda i, me, core, place: (i, 0))
    part_spec = pl.BlockSpec(
        (1, half_tile, width), lambda i, me, core, place: ((place[0] + places - i) % places, 0, 0)
    )
    return call(
        qkv_kernel,
        (places,),
        3,
        [
            part_spec,
            part_spec,
            pl.BlockSpec(weights.shape, lambda i, me, core, place: (0, 0, 0, 0)),
        ],
        [
            row_spec,
            row_spec,
            pl.BlockSpec((tile, 128), lambda i, me, core, place: (i, 0)),
            pl.BlockSpec((8, width), lambda i, me, core, place: (0, 0)),
            half_spec,
            half_spec,
            half_spec,
        ],
        [shaped((count, width), bf16)] * 2
        + [shaped((count, 128), f32), shaped((8, width), f32)]
        + [shaped((count, half), bf16)] * 3,
        [],
        2 * count * width * half * 3,
        12 << 20,
        40,
    )(me, core, place, own, other, weights)


def two_heads(rows):
    low = lax.broadcasted_iota(jnp.int32, rows.shape, 1) < HEAD
    zero = jnp.zeros_like(rows)
    return jnp.concatenate([jnp.where(low, rows, zero), jnp.where(low, zero, rows)], axis=0)


def one_pair(both):
    half = both.shape[1] // 2
    return jnp.concatenate([both[:HEAD, :half], both[HEAD:, half:]], axis=0)


def attend_kernel(flag_ref, q_ref, k_ref, v_ref, out_ref, probs_ref, v_turned):
    block = pl.program_id(1)

    @pl.when(block == 0)
    def _():
        v_turned[...] = v_ref[...].T

    queries = two_heads(q_ref[...])

    def attend(keys, values):
        scores = dot_nt(keys, queries)
        expo = jnp.exp(scores - jnp.max(scores, axis=0, keepdims=True))
        probs = (expo * (1.0 / jnp.sum(expo, axis=0, keepdims=True))).astype(bf16)
        probs_ref[0, 0, : keys.shape[0], :] = probs
        out_ref[...] = one_pair(dot_nn(values, probs)).T.astype(bf16)

    @pl.when(flag_ref[0] == 1)
    def _():
        attend(k_ref[...], v_turned[...])

    @pl.when(flag_ref[0] != 1)
    def _():
        start = pl.multiple_of(block * SHORT, SHORT)
        attend(k_ref[pl.ds(start, SHORT), :], v_turned[:, pl.ds(start, SHORT)])


def attend_call(flag, q, k, v):
    count, half = q.shape
    pairs, blocks = half // 128, count // SHORT
    some = pl.BlockSpec((SHORT, 128), lambda j, i, flag: (i, j))
    every = pl.BlockSpec((count, 128), lambda j, i, flag: (0, j))
    return call(
        attend_kernel,
        (pairs, blocks),
        1,
        [some, every, every],
        [some, pl.BlockSpec((1, 1, count, 2 * SHORT), lambda j, i, flag: (j, i, 0, 0))],
        [shaped(q.shape, bf16), shaped((pairs, blocks, count, 2 * SHORT), bf16)],
        [pltpu.VMEM((128, count), bf16)],
        4 * 4 * count * count * half,
        28 << 20,
        48,
    )(flag, q, k, v)


def branch_kernel(me_ref, att_ref, w_ref, out_ref):
    wide = w_ref.shape[3]
    for step in range(BLOCKS):
        start = pl.multiple_of((me_ref[0] ^ step) * wide, wide)
        weight = w_ref[step].reshape(att_ref.shape[1], wide)
        out_ref[:, pl.ds(start, wide)] = dot_nn(att_ref[...], weight).astype(bf16)


def branch_call(me, attended, weights):
    count, half = attended.shape
    width = weights.shape[0] * weights.shape[3]
    tile = count // 4
    block = weights.shape[:2] + (128,) + weights.shape[3:]
    return call(
        branch_kernel,
        (count // tile,),
        1,
        [
            pl.BlockSpec((tile, half), lambda i, me: (i, 0)),
            pl.BlockSpec(block, lambda i, me: (0, 0, 3, 0)),
        ],
        pl.BlockSpec((tile, width), lambda i, me: (i, 0)),
        shaped((count, width), bf16),
        [],
        2 * count * width * half,
        5 << 20,
        24,
    )(me, attended, weights)


def middle_kernel(
    core_ref, place_ref, x_ref, one_ref, two_ref, gain_ref, own_ref, other_ref, middle_ref, normed_ref, cot_ref
):
    middle = x_ref[...].astype(f32) + (one_ref[...].astype(f32) + two_ref[...].astype(f32))
    middle_ref[...] = middle
    normed_ref[...] = (middle * rms_of(middle) * gain_ref[1:2, :]).astype(bf16)
    join_rows(core_ref, own_ref, other_ref, cot_ref)


def middle_call(core, place, rows, one, two, gain, own, other):
    count, width = rows.shape
    places, half_tile = own.shape[:2]
    spec = pl.BlockSpec((2 * half_tile, width), lambda i, core, place: (i, 0))
    part_spec = pl.BlockSpec(
        (1, half_tile, width), lambda i, core, place: ((place[0] + places - i) % places, 0, 0)
    )
    return call(
        middle_kernel,
        (places,),
        2,
        [spec] * 3
        + [pl.BlockSpec((8, width), lambda i, core, place: (0, 0)), part_spec, part_spec],
        [spec] * 3,
        [shaped(rows.shape, f32), shaped(rows.shape, bf16), shaped(rows.shape, bf16)],
        [],
        0,
        14 << 20,
        32,
    )(core, place, rows, one, two, gain, own, other)


def ffn_kernel(given, prior, me_ref, normed_ref, d_out_ref, *refs):
    pieces_of, refs = refs[:given], refs[given:]
    before = refs[:2] if prior else None
    refs = refs[2 if prior else 0 :]
    result_ref, d_normed_ref = refs[:2]
    grad_refs = refs[2:6]
    weights, inner_t, gate_t, up_t = refs[6:]
    pieces, rows_all, wide = pieces_of[0].shape
    parts, kinds, depth = BLOCKS, 3, rows_all // 3
    units = pieces * depth
    tile = SHORT

    def columns(step):
        return pl.ds(pl.multiple_of((me_ref[0] ^ step) * wide, wide), wide)

    for kind in range(kinds):
        rows = slice(kind * depth, (kind + 1) * depth)
        for step in range(parts):
            start = 0
            for piece in pieces_of[step:] if step == parts - 1 else pieces_of[step : step + 1]:
                count = piece.shape[0] * depth
                value = piece[:, rows, :].reshape(count, wide)
                weights[kind, start : start + count, columns(step)] = value
                start += count

    def rows_step(index, carry):
        rows = pl.ds(pl.multiple_of(index * tile, tile), tile)
        normed = normed_ref[rows, :]
        gate, up = dot_nt(normed, weights[0]), dot_nt(normed, weights[1])
        d_inner = dot_nt(d_out_ref[rows, :], weights[2])
        square = gate * gate
        bent = jnp.tanh(gate * (0.7978845608 + 0.7978845608 * 0.044715 * square))
        half = 0.5 + 0.5 * bent
        gelu = gate * half
        slope = half + gate * (0.5 - 0.5 * bent * bent) * (
            0.7978845608 + 0.7978845608 * 3 * 0.044715 * square
        )
        inner = (gelu * up).astype(bf16)
        d_gate = (d_inner * up * slope).astype(bf16)
        d_up = (d_inner * gelu).astype(bf16)
        inner_t[:, rows] = inner.T
        gate_t[:, rows] = d_gate.T
        up_t[:, rows] = d_up.T
        forward = dot_nn(inner, weights[2])
        backward = dot_nn(d_gate, weights[0]) + dot_nn(d_up, weights[1])
        if prior:
            forward += before[0][rows, :].astype(f32)
            backward += before[1][rows, :].astype(f32)
        result_ref[rows, :] = forward.astype(bf16)
        d_normed_ref[rows, :] = backward.astype(bf16)
        return carry

    lax.fori_loop(0, normed_ref.shape[0] // tile, rows_step, 0)
    for step in range(parts):
        here, there = normed_ref[:, columns(step)], d_out_ref[:, columns(step)]
        for kind, (left, right) in enumerate(((gate_t, here), (up_t, here), (inner_t, there))):
            grad = dot_nn(left[...], right).astype(bf16)
            store_grad(grad_refs, step, grad.reshape(pieces, depth, wide), kind * depth)


def ffn_call(me, normed, d_out, weights, *before):
    count, width = normed.shape
    pieces, rows_all, wide = weights[0].shape
    units = pieces * rows_all // 3
    whole = pl.BlockSpec(memory_space=pltpu.VMEM)
    return call(
        functools.partial(ffn_kernel, len(weights), bool(before)),
        (),
        1,
        [whole] * (2 + len(weights) + len(before)),
        [whole] * 6,
        [shaped(normed.shape, bf16)] * 2 + grad_shapes(pieces, rows_all, wide),
        [pltpu.VMEM((3, units, width), bf16)] + [pltpu.VMEM((units, count), bf16)] * 3,
        18 * count * width * units,
        20 << 20,
        56,
    )(me, normed, d_out, *weights, *before)


def turn_kernel(
    me_ref,
    core_ref,
    middle_ref,
    one_ref,
    two_ref,
    cot_ref,
    gain_ref,
    w_ref,
    own_ref,
    other_ref,
    d_middle_ref,
    d_branch_ref,
    d_att_ref,
    gain_grad_ref,
    out_ref,
):
    middle = middle_ref[...]
    rms = rms_of(middle)
    scaled = middle * rms
    d_normed = one_ref[...].astype(f32) + two_ref[...].astype(f32)
    pulled = d_normed * gain_ref[1:2, :]
    d_middle = cot_ref[...].astype(f32) + rms * (
        pulled - scaled * jnp.mean(pulled * scaled, axis=-1, keepdims=True)
    )
    d_middle_ref[...] = d_middle
    d_branch_ref[...] = d_middle.astype(bf16)
    count = out_ref.shape[1]
    rows = pl.ds(pl.multiple_of(core_ref[0] * count, count), count)
    out_ref[0] = (
        middle_ref[rows, :] + (own_ref[0, 0].astype(f32) + other_ref[0].astype(f32))
    ).astype(bf16)

    @pl.when(pl.program_id(0) == 0)
    def _():
        gain_grad_ref[...] = jnp.zeros_like(gain_grad_ref)

    gain_grad_ref[...] += jnp.sum(d_normed * scaled, axis=0, keepdims=True)
    wide = w_ref.shape[3]
    total = None
    for step in range(BLOCKS):
        start = pl.multiple_of((me_ref[0] ^ step) * wide, wide)
        piece = dot_nt(d_branch_ref[:, pl.ds(start, wide)], w_ref[step].reshape(d_att_ref.shape[1], wide))
        total = piece if total is None else total + piece
    d_att_ref[...] = total.astype(bf16)


def turn_call(me, core, middle, one, two, cot, gain, weights, own, other):
    count, width = middle.shape
    half = weights.shape[1] * 128
    places, _, half_tile, _ = own.shape
    tile = 2 * half_tile
    spec = pl.BlockSpec((tile, width), lambda i, me, core: (i, 0))
    line = pl.BlockSpec((1, width), lambda i, me, core: (0, 0))
    gain_spec = pl.BlockSpec((8, width), lambda i, me, core: (0, 0))
    plain = pl.BlockSpec((1, half_tile, width), lambda i, me, core: (i, 0, 0))
    block = weights.shape[:2] + (128,) + weights.shape[3:]
    return call(
        turn_kernel,
        (places,),
        2,
        [spec, spec, spec, spec, gain_spec]
        + [pl.BlockSpec(block, lambda i, me, core: (0, 0, 3, 0))]
        + [pl.BlockSpec((1, 1, half_tile, width), lambda i, me, core: (i, core[0], 0, 0)), plain],
        [spec, spec, pl.BlockSpec((tile, half), lambda i, me, core: (i, 0)), line, plain],
        [
            shaped(middle.shape, f32),
            shaped(middle.shape, bf16),
            shaped((count, half), bf16),
            shaped((1, width), f32),
            shaped((places, half_tile, width), bf16),
        ],
        [],
        2 * count * width * half,
        22 << 20,
        40,
    )(me, core, middle, one, two, cot, gain, weights, own, other)


def attend_back_kernel(
    flag_ref, q_ref, k_ref, v_ref, out_ref, d_out_ref, probs_ref, dq_ref, dk_ref, dv_ref, k_turned, dk_sum, dv_sum
):
    block, blocks = pl.program_id(1), pl.num_programs(1)

    @pl.when(block == 0)
    def _():
        k_turned[...] = k_ref[...].T

    queries, grads = two_heads(q_ref[...]), two_heads(d_out_ref[...])
    turned = (d_out_ref[...].astype(f32) * out_ref[...].astype(f32)).T
    delta = jnp.concatenate(
        [
            jnp.sum(turned[:HEAD], axis=0, keepdims=True),
            jnp.sum(turned[HEAD:], axis=0, keepdims=True),
        ],
        axis=1,
    )

    def back(values, keys_turned):
        probs = probs_ref[0, 0, : values.shape[0], :]
        d_probs = dot_nt(values, grads)
        d_scores = (probs.astype(f32) * (d_probs - delta)).astype(bf16)
        d_query = one_pair(dot_nn(keys_turned, d_scores)).T * (HEAD**-0.5)
        dq_ref[...] = d_query.astype(bf16)
        return dot_nn(d_scores, queries), dot_nn(probs, grads)

    @pl.when(flag_ref[0] == 1)
    def _():
        d_key, d_value = back(v_ref[...], k_turned[...])

        @pl.when(block == 0)
        def _():
            dk_sum[...] = d_key
            dv_sum[...] = d_value

        @pl.when(block > 0)
        def _():
            dk_sum[...] += d_key
            dv_sum[...] += d_value

    @pl.when(flag_ref[0] != 1)
    def _():
        rows = pl.ds(pl.multiple_of(block * SHORT, SHORT), SHORT)
        d_key, d_value = back(v_ref[rows, :], k_turned[:, rows])
        dk_sum[rows, :] = d_key
        dv_sum[rows, :] = d_value

    @pl.when(block == blocks - 1)
    def _():
        dk_ref[...] = dk_sum[...].astype(bf16)
        dv_ref[...] = dv_sum[...].astype(bf16)


def attend_back_call(flag, q, k, v, out, d_out, probs):
    count, half = q.shape
    pairs, blocks = half // 128, count // SHORT
    some = pl.BlockSpec((SHORT, 128), lambda j, i, flag: (i, j))
    every = pl.BlockSpec((count, 128), lambda j, i, flag: (0, j))
    return call(
        attend_back_kernel,
        (pairs, blocks),
        1,
        [
            some,
            every,
            every,
            some,
            some,
            pl.BlockSpec((1, 1, count, 2 * SHORT), lambda j, i, flag: (j, i, 0, 0)),
        ],
        [some, every, every],
        [shaped(q.shape, bf16)] * 3,
        [pltpu.VMEM((128, count), bf16)] + [pltpu.VMEM((count, 128), f32)] * 2,
        4 * 8 * count * count * half,
        30 << 20,
        48,
    )(flag, q, k, v, out, d_out, probs)


def square_kernel(
    me_ref, dq_ref, dk_ref, dv_ref, att_ref, hidden_ref, d_branch_ref, w_ref, x_ref, rms_ref, line_ref, d_hidden_ref, *refs
):
    grad_refs, turned = refs[:4], refs[4]
    lefts = (dq_ref, dk_ref, dv_ref, att_ref)

    @pl.when(pl.program_id(0) == 0)
    def _():
        for part, ref in enumerate(lefts):
            turned[part] = ref[...].T

    pieces, wide = w_ref.shape[1], w_ref.shape[3]

    def put(grad, first):
        for step in range(BLOCKS):

            @pl.when(pl.program_id(0) == step)
            def _():
                store_grad(grad_refs, step, grad, first)

    total = None
    for part, ref in enumerate(lefts):
        rows = slice(part * 128, (part + 1) * 128)
        right = d_branch_ref if part == 3 else hidden_ref
        grad = dot_nn(turned[part], right[...])
        put(grad.reshape(pieces, 128, wide).astype(bf16), part * 128)
        if part < 3:
            piece = dot_nn(ref[...], w_ref[0, :, rows, :].reshape(pieces * 128, wide))
            total = piece if total is None else total + piece
    d_hidden_ref[...] = total.astype(bf16)
    scaled = x_ref[...].astype(f32) * rms_ref[:, :1]
    attn = jnp.sum(total * scaled, axis=0, keepdims=True)
    lines = jnp.concatenate([attn, line_ref[...], jnp.zeros((14, wide), f32)], axis=0).astype(bf16)
    put(jnp.broadcast_to(lines[None], (pieces, 16, wide)), 4 * 128)


def square_call(me, dq, dk, dv, attended, hidden, d_branch, weights, x_rows, rms, line):
    count, half = dq.shape
    width = hidden.shape[1]
    parts, pieces, depth, wide = weights.shape
    every = pl.BlockSpec((count, half), lambda d, me: (0, 0))
    column = pl.BlockSpec((count, wide), lambda d, me: (0, me[0] ^ d))
    return call(
        square_kernel,
        (parts,),
        1,
        [every] * 4
        + [column, column, pl.BlockSpec((1, pieces, depth, wide), lambda d, me: (d, 0, 0, 0))]
        + [column, pl.BlockSpec(rms.shape, lambda d, me: (0, 0))]
        + [pl.BlockSpec((1, wide), lambda d, me: (0, me[0] ^ d))],
        [column] + [pl.BlockSpec((2, pieces // 2, depth, wide), lambda d, me: (0, 0, 0, 0))] * 4,
        [shaped(hidden.shape, bf16)] + grad_shapes(pieces, depth, wide),
        [pltpu.VMEM((4, half, count), bf16)],
        14 * count * width * half,
        24 << 20,
        40,
    )(me, dq, dk, dv, attended, hidden, d_branch, weights, x_rows, rms, line)


def input_kernel(core_ref, x_ref, d_middle_ref, own_ref, other_ref, gain_ref, out_ref):
    rows = x_ref[0, 0].astype(f32)
    rms = rms_of(rows)
    scaled = rows * rms
    d_hidden = own_ref[0, 0].astype(f32) + other_ref[0].astype(f32)
    pulled = d_hidden * gain_ref[:1, :]
    out_ref[0] = (
        d_middle_ref[0, 0]
        + rms * (pulled - scaled * jnp.mean(pulled * scaled, axis=-1, keepdims=True))
    ).astype(bf16)


def input_call(core, rows, d_middle, own, other, gains):
    slots, halves, tile, width = own.shape
    mine = pl.BlockSpec((1, 1, tile, width), lambda i, core: (i, core[0], 0, 0))
    plain = pl.BlockSpec((1, tile, width), lambda i, core: (i, 0, 0))
    return call(
        input_kernel,
        (slots,),
        1,
        [mine, mine, mine, plain, pl.BlockSpec((8, width), lambda i, core: (0, 0))],
        plain,
        shaped((slots, tile, width), bf16),
        [],
        0,
        8 << 20,
        16,
    )(core, rows.reshape(own.shape), d_middle.reshape(own.shape), own, other, gains)


def per_device(
    inputs,
    bucket,
    attn_gain,
    w_query,
    w_key,
    w_value,
    w_out,
    ffn_gain,
    w_gate,
    w_up,
    w_down,
    cotangent,
):
    dp, narrow = lax.axis_size("dp"), lax.axis_size("narrow")
    chips = dp // 2
    core, chip = lax.axis_index("dp") % 2, lax.axis_index("dp") // 2
    place = lax.axis_index("narrow")
    same_core = [[2 * m + c for m in range(chips)] for c in range(2)]
    by_core = core == 0
    bundle, row_count, width = inputs.shape
    tile = row_count // 2
    own_width = w_query.shape[0]
    wide = width // BLOCKS

    def to_core(value):
        return lax.ppermute(value, "dp", [(i, i ^ 1) for i in range(dp)])

    def to_chip(value, flip):
        return lax.ppermute(value, "dp", [(i, i ^ (2 * flip)) for i in range(dp)])

    def along(value, shift):
        return lax.ppermute(
            value, "narrow", [(i, (i + shift) % narrow) for i in range(narrow)]
        )

    def stage(values, *done):
        return lax.optimization_barrier((values, done))[0]

    def ordered(mine, theirs, axis):
        join = functools.partial(jnp.concatenate, axis=axis)
        return jnp.where(by_core, join([mine, theirs]), join([theirs, mine]))

    def pick(value, index, axis):
        return lax.dynamic_index_in_dim(value, index, axis, keepdims=False)

    def mine_of(value, axis):
        low, high = (lax.index_in_dim(value, i, axis, keepdims=False) for i in range(2))
        return jnp.where(by_core, low, high), jnp.where(by_core, high, low)

    def turn(k):
        return lax.rem(place + (k + narrow), narrow)

    def blocks_for(value):
        return [pick(value, turn(k), 0) for k in range(narrow)]

    def across(blocks, *late):
        moved = [blocks[0]]
        for k in range(1, narrow):
            block = stage(blocks[k], *late) if late and 2 * k == narrow else blocks[k]
            moved.append(along(block, k))
        return moved

    def in_order(moved):
        stacked = jnp.stack(moved)
        return jnp.stack([pick(stacked, turn(-i), 0) for i in range(narrow)])

    def group_start(value):
        keep, give = mine_of(value.reshape(bundle, 2, tile, width), 1)
        return ordered(keep, to_core(give), 0)

    def group_back(moved):
        mine, give = mine_of(in_order(moved).reshape(2, bundle, tile, width), 0)
        theirs = to_core(give)
        return ordered(mine[:, None], theirs[:, None], 1).reshape(bundle, row_count, width)

    def split_far(*parts):
        return mine_of(jnp.concatenate(parts, axis=1), 0)

    def two(part):
        return part.reshape(2, part.shape[0] // 2, own_width)

    def canonical(value):
        if chips == BLOCKS:
            return value
        parts = value.reshape((BLOCKS, chips // BLOCKS) + value.shape[1:])
        return jnp.moveaxis(parts, 1, -2).reshape((BLOCKS,) + value.shape[1:-1] + (wide,))

    def scattered(value):
        if chips == BLOCKS:
            return value
        parts = value.reshape(value.shape[:-1] + (chips // BLOCKS, width // chips))
        return jnp.moveaxis(parts, -2, 1).reshape(
            (chips,) + value.shape[1:-1] + (width // chips,)
        )

    def spread(value, *late):
        return across([value] * narrow, *late)

    near = chips == BLOCKS

    def chips_first(value):
        return (to_chip(value, 1), to_chip(value, 2)) if near else ()

    def chips_second(first, second):
        return to_chip(first[: narrow // 2], 2), to_chip(second[narrow // 2 :], 1)

    def chips_full(value, firsts, seconds):
        if near:
            return jnp.stack([value, *firsts, jnp.concatenate(seconds)])
        return canonical(lax.all_gather(value, "dp", axis_index_groups=same_core))

    def chips_pieces(value, firsts, seconds):
        if near:
            return (value, *firsts, *seconds)
        full = chips_full(value, firsts, seconds)
        return full[0], full[1], full[2], full[3, : narrow // 2], full[3, narrow // 2 :]

    def sum_first(grads):
        x_keep, x_send, y_keep, y_send = grads
        return to_chip(x_send, 1), to_chip(y_send, 2)

    def sum_ready(grads, got):
        x_keep, _, y_keep, _ = grads
        return (
            (x_keep[1].astype(f32) + got[0][1].astype(f32)).astype(bf16),
            (y_keep[1].astype(f32) + got[1][1].astype(f32)).astype(bf16),
        )

    def sum_second(ready):
        return to_chip(ready[0], 2), to_chip(ready[1], 1)

    def sum_done(grads, got, last):
        x_keep, _, y_keep, _ = grads
        x_sum = x_keep[0].astype(f32) + got[0][0].astype(f32) + last[0].astype(f32)
        y_sum = y_keep[0].astype(f32) + got[1][0].astype(f32) + last[1].astype(f32)
        sent = [x_sum[k] for k in range(1, narrow // 2)] + [y_sum[k] for k in range(narrow // 2)]
        return x_sum[0], [block.astype(bf16) for block in sent]

    def sum_far(grads):
        x_keep, x_send, y_keep, y_send = grads
        x_all = jnp.stack([x_keep, x_send], axis=1).reshape((BLOCKS,) + x_keep.shape[1:])
        y_all = jnp.concatenate([y_keep, y_send])
        value = scattered(
            jnp.concatenate([x_all, y_all], axis=1).reshape(BLOCKS, narrow, -1, wide)
        )
        got = lax.psum_scatter(
            value.reshape(-1, value.shape[-1]),
            "dp",
            scatter_dimension=0,
            tiled=True,
            axis_index_groups=same_core,
        ).reshape(value.shape[1:])
        return got[0].astype(f32), [got[k] for k in range(1, narrow)]

    def sum_places(sent, *late):
        got = []
        for k, block in enumerate(sent, 1):
            got.append(along(stage(block, *late) if late and 2 * k == narrow else block, -k))
        return got

    def swap_ready(own, got):
        total = own
        for piece in got:
            total = total + piece.astype(f32)
        low, high = total[:, :own_width], total[:, own_width:]
        return jnp.where(by_core, low, high), jnp.where(by_core, high, low).astype(bf16)

    def finish(keep, theirs, parts, size):
        theirs = theirs.astype(f32)
        both = jnp.where(by_core, jnp.stack([keep, theirs]), jnp.stack([theirs, keep]))
        return [both[:, i * size : (i + 1) * size] for i in range(parts)]

    me = (chip if near else 0 * chip).astype(jnp.int32)[None]
    core_index, place_index = core.astype(jnp.int32)[None], place.astype(jnp.int32)[None]
    kinds = [w_gate.T, w_up.T, w_down]
    depth = w_down.shape[0] // 2
    cut = -(-depth // 32 // 2) * 32
    if near:
        keep, give = square_split_call(
            core_index, bucket, w_query, w_key, w_value, w_out, attn_gain, ffn_gain
        )
    else:
        extra = jnp.concatenate(
            [
                attn_gain[None],
                ffn_gain[None],
                jnp.pad(bucket.astype(bf16), (0, own_width - bundle))[None],
                jnp.zeros((13, own_width), bf16),
            ]
        )
        keep, give = split_far(
            two(w_query.T), two(w_key.T), two(w_value.T), two(w_out), jnp.stack([extra, extra])
        )
        halves = [two(kind) for kind in kinds]
        ffn_keep, ffn_give = split_far(
            *[half[:, :cut] for half in halves], *[half[:, cut:] for half in halves]
        )
    square = ordered(keep, to_core(give), 1)

    square_z = spread(square)
    own_inputs, own_cotangent, kinds, square = stage((inputs, cotangent, kinds, square))
    if near:
        ffn_keep, ffn_give = ffn_split_call(core_index, cut, *kinds)
    x_blocks = blocks_for(group_start(own_inputs))
    cot_blocks = blocks_for(group_start(own_cotangent))
    ffn_theirs = to_core(ffn_give)
    ffn_one = ordered(ffn_keep[: 3 * cut], ffn_theirs[: 3 * cut], 1)
    ffn_two = ordered(ffn_keep[3 * cut :], ffn_theirs[3 * cut :], 1)
    flags = square[4 * 128 + 2].reshape(2, own_width)[:, :bundle].reshape(-1)
    flag = pick(flags.astype(jnp.int32), place, 0)[None]

    square_z, x_blocks, cot_blocks, ffn_one, ffn_two, flag = stage(
        (square_z, x_blocks, cot_blocks, ffn_one, ffn_two, flag)
    )
    square_z = jnp.stack(square_z)
    square_first = chips_first(square_z)
    x_moved = across(x_blocks)

    square_first, x_moved, ffn_one = stage((square_first, x_moved, ffn_one))
    x_own = jnp.stack(x_moved)
    x_other = to_core(x_own)
    square_second = chips_second(*square_first) if near else ()
    one_z = spread(ffn_one, x_other)
    square_full = chips_full(square_z, square_first, square_second)
    x_rows, hidden, rms, gains, q, k, v = qkv_call(
        me, core_index, place_index, x_own, x_other, square_full
    )

    q, one_z, cot_blocks = stage((q, one_z, cot_blocks))
    one_z = jnp.stack(one_z)
    one_first = chips_first(one_z)
    cot_moved = across(cot_blocks)
    attended, probs = attend_call(flag, q, k, v)

    attended, one_first, cot_moved, ffn_two = stage((attended, one_first, cot_moved, ffn_two))
    one_second = chips_second(*one_first) if near else ()
    branch = branch_call(me, attended, square_full)
    cot_own = jnp.stack(cot_moved)
    two_z = spread(ffn_two, branch)
    middle_place = narrow // 2
    branch, cot_own, one_second, two_near = stage(
        (branch, cot_own, one_second, two_z[:middle_place] + two_z[middle_place + 1 :])
    )
    two_z = two_near[:middle_place] + [two_z[middle_place]] + two_near[middle_place:]
    branch_other, cot_other = to_core(branch), to_core(cot_own)
    middle, normed, cot_rows = middle_call(
        core_index, place_index, x_rows, branch, branch_other, gains, cot_own, cot_other
    )

    normed, two_z = stage((normed, two_z))
    two_z = jnp.stack(two_z)
    two_first = chips_first(two_z)
    part_result, part_d_normed, *one_grads = ffn_call(
        me, normed, cot_rows, chips_pieces(one_z, one_first, one_second)
    )

    part_result, part_d_normed, one_grads, two_first = stage(
        (part_result, part_d_normed, one_grads, two_first)
    )
    two_second = chips_second(*two_first) if near else ()

    part_result, part_d_normed, one_grads, two_second = stage(
        (part_result, part_d_normed, one_grads, two_second)
    )
    one_got = sum_first(one_grads) if near else ()
    result, d_normed, *two_grads = ffn_call(
        me,
        normed,
        cot_rows,
        chips_pieces(two_z, two_first, two_second),
        part_result,
        part_d_normed,
    )

    result, d_normed, two_grads, one_got = stage((result, d_normed, two_grads, one_got))
    by_rows = (narrow, 2, tile, width)
    d_normed_other = to_core(d_normed)
    one_last = sum_second(sum_ready(one_grads, one_got)) if near else ()
    result = result.reshape(by_rows)
    result_other = to_core(mine_of(result, 1)[1])
    d_middle, d_branch, d_att, ffn_gain_grad, out_rows = turn_call(
        me,
        core_index,
        middle,
        d_normed,
        d_normed_other,
        cot_rows,
        gains,
        square_full,
        result,
        result_other,
    )
    out_blocks = blocks_for(out_rows)

    d_att, out_blocks, one_last, two_grads = stage((d_att, out_blocks, one_last, two_grads))
    two_got = sum_first(two_grads) if near else ()
    out_moved = across(out_blocks)
    dq, dk, dv = attend_back_call(flag, q, k, v, attended, d_att, probs)
    one_own, one_sent = sum_done(one_grads, one_got, one_last) if near else sum_far(one_grads)

    dq, one_sent, two_got, out_moved = stage((dq, one_sent, two_got, out_moved))
    two_last = sum_second(sum_ready(two_grads, two_got)) if near else ()
    one_places = sum_places(one_sent)
    d_hidden, *square_grads = square_call(
        me, dq, dk, dv, attended, hidden, d_branch, square_full, x_rows, rms, 0.5 * ffn_gain_grad
    )
    outputs = group_back(out_moved)

    d_hidden, square_grads, two_last, one_places = stage(
        (d_hidden, square_grads, two_last, one_places)
    )
    square_got = sum_first(square_grads) if near else ()
    d_hidden = d_hidden.reshape(by_rows)
    d_hidden_other = to_core(mine_of(d_hidden, 1)[1])
    two_own, two_sent = sum_done(two_grads, two_got, two_last) if near else sum_far(two_grads)
    two_places = sum_places(two_sent, d_hidden_other)
    input_blocks = blocks_for(
        input_call(core_index, x_rows, d_middle, d_hidden, d_hidden_other, gains)
    )
    one_keep, one_swap = swap_ready(one_own, one_places)

    input_blocks, square_got, two_places, one_swap = stage(
        (input_blocks, square_got, two_places, one_swap)
    )
    square_last = sum_second(sum_ready(square_grads, square_got)) if near else ()
    input_moved = across(input_blocks)
    one_theirs = to_core(one_swap)
    two_keep, two_swap = swap_ready(two_own, two_places)
    two_theirs = to_core(two_swap)

    square_last, input_moved, one_theirs, two_theirs = stage(
        (square_last, input_moved, one_theirs, two_theirs)
    )
    square_own, square_sent = (
        sum_done(square_grads, square_got, square_last) if near else sum_far(square_grads)
    )
    square_places = sum_places(square_sent)
    input_grad = group_back(input_moved).astype(f32)
    one_parts = finish(one_keep, one_theirs, 3, cut)
    two_parts = finish(two_keep, two_theirs, 3, depth - cut)
    g_gate, g_up, g_down = [
        jnp.concatenate(parts, axis=1).reshape(2 * depth, own_width)
        for parts in zip(one_parts, two_parts)
    ]
    g_gate, g_up = g_gate.T, g_up.T
    square_places, outputs, input_grad, g_gate, g_up, g_down = stage(
        (square_places, outputs, input_grad, g_gate, g_up, g_down)
    )
    square_keep, square_swap = swap_ready(square_own, square_places)
    square_theirs = to_core(square_swap)
    g_query, g_key, g_value, g_out = [
        part.reshape(-1, own_width) for part in finish(square_keep, square_theirs, 4, 128)
    ]
    gain_own = square_keep[4 * 128 :] + square_theirs[4 * 128 :].astype(f32)
    return (
        outputs,
        input_grad,
        gain_own[0],
        g_query.T,
        g_key.T,
        g_value.T,
        g_out,
        gain_own[1],
        g_gate,
        g_up,
        g_down,
    )


def solution(mesh):
    rows = P("dp", "narrow", None)
    tall, flat = P("dp", "narrow"), P("narrow", "dp")
    return jax.shard_map(
        per_device,
        mesh=mesh,
        in_specs=(rows, P("dp"), P("dp"), tall, tall, tall, flat, P("dp"), tall, tall, flat, rows),
        out_specs=(rows, rows, P("dp"), tall, tall, tall, flat, P("dp"), tall, tall, flat),
        check_vma=False,
    )
```

```python
import functools

import jax
import jax.numpy as jnp
from jax import lax
from jax.experimental import pallas as pl
from jax.experimental.pallas import tpu as pltpu
from jax.sharding import PartitionSpec as P

HEAD = 64
SHORT = 384
EPS = 1e-06
BLOCKS = 4
f32 = jnp.float32
bf16 = jnp.bfloat16


def dot_nn(left, right):
    return jnp.dot(left, right, preferred_element_type=f32)


def dot_nt(left, right):
    return lax.dot_general(left, right, (((1,), (1,)), ((), ())), preferred_element_type=f32)


def call(kernel, grid, prefetch, in_specs, out_specs, out_shape, scratch, flops, moved, vmem):
    return pl.pallas_call(
        kernel,
        grid_spec=pltpu.PrefetchScalarGridSpec(
            num_scalar_prefetch=prefetch,
            grid=grid,
            in_specs=in_specs,
            out_specs=out_specs,
            scratch_shapes=scratch,
        ),
        out_shape=out_shape,
        compiler_params=pltpu.CompilerParams(vmem_limit_bytes=vmem << 20),
        cost_estimate=pl.CostEstimate(flops=flops, bytes_accessed=moved, transcendentals=0),
    )


def shaped(shape, dtype):
    return jax.ShapeDtypeStruct(shape, dtype)


def rms_of(rows):
    return lax.rsqrt(jnp.mean(rows * rows, axis=-1, keepdims=True) + EPS)


def store_grad(refs, step, grad, first):
    x_keep, x_send, y_keep, y_send = refs
    half, rows = grad.shape[0] // 2, slice(first, first + grad.shape[1])
    (x_send if step % 2 else x_keep)[step // 2, :, rows] = grad[:half]
    (y_send if step // 2 else y_keep)[step % 2, :, rows] = grad[half:]


def grad_shapes(pieces, rows, wide):
    return [shaped((2, pieces // 2, rows, wide), bf16)] * 4


def square_split_kernel(
    core_ref, bucket_ref, q_ref, k_ref, v_ref, o_ref, attn_ref, ffn_ref, keep_ref, give_ref
):
    halves = [ref[...].T for ref in (q_ref, k_ref, v_ref)] + [o_ref[...]]
    shape = (16, keep_ref.shape[1])
    row, lane = (lax.broadcasted_iota(jnp.int32, shape, axis) for axis in range(2))
    flags = jnp.zeros(shape, f32)
    for i in range(bucket_ref.shape[0]):
        flags = jnp.where(lane == i, bucket_ref[i].astype(f32), flags)
    flags = jnp.where(row == 2, flags, 0.0)
    flags = jnp.where(row == 1, ffn_ref[...].astype(f32), flags)
    extra = jnp.where(row == 0, attn_ref[...].astype(f32), flags).astype(bf16)

    def store(low_ref, high_ref):
        start = 0
        for half in halves:
            count = half.shape[0] // 2
            low_ref[start : start + count] = half[:count]
            high_ref[start : start + count] = half[count:]
            start += count
        low_ref[start:] = extra
        high_ref[start:] = extra

    @pl.when(core_ref[0] == 0)
    def _():
        store(keep_ref, give_ref)

    @pl.when(core_ref[0] != 0)
    def _():
        store(give_ref, keep_ref)


def square_split_call(core, bucket, q, k, v, o, attn, ffn):
    rows, cols = q.shape[1] // 2 * 4 + 16, o.shape[1]
    whole = pl.BlockSpec(memory_space=pltpu.VMEM)
    return call(
        square_split_kernel,
        (),
        2,
        [whole] * 6,
        [whole] * 2,
        [shaped((rows, cols), bf16)] * 2,
        [],
        0,
        1 << 20,
        16,
    )(core, bucket, q, k, v, o, attn[None], ffn[None])


def ffn_split_kernel(cut, core_ref, *refs):
    parts, (keep_ref, give_ref) = refs[:3], refs[3:]

    def store(low_ref, high_ref):
        start = 0
        half = parts[0].shape[0] // 2
        for first, last in ((0, cut), (cut, half)):
            for part in parts:
                count = last - first
                low_ref[start : start + count] = part[first:last]
                high_ref[start : start + count] = part[half + first : half + last]
                start += count

    @pl.when(core_ref[0] == 0)
    def _():
        store(keep_ref, give_ref)

    @pl.when(core_ref[0] != 0)
    def _():
        store(give_ref, keep_ref)


def ffn_split_call(core, cut, gate, up, down):
    rows, cols = gate.shape[0] // 2 * 3, gate.shape[1]
    whole = pl.BlockSpec(memory_space=pltpu.VMEM)
    return call(
        functools.partial(ffn_split_kernel, cut),
        (),
        1,
        [whole] * 3,
        [whole] * 2,
        [shaped((rows, cols), bf16)] * 2,
        [],
        0,
        1 << 20,
        16,
    )(core, gate, up, down)


def join_rows(core_ref, own_ref, other_ref, out_ref):
    count = own_ref.shape[1]

    @pl.when(core_ref[0] == 0)
    def _():
        out_ref[:count] = own_ref[0]
        out_ref[count:] = other_ref[0]

    @pl.when(core_ref[0] != 0)
    def _():
        out_ref[:count] = other_ref[0]
        out_ref[count:] = own_ref[0]


def qkv_kernel(
    me_ref, core_ref, place_ref, own_ref, other_ref, w0, w1, w2, w3, w4, x_ref, hidden_ref, rms_ref, gains_ref, w_ref, q_ref, k_ref, v_ref
):
    @pl.when(pl.program_id(0) == 0)
    def _():
        for step, piece in enumerate((w0, w1, w2)):
            w_ref[step] = piece[...]
        w_ref[3, : w3.shape[0]] = w3[...]
        w_ref[3, w3.shape[0] :] = w4[...]

    join_rows(core_ref, own_ref, other_ref, x_ref)
    rows = x_ref[...].astype(f32)
    rms = rms_of(rows)
    rms_ref[...] = jnp.broadcast_to(rms, rms_ref.shape)
    wide = w_ref.shape[3]
    half = w_ref.shape[1] * 128
    for step in range(BLOCKS):
        columns = pl.ds(pl.multiple_of((me_ref[0] ^ step) * wide, wide), wide)
        gains = w_ref[step, 0, 4 * 128 :, :].astype(f32)
        gains_ref[:, columns] = gains[:8]
        hidden_ref[:, columns] = (x_ref[:, columns].astype(f32) * rms * gains[:1]).astype(bf16)
    for part, ref in enumerate((q_ref, k_ref, v_ref)):
        total = None
        for step in range(BLOCKS):
            start = pl.multiple_of((me_ref[0] ^ step) * wide, wide)
            weight = w_ref[step, :, part * 128 : (part + 1) * 128, :].reshape(half, wide)
            piece = dot_nt(hidden_ref[:, pl.ds(start, wide)], weight)
            total = piece if total is None else total + piece
        if part == 0:
            total = total * (HEAD**-0.5)
        ref[...] = total.astype(bf16)


def qkv_call(me, core, place, own, other, weights):
    places, half_tile, width = own.shape
    half = weights[0].shape[0] * 128
    tile, count = 2 * half_tile, 2 * half_tile * places
    all_shape = (BLOCKS,) + weights[0].shape
    row_spec = pl.BlockSpec((tile, width), lambda i, me, core, place: (i, 0))
    half_spec = pl.BlockSpec((tile, half), lambda i, me, core, place: (i, 0))
    part_spec = pl.BlockSpec(
        (1, half_tile, width), lambda i, me, core, place: ((place[0] + places - i) % places, 0, 0)
    )
    return call(
        qkv_kernel,
        (places,),
        3,
        [
            part_spec,
            part_spec,
        ]
        + [pl.BlockSpec(w.shape, lambda i, me, core, place: (0, 0, 0)) for w in weights],
        [
            row_spec,
            row_spec,
            pl.BlockSpec((tile, 128), lambda i, me, core, place: (i, 0)),
            pl.BlockSpec((8, width), lambda i, me, core, place: (0, 0)),
            pl.BlockSpec(all_shape, lambda i, me, core, place: (0, 0, 0, 0)),
            half_spec,
            half_spec,
            half_spec,
        ],
        [shaped((count, width), bf16)] * 2
        + [shaped((count, 128), f32), shaped((8, width), f32), shaped(all_shape, bf16)]
        + [shaped((count, half), bf16)] * 3,
        [],
        2 * count * width * half * 3,
        12 << 20,
        40,
    )(me, core, place, own, other, *weights)


def two_heads(rows):
    low = lax.broadcasted_iota(jnp.int32, rows.shape, 1) < HEAD
    zero = jnp.zeros_like(rows)
    return jnp.concatenate([jnp.where(low, rows, zero), jnp.where(low, zero, rows)], axis=0)


def one_pair(both):
    half = both.shape[1] // 2
    return jnp.concatenate([both[:HEAD, :half], both[HEAD:, half:]], axis=0)


def attend_kernel(flag_ref, q_ref, k_ref, v_ref, out_ref, probs_ref, v_turned):
    block = pl.program_id(1)

    @pl.when(block == 0)
    def _():
        v_turned[...] = v_ref[...].T

    queries = two_heads(q_ref[...])

    def attend(keys, values):
        scores = dot_nt(keys, queries)
        expo = jnp.exp(scores - jnp.max(scores, axis=0, keepdims=True))
        probs = (expo * (1.0 / jnp.sum(expo, axis=0, keepdims=True))).astype(bf16)
        probs_ref[0, 0, : keys.shape[0], :] = probs
        out_ref[...] = one_pair(dot_nn(values, probs)).T.astype(bf16)

    @pl.when(flag_ref[0] == 1)
    def _():
        attend(k_ref[...], v_turned[...])

    @pl.when(flag_ref[0] != 1)
    def _():
        start = pl.multiple_of(block * SHORT, SHORT)
        attend(k_ref[pl.ds(start, SHORT), :], v_turned[:, pl.ds(start, SHORT)])


def attend_call(flag, q, k, v):
    count, half = q.shape
    pairs, blocks = half // 128, count // SHORT
    some = pl.BlockSpec((SHORT, 128), lambda j, i, flag: (i, j))
    every = pl.BlockSpec((count, 128), lambda j, i, flag: (0, j))
    return call(
        attend_kernel,
        (pairs, blocks),
        1,
        [some, every, every],
        [some, pl.BlockSpec((1, 1, count, 2 * SHORT), lambda j, i, flag: (j, i, 0, 0))],
        [shaped(q.shape, bf16), shaped((pairs, blocks, count, 2 * SHORT), bf16)],
        [pltpu.VMEM((128, count), bf16)],
        4 * 4 * count * count * half,
        28 << 20,
        48,
    )(flag, q, k, v)


def branch_kernel(me_ref, att_ref, w_ref, out_ref):
    wide = w_ref.shape[3]
    for step in range(BLOCKS):
        start = pl.multiple_of((me_ref[0] ^ step) * wide, wide)
        weight = w_ref[step].reshape(att_ref.shape[1], wide)
        out_ref[:, pl.ds(start, wide)] = dot_nn(att_ref[...], weight).astype(bf16)


def branch_call(me, attended, weights):
    count, half = attended.shape
    width = weights.shape[0] * weights.shape[3]
    tile = count // 4
    block = weights.shape[:2] + (128,) + weights.shape[3:]
    return call(
        branch_kernel,
        (count // tile,),
        1,
        [
            pl.BlockSpec((tile, half), lambda i, me: (i, 0)),
            pl.BlockSpec(block, lambda i, me: (0, 0, 3, 0)),
        ],
        pl.BlockSpec((tile, width), lambda i, me: (i, 0)),
        shaped((count, width), bf16),
        [],
        2 * count * width * half,
        5 << 20,
        24,
    )(me, attended, weights)


def middle_kernel(
    core_ref, place_ref, x_ref, one_ref, two_ref, gain_ref, own_ref, other_ref, middle_ref, normed_ref, cot_ref
):
    middle = x_ref[...].astype(f32) + (one_ref[...].astype(f32) + two_ref[...].astype(f32))
    middle_ref[...] = middle
    normed_ref[...] = (middle * rms_of(middle) * gain_ref[1:2, :]).astype(bf16)
    join_rows(core_ref, own_ref, other_ref, cot_ref)


def middle_call(core, place, rows, one, two, gain, own, other):
    count, width = rows.shape
    places, half_tile = own.shape[:2]
    spec = pl.BlockSpec((2 * half_tile, width), lambda i, core, place: (i, 0))
    part_spec = pl.BlockSpec(
        (1, half_tile, width), lambda i, core, place: ((place[0] + places - i) % places, 0, 0)
    )
    return call(
        middle_kernel,
        (places,),
        2,
        [spec] * 3
        + [pl.BlockSpec((8, width), lambda i, core, place: (0, 0)), part_spec, part_spec],
        [spec] * 3,
        [shaped(rows.shape, f32), shaped(rows.shape, bf16), shaped(rows.shape, bf16)],
        [],
        0,
        14 << 20,
        32,
    )(core, place, rows, one, two, gain, own, other)


def ffn_kernel(given, prior, me_ref, core_ref, normed_ref, d_out_ref, *refs):
    pieces_of, refs = refs[:given], refs[given:]
    before = refs[:2] if prior else None
    refs = refs[2 if prior else 0 :]
    result_ref, d_normed_ref = refs[:2]
    grad_refs, refs = refs[2:6], refs[6:]
    give_ref = refs[0] if prior else None
    weights, inner_t, gate_t, up_t = refs[1 if prior else 0 :]
    pieces, rows_all, wide = pieces_of[0].shape
    parts, kinds, depth = BLOCKS, 3, rows_all // 3
    units = pieces * depth
    tile = SHORT

    def columns(step):
        return pl.ds(pl.multiple_of((me_ref[0] ^ step) * wide, wide), wide)

    for kind in range(kinds):
        rows = slice(kind * depth, (kind + 1) * depth)
        for step in range(parts):
            start = 0
            for piece in pieces_of[step:] if step == parts - 1 else pieces_of[step : step + 1]:
                count = piece.shape[0] * depth
                value = piece[:, rows, :].reshape(count, wide)
                weights[kind, start : start + count, columns(step)] = value
                start += count

    def rows_step(index, carry):
        rows = pl.ds(pl.multiple_of(index * tile, tile), tile)
        normed = normed_ref[rows, :]
        gate, up = dot_nt(normed, weights[0]), dot_nt(normed, weights[1])
        d_inner = dot_nt(d_out_ref[rows, :], weights[2])
        square = gate * gate
        bent = jnp.tanh(gate * (0.7978845608 + 0.7978845608 * 0.044715 * square))
        half = 0.5 + 0.5 * bent
        gelu = gate * half
        slope = half + gate * (0.5 - 0.5 * bent * bent) * (
            0.7978845608 + 0.7978845608 * 3 * 0.044715 * square
        )
        inner = (gelu * up).astype(bf16)
        d_gate = (d_inner * up * slope).astype(bf16)
        d_up = (d_inner * gelu).astype(bf16)
        inner_t[:, rows] = inner.T
        gate_t[:, rows] = d_gate.T
        up_t[:, rows] = d_up.T
        forward = dot_nn(inner, weights[2])
        backward = dot_nn(d_gate, weights[0]) + dot_nn(d_up, weights[1])
        if prior:
            forward += before[0][rows, :].astype(f32)
            backward += before[1][rows, :].astype(f32)
        result_ref[rows, :] = forward.astype(bf16)
        d_normed_ref[rows, :] = backward.astype(bf16)
        return carry

    lax.fori_loop(0, normed_ref.shape[0] // tile, rows_step, 0)
    for step in range(parts):
        here, there = normed_ref[:, columns(step)], d_out_ref[:, columns(step)]
        for kind, (left, right) in enumerate(((gate_t, here), (up_t, here), (inner_t, there))):
            grad = dot_nn(left[...], right).astype(bf16)
            store_grad(grad_refs, step, grad.reshape(pieces, depth, wide), kind * depth)
    if prior:
        give_rows(core_ref, result_ref, give_ref)


def give_rows(core_ref, all_ref, give_ref):
    places, count = give_ref.shape[:2]
    for place in range(places):
        start = (2 * place + 1 - core_ref[0]) * count
        give_ref[place] = all_ref[pl.ds(pl.multiple_of(start, count), count), :]


def ffn_call(me, core, places, normed, d_out, weights, *before):
    count, width = normed.shape
    pieces, rows_all, wide = weights[0].shape
    units = pieces * rows_all // 3
    whole = pl.BlockSpec(memory_space=pltpu.VMEM)
    return call(
        functools.partial(ffn_kernel, len(weights), bool(before)),
        (),
        2,
        [whole] * (2 + len(weights) + len(before)),
        [whole] * (7 if before else 6),
        [shaped(normed.shape, bf16)] * 2
        + grad_shapes(pieces, rows_all, wide)
        + ([shaped((places, count // places // 2, width), bf16)] if before else []),
        [pltpu.VMEM((3, units, width), bf16)] + [pltpu.VMEM((units, count), bf16)] * 3,
        18 * count * width * units,
        20 << 20,
        56,
    )(me, core, normed, d_out, *weights, *before)


def turn_kernel(
    me_ref,
    core_ref,
    middle_ref,
    one_ref,
    two_ref,
    cot_ref,
    gain_ref,
    w_ref,
    own_ref,
    other_ref,
    d_middle_ref,
    d_branch_ref,
    d_att_ref,
    gain_grad_ref,
    out_ref,
):
    middle = middle_ref[...]
    rms = rms_of(middle)
    scaled = middle * rms
    d_normed = one_ref[...].astype(f32) + two_ref[...].astype(f32)
    pulled = d_normed * gain_ref[1:2, :]
    d_middle = cot_ref[...].astype(f32) + rms * (
        pulled - scaled * jnp.mean(pulled * scaled, axis=-1, keepdims=True)
    )
    d_middle_ref[...] = d_middle
    d_branch_ref[...] = d_middle.astype(bf16)
    count = out_ref.shape[1]
    rows = pl.ds(pl.multiple_of(core_ref[0] * count, count), count)
    out_ref[0] = (
        middle_ref[rows, :] + (own_ref[0, 0].astype(f32) + other_ref[0].astype(f32))
    ).astype(bf16)

    @pl.when(pl.program_id(0) == 0)
    def _():
        gain_grad_ref[...] = jnp.zeros_like(gain_grad_ref)

    gain_grad_ref[...] += jnp.sum(d_normed * scaled, axis=0, keepdims=True)
    wide = w_ref.shape[3]
    total = None
    for step in range(BLOCKS):
        start = pl.multiple_of((me_ref[0] ^ step) * wide, wide)
        piece = dot_nt(d_branch_ref[:, pl.ds(start, wide)], w_ref[step].reshape(d_att_ref.shape[1], wide))
        total = piece if total is None else total + piece
    d_att_ref[...] = total.astype(bf16)


def turn_call(me, core, middle, one, two, cot, gain, weights, own, other):
    count, width = middle.shape
    half = weights.shape[1] * 128
    places, _, half_tile, _ = own.shape
    tile = 2 * half_tile
    spec = pl.BlockSpec((tile, width), lambda i, me, core: (i, 0))
    line = pl.BlockSpec((1, width), lambda i, me, core: (0, 0))
    gain_spec = pl.BlockSpec((8, width), lambda i, me, core: (0, 0))
    plain = pl.BlockSpec((1, half_tile, width), lambda i, me, core: (i, 0, 0))
    block = weights.shape[:2] + (128,) + weights.shape[3:]
    return call(
        turn_kernel,
        (places,),
        2,
        [spec, spec, spec, spec, gain_spec]
        + [pl.BlockSpec(block, lambda i, me, core: (0, 0, 3, 0))]
        + [pl.BlockSpec((1, 1, half_tile, width), lambda i, me, core: (i, core[0], 0, 0)), plain],
        [spec, spec, pl.BlockSpec((tile, half), lambda i, me, core: (i, 0)), line, plain],
        [
            shaped(middle.shape, f32),
            shaped(middle.shape, bf16),
            shaped((count, half), bf16),
            shaped((1, width), f32),
            shaped((places, half_tile, width), bf16),
        ],
        [],
        2 * count * width * half,
        22 << 20,
        40,
    )(me, core, middle, one, two, cot, gain, weights, own, other)


def attend_back_kernel(
    flag_ref, q_ref, k_ref, v_ref, out_ref, d_out_ref, probs_ref, dq_ref, dk_ref, dv_ref, k_turned, dk_sum, dv_sum
):
    block, blocks = pl.program_id(1), pl.num_programs(1)

    @pl.when(block == 0)
    def _():
        k_turned[...] = k_ref[...].T

    queries, grads = two_heads(q_ref[...]), two_heads(d_out_ref[...])
    turned = (d_out_ref[...].astype(f32) * out_ref[...].astype(f32)).T
    delta = jnp.concatenate(
        [
            jnp.sum(turned[:HEAD], axis=0, keepdims=True),
            jnp.sum(turned[HEAD:], axis=0, keepdims=True),
        ],
        axis=1,
    )

    def back(values, keys_turned):
        probs = probs_ref[0, 0, : values.shape[0], :]
        d_probs = dot_nt(values, grads)
        d_scores = (probs.astype(f32) * (d_probs - delta)).astype(bf16)
        d_query = one_pair(dot_nn(keys_turned, d_scores)).T * (HEAD**-0.5)
        dq_ref[...] = d_query.astype(bf16)
        return dot_nn(d_scores, queries), dot_nn(probs, grads)

    @pl.when(flag_ref[0] == 1)
    def _():
        d_key, d_value = back(v_ref[...], k_turned[...])

        @pl.when(block == 0)
        def _():
            dk_sum[...] = d_key
            dv_sum[...] = d_value

        @pl.when(block > 0)
        def _():
            dk_sum[...] += d_key
            dv_sum[...] += d_value

    @pl.when(flag_ref[0] != 1)
    def _():
        rows = pl.ds(pl.multiple_of(block * SHORT, SHORT), SHORT)
        d_key, d_value = back(v_ref[rows, :], k_turned[:, rows])
        dk_sum[rows, :] = d_key
        dv_sum[rows, :] = d_value

    @pl.when(block == blocks - 1)
    def _():
        dk_ref[...] = dk_sum[...].astype(bf16)
        dv_ref[...] = dv_sum[...].astype(bf16)


def attend_back_call(first, pairs, flag, q, k, v, out, d_out, probs):
    count, half = q.shape
    blocks = count // SHORT
    some = pl.BlockSpec((SHORT, 128), lambda j, i, flag: (i, j + first))
    every = pl.BlockSpec((count, 128), lambda j, i, flag: (0, j + first))
    some_out = pl.BlockSpec((SHORT, 128), lambda j, i, flag: (i, j))
    every_out = pl.BlockSpec((count, 128), lambda j, i, flag: (0, j))
    return call(
        attend_back_kernel,
        (pairs, blocks),
        1,
        [
            some,
            every,
            every,
            some,
            some,
            pl.BlockSpec((1, 1, count, 2 * SHORT), lambda j, i, flag: (j + first, i, 0, 0)),
        ],
        [some_out, every_out, every_out],
        [shaped((count, pairs * 128), bf16)] * 3,
        [pltpu.VMEM((128, count), bf16)] + [pltpu.VMEM((count, 128), f32)] * 2,
        4 * 8 * count * count * pairs * 128,
        16 << 20,
        48,
    )(flag, q, k, v, out, d_out, probs)


def square_kernel(
    me_ref,
    core_ref,
    dq_one,
    dq_two,
    dk_one,
    dk_two,
    dv_one,
    dv_two,
    att_ref,
    hidden_ref,
    d_branch_ref,
    w_ref,
    x_ref,
    rms_ref,
    line_ref,
    d_hidden_ref,
    give_ref,
    *refs,
):
    grad_refs, turned = refs[:4], refs[4]
    pieces, wide = w_ref.shape[1], w_ref.shape[3]
    lefts = (dq_one, dq_two, dk_one, dk_two, dv_one, dv_two)
    start = 0
    for ref in (*lefts, att_ref):
        stop = start + ref.shape[1]
        turned[start:stop, :] = ref[...].T
        start = stop
    half = att_ref.shape[1]
    for step in range(BLOCKS):
        columns = pl.ds(pl.multiple_of((me_ref[0] ^ step) * wide, wide), wide)
        for part in range(4):
            right = d_branch_ref if part == 3 else hidden_ref
            grad = dot_nn(turned[part * half : (part + 1) * half, :], right[:, columns])
            grad = grad.astype(bf16).reshape(pieces, 128, wide)
            store_grad(grad_refs, step, grad, part * 128)
        total = None
        for index, ref in enumerate(lefts):
            part, side = index // 2, index % 2 * pieces // 2
            rows = slice(part * 128, (part + 1) * 128)
            weight = w_ref[step, side : side + pieces // 2, rows, :].reshape(half // 2, wide)
            piece = dot_nn(ref[...], weight)
            total = piece if total is None else total + piece
        d_hidden_ref[:, columns] = total.astype(bf16)
        scaled = x_ref[:, columns].astype(f32) * rms_ref[:, :1]
        attn = jnp.sum(total * scaled, axis=0, keepdims=True)
        lines = jnp.concatenate(
            [attn, line_ref[:, columns], jnp.zeros((14, wide), f32)], axis=0
        ).astype(bf16)
        store_grad(grad_refs, step, jnp.broadcast_to(lines[None], (pieces, 16, wide)), 4 * 128)
    give_rows(core_ref, d_hidden_ref, give_ref)


def square_call(me, core, lefts, attended, hidden, d_branch, weights, x_rows, rms, line):
    count, half = attended.shape
    width = hidden.shape[1]
    pieces, depth, wide = weights.shape[1:]
    whole = pl.BlockSpec(memory_space=pltpu.VMEM)
    return call(
        square_kernel,
        (),
        2,
        [whole] * (len(lefts) + 7),
        [whole] * 6,
        [shaped(hidden.shape, bf16), shaped((pieces, count // pieces // 2, width), bf16)]
        + grad_shapes(pieces, depth, wide),
        [pltpu.VMEM((4 * half, count), bf16)],
        14 * count * width * half,
        24 << 20,
        52,
    )(me, core, *lefts, attended, hidden, d_branch, weights, x_rows, rms, line)


def input_kernel(core_ref, x_ref, d_middle_ref, own_ref, other_ref, gain_ref, out_ref):
    rows = x_ref[0, 0].astype(f32)
    rms = rms_of(rows)
    scaled = rows * rms
    d_hidden = own_ref[0, 0].astype(f32) + other_ref[0].astype(f32)
    pulled = d_hidden * gain_ref[:1, :]
    out_ref[0] = (
        d_middle_ref[0, 0]
        + rms * (pulled - scaled * jnp.mean(pulled * scaled, axis=-1, keepdims=True))
    ).astype(bf16)


def input_call(core, rows, d_middle, own, other, gains):
    slots, halves, tile, width = own.shape
    mine = pl.BlockSpec((1, 1, tile, width), lambda i, core: (i, core[0], 0, 0))
    plain = pl.BlockSpec((1, tile, width), lambda i, core: (i, 0, 0))
    return call(
        input_kernel,
        (slots,),
        1,
        [mine, mine, mine, plain, pl.BlockSpec((8, width), lambda i, core: (0, 0))],
        plain,
        shaped((slots, tile, width), bf16),
        [],
        0,
        8 << 20,
        16,
    )(core, rows.reshape(own.shape), d_middle.reshape(own.shape), own, other, gains)


def per_device(
    inputs,
    bucket,
    attn_gain,
    w_query,
    w_key,
    w_value,
    w_out,
    ffn_gain,
    w_gate,
    w_up,
    w_down,
    cotangent,
):
    dp, narrow = lax.axis_size("dp"), lax.axis_size("narrow")
    chips = dp // 2
    core, chip = lax.axis_index("dp") % 2, lax.axis_index("dp") // 2
    place = lax.axis_index("narrow")
    same_core = [[2 * m + c for m in range(chips)] for c in range(2)]
    by_core = core == 0
    bundle, row_count, width = inputs.shape
    tile = row_count // 2
    own_width = w_query.shape[0]
    wide = width // BLOCKS

    def to_core(value):
        return lax.ppermute(value, "dp", [(i, i ^ 1) for i in range(dp)])

    def to_chip(value, flip):
        return lax.ppermute(value, "dp", [(i, i ^ (2 * flip)) for i in range(dp)])

    def along(value, shift):
        return lax.ppermute(
            value, "narrow", [(i, (i + shift) % narrow) for i in range(narrow)]
        )

    def stage(values, *done):
        return lax.optimization_barrier((values, done))[0]

    def ordered(mine, theirs, axis):
        join = functools.partial(jnp.concatenate, axis=axis)
        return jnp.where(by_core, join([mine, theirs]), join([theirs, mine]))

    def pick(value, index, axis):
        return lax.dynamic_index_in_dim(value, index, axis, keepdims=False)

    def mine_of(value, axis):
        low, high = (lax.index_in_dim(value, i, axis, keepdims=False) for i in range(2))
        return jnp.where(by_core, low, high), jnp.where(by_core, high, low)

    def turn(k):
        return lax.rem(place + (k + narrow), narrow)

    def blocks_for(value):
        return [pick(value, turn(k), 0) for k in range(narrow)]

    far_place = narrow // 2

    def across(blocks, near_late=(), far_late=(), sign=1):
        moved = [blocks[0]]
        for k in range(1, narrow):
            late = far_late if k == far_place else near_late
            moved.append(along(stage(blocks[k], *late) if late else blocks[k], sign * k))
        return moved

    def across_near(blocks, sign=1):
        return [along(blocks[k], sign * k) for k in range(1, narrow) if k != far_place]

    def across_far(block, sign=1):
        return along(block, sign * far_place)

    def joined(own, near, far):
        return [own] + near[: far_place - 1] + [far] + near[far_place - 1 :]

    def near_of(moved):
        return [moved[k] for k in range(1, narrow) if k != far_place]

    def in_order(moved):
        stacked = jnp.stack(moved)
        return jnp.stack([pick(stacked, turn(-i), 0) for i in range(narrow)])

    def group_start(value):
        keep, give = mine_of(value.reshape(bundle, 2, tile, width), 1)
        return ordered(keep, to_core(give), 0)

    def group_back(moved):
        mine, give = mine_of(in_order(moved).reshape(2, bundle, tile, width), 0)
        theirs = to_core(give)
        return ordered(mine[:, None], theirs[:, None], 1).reshape(bundle, row_count, width)

    def split_far(*parts):
        return mine_of(jnp.concatenate(parts, axis=1), 0)

    def two(part):
        return part.reshape(2, part.shape[0] // 2, own_width)

    def canonical(value):
        if chips == BLOCKS:
            return value
        parts = value.reshape((BLOCKS, chips // BLOCKS) + value.shape[1:])
        return jnp.moveaxis(parts, 1, -2).reshape((BLOCKS,) + value.shape[1:-1] + (wide,))

    def scattered(value):
        if chips == BLOCKS:
            return value
        parts = value.reshape(value.shape[:-1] + (chips // BLOCKS, width // chips))
        return jnp.moveaxis(parts, -2, 1).reshape(
            (chips,) + value.shape[1:-1] + (width // chips,)
        )

    def spread(value, *late):
        return across([value] * narrow, (), late)

    near = chips == BLOCKS

    def chips_first(value):
        return (to_chip(value, 1), to_chip(value, 2)) if near else ()

    def chips_second(first, second):
        return to_chip(first[: narrow // 2], 2), to_chip(second[narrow // 2 :], 1)

    def chips_full(value, firsts, seconds):
        if near:
            return jnp.stack([value, *firsts, jnp.concatenate(seconds)])
        return canonical(lax.all_gather(value, "dp", axis_index_groups=same_core))

    def chips_pieces(value, firsts, seconds):
        if near:
            return (value, *firsts, *seconds)
        full = chips_full(value, firsts, seconds)
        return full[0], full[1], full[2], full[3, : narrow // 2], full[3, narrow // 2 :]

    def sum_first(grads):
        x_keep, x_send, y_keep, y_send = grads
        return to_chip(x_send, 1), to_chip(y_send, 2)

    def sum_ready(grads, got):
        x_keep, _, y_keep, _ = grads
        return (
            (x_keep[1].astype(f32) + got[0][1].astype(f32)).astype(bf16),
            (y_keep[1].astype(f32) + got[1][1].astype(f32)).astype(bf16),
        )

    def sum_second(ready):
        return to_chip(ready[0], 2), to_chip(ready[1], 1)

    def sum_done(grads, got, last):
        x_keep, _, y_keep, _ = grads
        x_sum = x_keep[0].astype(f32) + got[0][0].astype(f32) + last[0].astype(f32)
        y_sum = y_keep[0].astype(f32) + got[1][0].astype(f32) + last[1].astype(f32)
        sent = [x_sum[k] for k in range(1, narrow // 2)] + [y_sum[k] for k in range(narrow // 2)]
        return x_sum[0], [None] + [block.astype(bf16) for block in sent]

    def sum_far(grads):
        x_keep, x_send, y_keep, y_send = grads
        x_all = jnp.stack([x_keep, x_send], axis=1).reshape((BLOCKS,) + x_keep.shape[1:])
        y_all = jnp.concatenate([y_keep, y_send])
        value = scattered(
            jnp.concatenate([x_all, y_all], axis=1).reshape(BLOCKS, narrow, -1, wide)
        )
        got = lax.psum_scatter(
            value.reshape(-1, value.shape[-1]),
            "dp",
            scatter_dimension=0,
            tiled=True,
            axis_index_groups=same_core,
        ).reshape(value.shape[1:])
        return got[0].astype(f32), [None] + [got[k] for k in range(1, narrow)]

    def swap_ready(own, got):
        total = own
        for piece in got[1:]:
            total = total + piece.astype(f32)
        low, high = total[:, :own_width], total[:, own_width:]
        return jnp.where(by_core, low, high), jnp.where(by_core, high, low).astype(bf16)

    def finish(keep, theirs, parts, size):
        theirs = theirs.astype(f32)
        both = jnp.where(by_core, jnp.stack([keep, theirs]), jnp.stack([theirs, keep]))
        return [both[:, i * size : (i + 1) * size] for i in range(parts)]

    me = (chip if near else 0 * chip).astype(jnp.int32)[None]
    core_index, place_index = core.astype(jnp.int32)[None], place.astype(jnp.int32)[None]
    kinds = [w_gate.T, w_up.T, w_down]
    depth = w_down.shape[0] // 2
    cut = -(-depth // 32 // 2) * 32
    if near:
        keep, give = square_split_call(
            core_index, bucket, w_query, w_key, w_value, w_out, attn_gain, ffn_gain
        )
    else:
        extra = jnp.concatenate(
            [
                attn_gain[None],
                ffn_gain[None],
                jnp.pad(bucket.astype(bf16), (0, own_width - bundle))[None],
                jnp.zeros((13, own_width), bf16),
            ]
        )
        keep, give = split_far(
            two(w_query.T), two(w_key.T), two(w_value.T), two(w_out), jnp.stack([extra, extra])
        )
        halves = [two(kind) for kind in kinds]
        ffn_keep, ffn_give = split_far(
            *[half[:, :cut] for half in halves], *[half[:, cut:] for half in halves]
        )
    square = ordered(keep, to_core(give), 1)

    square_z = spread(square)
    own_inputs, own_cotangent, kinds, square = stage((inputs, cotangent, kinds, square))
    if near:
        ffn_keep, ffn_give = ffn_split_call(core_index, cut, *kinds)
    x_blocks = blocks_for(group_start(own_inputs))
    cot_blocks = blocks_for(group_start(own_cotangent))
    ffn_theirs = to_core(ffn_give)
    ffn_one = ordered(ffn_keep[: 3 * cut], ffn_theirs[: 3 * cut], 1)
    ffn_two = ordered(ffn_keep[3 * cut :], ffn_theirs[3 * cut :], 1)
    flags = square[4 * 128 + 2].reshape(2, own_width)[:, :bundle].reshape(-1)
    flag = pick(flags.astype(jnp.int32), place, 0)[None]

    square_z, x_blocks, cot_blocks, ffn_one, ffn_two, flag = stage(
        (square_z, x_blocks, cot_blocks, ffn_one, ffn_two, flag)
    )
    square_z = jnp.stack(square_z)
    square_first = chips_first(square_z)
    x_moved = across(x_blocks)

    square_first, x_moved, ffn_one = stage((square_first, x_moved, ffn_one))
    x_own = jnp.stack(x_moved)
    x_other = to_core(x_own)
    square_second = chips_second(*square_first) if near else ()
    one_z = spread(ffn_one, x_other)
    x_rows, hidden, rms, gains, square_full, q, k, v = qkv_call(
        me,
        core_index,
        place_index,
        x_own,
        x_other,
        chips_pieces(square_z, square_first, square_second),
    )

    q, one_z, cot_blocks = stage((q, one_z, cot_blocks))
    one_z = jnp.stack(one_z)
    one_first = chips_first(one_z)
    cot_moved = across(cot_blocks)
    attended, probs = attend_call(flag, q, k, v)

    attended, one_first, cot_moved, ffn_two = stage((attended, one_first, cot_moved, ffn_two))
    one_second = chips_second(*one_first) if near else ()
    branch = branch_call(me, attended, square_full)
    cot_own = jnp.stack(cot_moved)
    two_z = spread(ffn_two, branch)
    middle_place = narrow // 2
    branch, cot_own, one_second, two_near = stage(
        (branch, cot_own, one_second, two_z[:middle_place] + two_z[middle_place + 1 :])
    )
    two_z = two_near[:middle_place] + [two_z[middle_place]] + two_near[middle_place:]
    branch_other, cot_other = to_core(branch), to_core(cot_own)
    middle, normed, cot_rows = middle_call(
        core_index, place_index, x_rows, branch, branch_other, gains, cot_own, cot_other
    )

    normed, two_z = stage((normed, two_z))
    two_z = jnp.stack(two_z)
    two_first = chips_first(two_z)
    part_result, part_d_normed, *one_grads = ffn_call(
        me, core_index, narrow, normed, cot_rows, chips_pieces(one_z, one_first, one_second)
    )

    part_result, part_d_normed, one_grads, two_first = stage(
        (part_result, part_d_normed, one_grads, two_first)
    )
    two_second = chips_second(*two_first) if near else ()

    part_result, part_d_normed, one_grads, two_second = stage(
        (part_result, part_d_normed, one_grads, two_second)
    )
    one_got = sum_first(one_grads) if near else ()
    result, d_normed, *two_grads, result_give = ffn_call(
        me,
        core_index,
        narrow,
        normed,
        cot_rows,
        chips_pieces(two_z, two_first, two_second),
        part_result,
        part_d_normed,
    )

    result_give, d_normed, one_got, two_grads = stage((result_give, d_normed, one_got, two_grads))
    by_rows = (narrow, 2, tile, width)
    d_normed_other, result_other = to_core(d_normed), to_core(result_give)
    one_last = sum_second(sum_ready(one_grads, one_got)) if near else ()
    d_middle, d_branch, d_att, ffn_gain_grad, out_rows = turn_call(
        me,
        core_index,
        middle,
        d_normed,
        d_normed_other,
        cot_rows,
        gains,
        square_full,
        result.reshape(by_rows),
        result_other,
    )
    out_moved = across(blocks_for(out_rows))

    d_att, one_last, two_grads = stage((d_att, one_last, two_grads))
    two_got = sum_first(two_grads) if near else ()
    pairs = d_att.shape[1] // 256
    lefts_one = attend_back_call(0, pairs, flag, q, k, v, attended, d_att, probs)

    lefts_one, d_att, one_grads, one_got, one_last, two_grads, two_got = stage(
        (lefts_one, d_att, one_grads, one_got, one_last, two_grads, two_got), near_of(out_moved)
    )
    two_last = sum_second(sum_ready(two_grads, two_got)) if near else ()
    one_own, one_sent = sum_done(one_grads, one_got, one_last) if near else sum_far(one_grads)
    lefts_two = attend_back_call(pairs, pairs, flag, q, k, v, attended, d_att, probs)
    one_near = across_near(one_sent, -1)

    lefts_two, two_last, out_moved, one_near, one_far = stage(
        (lefts_two, two_last, out_moved, one_near, one_sent[far_place])
    )
    one_places = joined(None, one_near, across_far(one_far, -1))
    two_own, two_sent = sum_done(two_grads, two_got, two_last) if near else sum_far(two_grads)
    two_sent[0] = two_own
    two_places = across(two_sent, (), (), -1)
    lefts = [left for both in zip(lefts_one, lefts_two) for left in both]
    d_hidden, d_hidden_give, *square_grads = square_call(
        me, core_index, lefts, attended, hidden, d_branch, square_full, x_rows, rms, 0.5 * ffn_gain_grad
    )

    d_hidden_give, square_grads, out_moved = stage(
        (d_hidden_give, square_grads, out_moved), near_of(two_places), one_places[far_place]
    )
    square_got = sum_first(square_grads) if near else ()
    d_hidden_other = to_core(d_hidden_give)
    input_blocks = blocks_for(
        input_call(
            core_index, x_rows, d_middle, d_hidden.reshape(by_rows), d_hidden_other, gains
        )
    )
    input_near = across_near(input_blocks)
    outputs = group_back(out_moved)
    one_keep, one_swap = swap_ready(one_own, one_places)

    square_got, one_swap, input_near, input_far, two_places = stage(
        (square_got, one_swap, input_near, input_blocks[far_place], two_places)
    )
    input_moved = joined(input_blocks[0], input_near, across_far(input_far))
    square_last = sum_second(sum_ready(square_grads, square_got)) if near else ()
    one_theirs = to_core(one_swap)
    two_keep, two_swap = swap_ready(two_own, two_places)

    square_last, input_moved, two_swap = stage((square_last, input_moved, two_swap))
    square_own, square_sent = (
        sum_done(square_grads, square_got, square_last) if near else sum_far(square_grads)
    )
    square_places = across(square_sent, (), (), -1)
    two_theirs = to_core(two_swap)
    input_grad = group_back(input_moved).astype(f32)
    one_parts = finish(one_keep, one_theirs, 3, cut)
    two_parts = finish(two_keep, two_theirs, 3, depth - cut)
    g_gate, g_up, g_down = [
        jnp.concatenate(parts, axis=1).reshape(2 * depth, own_width)
        for parts in zip(one_parts, two_parts)
    ]
    g_gate, g_up = g_gate.T, g_up.T
    square_places, outputs, input_grad, g_gate, g_up, g_down = stage(
        (square_places, outputs, input_grad, g_gate, g_up, g_down)
    )
    square_keep, square_swap = swap_ready(square_own, square_places)
    square_theirs = to_core(square_swap)
    g_query, g_key, g_value, g_out = [
        part.reshape(-1, own_width) for part in finish(square_keep, square_theirs, 4, 128)
    ]
    gain_own = square_keep[4 * 128 :] + square_theirs[4 * 128 :].astype(f32)
    return (
        outputs,
        input_grad,
        gain_own[0],
        g_query.T,
        g_key.T,
        g_value.T,
        g_out,
        gain_own[1],
        g_gate,
        g_up,
        g_down,
    )


def solution(mesh):
    rows = P("dp", "narrow", None)
    tall, flat = P("dp", "narrow"), P("narrow", "dp")
    return jax.shard_map(
        per_device,
        mesh=mesh,
        in_specs=(rows, P("dp"), P("dp"), tall, tall, tall, flat, P("dp"), tall, tall, flat, rows),
        out_specs=(rows, rows, P("dp"), tall, tall, tall, flat, P("dp"), tall, tall, flat),
        check_vma=False,
    )
```

```python
import functools

import jax
import jax.numpy as jnp
from jax import lax
from jax.experimental import pallas as pl
from jax.experimental.pallas import tpu as pltpu
from jax.sharding import PartitionSpec as P

HEAD = 64
SHORT = 384
EPS = 1e-06
BLOCKS = 4
f32 = jnp.float32
bf16 = jnp.bfloat16


def dot_nn(left, right):
    return jnp.dot(left, right, preferred_element_type=f32)


def dot_nt(left, right):
    return lax.dot_general(left, right, (((1,), (1,)), ((), ())), preferred_element_type=f32)


def call(kernel, grid, prefetch, in_specs, out_specs, out_shape, scratch, flops, moved, vmem):
    return pl.pallas_call(
        kernel,
        grid_spec=pltpu.PrefetchScalarGridSpec(
            num_scalar_prefetch=prefetch,
            grid=grid,
            in_specs=in_specs,
            out_specs=out_specs,
            scratch_shapes=scratch,
        ),
        out_shape=out_shape,
        compiler_params=pltpu.CompilerParams(vmem_limit_bytes=vmem << 20),
        cost_estimate=pl.CostEstimate(flops=flops, bytes_accessed=moved, transcendentals=0),
    )


def shaped(shape, dtype):
    return jax.ShapeDtypeStruct(shape, dtype)


def rms_of(rows):
    return lax.rsqrt(jnp.mean(rows * rows, axis=-1, keepdims=True) + EPS)


def store_grad(refs, step, grad, first):
    x_keep, x_send, y_keep, y_send = refs
    half, rows = grad.shape[0] // 2, slice(first, first + grad.shape[1])
    (x_send if step % 2 else x_keep)[step // 2, :, rows] = grad[:half]
    (y_send if step // 2 else y_keep)[step % 2, :, rows] = grad[half:]


def grad_shapes(pieces, rows, wide):
    return [shaped((2, pieces // 2, rows, wide), bf16)] * 4


def square_split_kernel(
    core_ref, bucket_ref, q_ref, k_ref, v_ref, o_ref, attn_ref, ffn_ref, keep_ref, give_ref
):
    halves = [ref[...].T for ref in (q_ref, k_ref, v_ref)] + [o_ref[...]]
    shape = (16, keep_ref.shape[1])
    row, lane = (lax.broadcasted_iota(jnp.int32, shape, axis) for axis in range(2))
    flags = jnp.zeros(shape, f32)
    for i in range(bucket_ref.shape[0]):
        flags = jnp.where(lane == i, bucket_ref[i].astype(f32), flags)
    flags = jnp.where(row == 2, flags, 0.0)
    flags = jnp.where(row == 1, ffn_ref[...].astype(f32), flags)
    extra = jnp.where(row == 0, attn_ref[...].astype(f32), flags).astype(bf16)

    def store(low_ref, high_ref):
        start = 0
        for half in halves:
            count = half.shape[0] // 2
            low_ref[start : start + count] = half[:count]
            high_ref[start : start + count] = half[count:]
            start += count
        low_ref[start:] = extra
        high_ref[start:] = extra

    @pl.when(core_ref[0] == 0)
    def _():
        store(keep_ref, give_ref)

    @pl.when(core_ref[0] != 0)
    def _():
        store(give_ref, keep_ref)


def square_split_call(core, bucket, q, k, v, o, attn, ffn):
    rows, cols = q.shape[1] // 2 * 4 + 16, o.shape[1]
    whole = pl.BlockSpec(memory_space=pltpu.VMEM)
    return call(
        square_split_kernel,
        (),
        2,
        [whole] * 6,
        [whole] * 2,
        [shaped((rows, cols), bf16)] * 2,
        [],
        0,
        1 << 20,
        16,
    )(core, bucket, q, k, v, o, attn[None], ffn[None])


def ffn_split_kernel(cut, core_ref, *refs):
    parts, (keep_ref, give_ref) = refs[:3], refs[3:]

    def store(low_ref, high_ref):
        start = 0
        half = parts[0].shape[0] // 2
        for first, last in ((0, cut), (cut, half)):
            for part in parts:
                count = last - first
                low_ref[start : start + count] = part[first:last]
                high_ref[start : start + count] = part[half + first : half + last]
                start += count

    @pl.when(core_ref[0] == 0)
    def _():
        store(keep_ref, give_ref)

    @pl.when(core_ref[0] != 0)
    def _():
        store(give_ref, keep_ref)


def ffn_split_call(core, cut, gate, up, down):
    rows, cols = gate.shape[0] // 2 * 3, gate.shape[1]
    whole = pl.BlockSpec(memory_space=pltpu.VMEM)
    return call(
        functools.partial(ffn_split_kernel, cut),
        (),
        1,
        [whole] * 3,
        [whole] * 2,
        [shaped((rows, cols), bf16)] * 2,
        [],
        0,
        1 << 20,
        16,
    )(core, gate, up, down)


def join_rows(core_ref, own_ref, other_ref, out_ref):
    count = own_ref.shape[1]

    @pl.when(core_ref[0] == 0)
    def _():
        out_ref[:count] = own_ref[0]
        out_ref[count:] = other_ref[0]

    @pl.when(core_ref[0] != 0)
    def _():
        out_ref[:count] = other_ref[0]
        out_ref[count:] = own_ref[0]


def qkv_kernel(
    me_ref, core_ref, place_ref, own_ref, other_ref, w0, w1, w2, w3, w4, x_ref, hidden_ref, rms_ref, gains_ref, w_ref, q_ref, k_ref, v_ref
):
    @pl.when(pl.program_id(0) == 0)
    def _():
        for step, piece in enumerate((w0, w1, w2)):
            w_ref[step] = piece[...]
        w_ref[3, : w3.shape[0]] = w3[...]
        w_ref[3, w3.shape[0] :] = w4[...]

    join_rows(core_ref, own_ref, other_ref, x_ref)
    rows = x_ref[...].astype(f32)
    rms = rms_of(rows)
    rms_ref[...] = jnp.broadcast_to(rms, rms_ref.shape)
    wide = w_ref.shape[3]
    half = w_ref.shape[1] * 128
    for step in range(BLOCKS):
        columns = pl.ds(pl.multiple_of((me_ref[0] ^ step) * wide, wide), wide)
        gains = w_ref[step, 0, 4 * 128 :, :].astype(f32)
        gains_ref[:, columns] = gains[:8]
        hidden_ref[:, columns] = (x_ref[:, columns].astype(f32) * rms * gains[:1]).astype(bf16)
    for part, ref in enumerate((q_ref, k_ref, v_ref)):
        total = None
        for step in range(BLOCKS):
            start = pl.multiple_of((me_ref[0] ^ step) * wide, wide)
            weight = w_ref[step, :, part * 128 : (part + 1) * 128, :].reshape(half, wide)
            piece = dot_nt(hidden_ref[:, pl.ds(start, wide)], weight)
            total = piece if total is None else total + piece
        if part == 0:
            total = total * (HEAD**-0.5)
        ref[...] = total.astype(bf16)


def qkv_call(me, core, place, own, other, weights):
    places, half_tile, width = own.shape
    half = weights[0].shape[0] * 128
    tile, count = 2 * half_tile, 2 * half_tile * places
    all_shape = (BLOCKS,) + weights[0].shape
    row_spec = pl.BlockSpec((tile, width), lambda i, me, core, place: (i, 0))
    half_spec = pl.BlockSpec((tile, half), lambda i, me, core, place: (i, 0))
    part_spec = pl.BlockSpec(
        (1, half_tile, width), lambda i, me, core, place: ((place[0] + places - i) % places, 0, 0)
    )
    return call(
        qkv_kernel,
        (places,),
        3,
        [
            part_spec,
            part_spec,
        ]
        + [pl.BlockSpec(w.shape, lambda i, me, core, place: (0, 0, 0)) for w in weights],
        [
            row_spec,
            row_spec,
            pl.BlockSpec((tile, 128), lambda i, me, core, place: (i, 0)),
            pl.BlockSpec((8, width), lambda i, me, core, place: (0, 0)),
            pl.BlockSpec(all_shape, lambda i, me, core, place: (0, 0, 0, 0)),
            half_spec,
            half_spec,
            half_spec,
        ],
        [shaped((count, width), bf16)] * 2
        + [shaped((count, 128), f32), shaped((8, width), f32), shaped(all_shape, bf16)]
        + [shaped((count, half), bf16)] * 3,
        [],
        2 * count * width * half * 3,
        12 << 20,
        40,
    )(me, core, place, own, other, *weights)


def two_heads(rows):
    low = lax.broadcasted_iota(jnp.int32, rows.shape, 1) < HEAD
    zero = jnp.zeros_like(rows)
    return jnp.concatenate([jnp.where(low, rows, zero), jnp.where(low, zero, rows)], axis=0)


def one_pair(both):
    half = both.shape[1] // 2
    return jnp.concatenate([both[:HEAD, :half], both[HEAD:, half:]], axis=0)


def attend_kernel(flag_ref, q_ref, k_ref, v_ref, out_ref, probs_ref, v_turned):
    block = pl.program_id(1)

    @pl.when(block == 0)
    def _():
        v_turned[...] = v_ref[...].T

    queries = two_heads(q_ref[...])

    def attend(keys, values):
        scores = dot_nt(keys, queries)
        expo = jnp.exp(scores - jnp.max(scores, axis=0, keepdims=True))
        probs = (expo * (1.0 / jnp.sum(expo, axis=0, keepdims=True))).astype(bf16)
        probs_ref[0, 0, : keys.shape[0], :] = probs
        out_ref[...] = one_pair(dot_nn(values, probs)).T.astype(bf16)

    @pl.when(flag_ref[0] == 1)
    def _():
        attend(k_ref[...], v_turned[...])

    @pl.when(flag_ref[0] != 1)
    def _():
        start = pl.multiple_of(block * SHORT, SHORT)
        attend(k_ref[pl.ds(start, SHORT), :], v_turned[:, pl.ds(start, SHORT)])


def attend_call(flag, q, k, v):
    count, half = q.shape
    pairs, blocks = half // 128, count // SHORT
    some = pl.BlockSpec((SHORT, 128), lambda j, i, flag: (i, j))
    every = pl.BlockSpec((count, 128), lambda j, i, flag: (0, j))
    return call(
        attend_kernel,
        (pairs, blocks),
        1,
        [some, every, every],
        [some, pl.BlockSpec((1, 1, count, 2 * SHORT), lambda j, i, flag: (j, i, 0, 0))],
        [shaped(q.shape, bf16), shaped((pairs, blocks, count, 2 * SHORT), bf16)],
        [pltpu.VMEM((128, count), bf16)],
        4 * 4 * count * count * half,
        28 << 20,
        40,
    )(flag, q, k, v)


def branch_kernel(me_ref, att_ref, w_ref, out_ref):
    wide = w_ref.shape[3]
    for step in range(BLOCKS):
        start = pl.multiple_of((me_ref[0] ^ step) * wide, wide)
        weight = w_ref[step].reshape(att_ref.shape[1], wide)
        out_ref[:, pl.ds(start, wide)] = dot_nn(att_ref[...], weight).astype(bf16)


def branch_call(me, attended, weights):
    count, half = attended.shape
    width = weights.shape[0] * weights.shape[3]
    tile = count // 4
    block = weights.shape[:2] + (128,) + weights.shape[3:]
    return call(
        branch_kernel,
        (count // tile,),
        1,
        [
            pl.BlockSpec((tile, half), lambda i, me: (i, 0)),
            pl.BlockSpec(block, lambda i, me: (0, 0, 3, 0)),
        ],
        pl.BlockSpec((tile, width), lambda i, me: (i, 0)),
        shaped((count, width), bf16),
        [],
        2 * count * width * half,
        5 << 20,
        24,
    )(me, attended, weights)


def middle_kernel(
    core_ref, place_ref, x_ref, one_ref, two_ref, gain_ref, own_ref, other_ref, middle_ref, normed_ref, cot_ref
):
    middle = x_ref[...].astype(f32) + (one_ref[...].astype(f32) + two_ref[...].astype(f32))
    middle_ref[...] = middle
    normed_ref[...] = (middle * rms_of(middle) * gain_ref[1:2, :]).astype(bf16)
    join_rows(core_ref, own_ref, other_ref, cot_ref)


def middle_call(core, place, rows, one, two, gain, own, other):
    count, width = rows.shape
    places, half_tile = own.shape[:2]
    spec = pl.BlockSpec((2 * half_tile, width), lambda i, core, place: (i, 0))
    part_spec = pl.BlockSpec(
        (1, half_tile, width), lambda i, core, place: ((place[0] + places - i) % places, 0, 0)
    )
    return call(
        middle_kernel,
        (places,),
        2,
        [spec] * 3
        + [pl.BlockSpec((8, width), lambda i, core, place: (0, 0)), part_spec, part_spec],
        [spec] * 3,
        [shaped(rows.shape, f32), shaped(rows.shape, bf16), shaped(rows.shape, bf16)],
        [],
        0,
        14 << 20,
        32,
    )(core, place, rows, one, two, gain, own, other)


def ffn_kernel(given, prior, me_ref, core_ref, normed_ref, d_out_ref, *refs):
    pieces_of, refs = refs[:given], refs[given:]
    before = refs[:2] if prior else None
    refs = refs[2 if prior else 0 :]
    result_ref, d_normed_ref = refs[:2]
    grad_refs, refs = refs[2:6], refs[6:]
    give_ref = refs[0] if prior else None
    weights, inner_t, gate_t, up_t = refs[1 if prior else 0 :]
    pieces, rows_all, wide = pieces_of[0].shape
    parts, kinds, depth = BLOCKS, 3, rows_all // 3
    units = pieces * depth
    tile = SHORT

    def columns(step):
        return pl.ds(pl.multiple_of((me_ref[0] ^ step) * wide, wide), wide)

    for kind in range(kinds):
        rows = slice(kind * depth, (kind + 1) * depth)
        for step in range(parts):
            start = 0
            for piece in pieces_of[step:] if step == parts - 1 else pieces_of[step : step + 1]:
                count = piece.shape[0] * depth
                value = piece[:, rows, :].reshape(count, wide)
                weights[kind, start : start + count, columns(step)] = value
                start += count

    def rows_step(index, carry):
        rows = pl.ds(pl.multiple_of(index * tile, tile), tile)
        normed = normed_ref[rows, :]
        gate, up = dot_nt(normed, weights[0]), dot_nt(normed, weights[1])
        d_inner = dot_nt(d_out_ref[rows, :], weights[2])
        square = gate * gate
        bent = jnp.tanh(gate * (0.7978845608 + 0.7978845608 * 0.044715 * square))
        half = 0.5 + 0.5 * bent
        gelu = gate * half
        slope = half + gate * (0.5 - 0.5 * bent * bent) * (
            0.7978845608 + 0.7978845608 * 3 * 0.044715 * square
        )
        inner = (gelu * up).astype(bf16)
        d_gate = (d_inner * up * slope).astype(bf16)
        d_up = (d_inner * gelu).astype(bf16)
        inner_t[:, rows] = inner.T
        gate_t[:, rows] = d_gate.T
        up_t[:, rows] = d_up.T
        forward = dot_nn(inner, weights[2])
        backward = dot_nn(d_gate, weights[0]) + dot_nn(d_up, weights[1])
        if prior:
            forward += before[0][rows, :].astype(f32)
            backward += before[1][rows, :].astype(f32)
        result_ref[rows, :] = forward.astype(bf16)
        d_normed_ref[rows, :] = backward.astype(bf16)
        return carry

    lax.fori_loop(0, normed_ref.shape[0] // tile, rows_step, 0)
    for step in range(parts):
        here, there = normed_ref[:, columns(step)], d_out_ref[:, columns(step)]
        for kind, (left, right) in enumerate(((gate_t, here), (up_t, here), (inner_t, there))):
            grad = dot_nn(left[...], right).astype(bf16)
            store_grad(grad_refs, step, grad.reshape(pieces, depth, wide), kind * depth)
    if prior:
        give_rows(core_ref, result_ref, give_ref)


def give_rows(core_ref, all_ref, give_ref):
    places, count = give_ref.shape[:2]
    for place in range(places):
        start = (2 * place + 1 - core_ref[0]) * count
        give_ref[place] = all_ref[pl.ds(pl.multiple_of(start, count), count), :]


def ffn_call(me, core, places, normed, d_out, weights, *before):
    count, width = normed.shape
    pieces, rows_all, wide = weights[0].shape
    units = pieces * rows_all // 3
    whole = pl.BlockSpec(memory_space=pltpu.VMEM)
    return call(
        functools.partial(ffn_kernel, len(weights), bool(before)),
        (),
        2,
        [whole] * (2 + len(weights) + len(before)),
        [whole] * (7 if before else 6),
        [shaped(normed.shape, bf16)] * 2
        + grad_shapes(pieces, rows_all, wide)
        + ([shaped((places, count // places // 2, width), bf16)] if before else []),
        [pltpu.VMEM((3, units, width), bf16)] + [pltpu.VMEM((units, count), bf16)] * 3,
        18 * count * width * units,
        20 << 20,
        48,
    )(me, core, normed, d_out, *weights, *before)


def turn_kernel(
    me_ref,
    core_ref,
    middle_ref,
    one_ref,
    two_ref,
    cot_ref,
    gain_ref,
    w_ref,
    own_ref,
    other_ref,
    d_middle_ref,
    d_branch_ref,
    d_att_ref,
    gain_grad_ref,
    out_ref,
):
    middle = middle_ref[...]
    rms = rms_of(middle)
    scaled = middle * rms
    d_normed = one_ref[...].astype(f32) + two_ref[...].astype(f32)
    pulled = d_normed * gain_ref[1:2, :]
    d_middle = cot_ref[...].astype(f32) + rms * (
        pulled - scaled * jnp.mean(pulled * scaled, axis=-1, keepdims=True)
    )
    d_branch_ref[...] = d_middle.astype(bf16)
    count = out_ref.shape[1]

    @pl.when(core_ref[0] == 0)
    def _():
        d_middle_ref[0] = d_middle[:count]

    @pl.when(core_ref[0] != 0)
    def _():
        d_middle_ref[0] = d_middle[count:]

    rows = pl.ds(pl.multiple_of(core_ref[0] * count, count), count)
    out_ref[0] = (
        middle_ref[rows, :] + (own_ref[0, 0].astype(f32) + other_ref[0].astype(f32))
    ).astype(bf16)

    @pl.when(pl.program_id(0) == 0)
    def _():
        gain_grad_ref[...] = jnp.zeros_like(gain_grad_ref)

    gain_grad_ref[...] += jnp.sum(d_normed * scaled, axis=0, keepdims=True)
    wide = w_ref.shape[3]
    total = None
    for step in range(BLOCKS):
        start = pl.multiple_of((me_ref[0] ^ step) * wide, wide)
        piece = dot_nt(d_branch_ref[:, pl.ds(start, wide)], w_ref[step].reshape(d_att_ref.shape[1], wide))
        total = piece if total is None else total + piece
    d_att_ref[...] = total.astype(bf16)


def turn_call(me, core, middle, one, two, cot, gain, weights, own, other):
    count, width = middle.shape
    half = weights.shape[1] * 128
    places, _, half_tile, _ = own.shape
    tile = 2 * half_tile
    spec = pl.BlockSpec((tile, width), lambda i, me, core: (i, 0))
    line = pl.BlockSpec((1, width), lambda i, me, core: (0, 0))
    gain_spec = pl.BlockSpec((8, width), lambda i, me, core: (0, 0))
    plain = pl.BlockSpec((1, half_tile, width), lambda i, me, core: (i, 0, 0))
    block = weights.shape[:2] + (128,) + weights.shape[3:]
    return call(
        turn_kernel,
        (places,),
        2,
        [spec, spec, spec, spec, gain_spec]
        + [pl.BlockSpec(block, lambda i, me, core: (0, 0, 3, 0))]
        + [pl.BlockSpec((1, 1, half_tile, width), lambda i, me, core: (i, core[0], 0, 0)), plain],
        [plain, spec, pl.BlockSpec((tile, half), lambda i, me, core: (i, 0)), line, plain],
        [
            shaped((places, half_tile, width), f32),
            shaped(middle.shape, bf16),
            shaped((count, half), bf16),
            shaped((1, width), f32),
            shaped((places, half_tile, width), bf16),
        ],
        [],
        2 * count * width * half,
        22 << 20,
        40,
    )(me, core, middle, one, two, cot, gain, weights, own, other)


def attend_back_kernel(
    flag_ref, q_ref, k_ref, v_ref, out_ref, d_out_ref, probs_ref, dq_ref, dk_ref, dv_ref, k_turned, dk_sum, dv_sum
):
    block, blocks = pl.program_id(1), pl.num_programs(1)

    @pl.when(block == 0)
    def _():
        k_turned[...] = k_ref[...].T

    queries, grads = two_heads(q_ref[...]), two_heads(d_out_ref[...])
    turned = (d_out_ref[...].astype(f32) * out_ref[...].astype(f32)).T
    delta = jnp.concatenate(
        [
            jnp.sum(turned[:HEAD], axis=0, keepdims=True),
            jnp.sum(turned[HEAD:], axis=0, keepdims=True),
        ],
        axis=1,
    )

    def back(values, keys_turned):
        probs = probs_ref[0, 0, : values.shape[0], :]
        d_probs = dot_nt(values, grads)
        d_scores = (probs.astype(f32) * (d_probs - delta)).astype(bf16)
        d_query = one_pair(dot_nn(keys_turned, d_scores)).T * (HEAD**-0.5)
        dq_ref[...] = d_query.astype(bf16)
        return dot_nn(d_scores, queries), dot_nn(probs, grads)

    @pl.when(flag_ref[0] == 1)
    def _():
        d_key, d_value = back(v_ref[...], k_turned[...])

        @pl.when(block == 0)
        def _():
            dk_sum[...] = d_key
            dv_sum[...] = d_value

        @pl.when(block > 0)
        def _():
            dk_sum[...] += d_key
            dv_sum[...] += d_value

    @pl.when(flag_ref[0] != 1)
    def _():
        rows = pl.ds(pl.multiple_of(block * SHORT, SHORT), SHORT)
        d_key, d_value = back(v_ref[rows, :], k_turned[:, rows])
        dk_sum[rows, :] = d_key
        dv_sum[rows, :] = d_value

    @pl.when(block == blocks - 1)
    def _():
        dk_ref[...] = dk_sum[...].astype(bf16)
        dv_ref[...] = dv_sum[...].astype(bf16)


def attend_back_call(first, pairs, flag, q, k, v, out, d_out, probs):
    count, half = q.shape
    blocks = count // SHORT
    some = pl.BlockSpec((SHORT, 128), lambda j, i, flag: (i, j + first))
    every = pl.BlockSpec((count, 128), lambda j, i, flag: (0, j + first))
    some_out = pl.BlockSpec((SHORT, 128), lambda j, i, flag: (i, j))
    every_out = pl.BlockSpec((count, 128), lambda j, i, flag: (0, j))
    return call(
        attend_back_kernel,
        (pairs, blocks),
        1,
        [
            some,
            every,
            every,
            some,
            some,
            pl.BlockSpec((1, 1, count, 2 * SHORT), lambda j, i, flag: (j + first, i, 0, 0)),
        ],
        [some_out, every_out, every_out],
        [shaped((count, pairs * 128), bf16)] * 3,
        [pltpu.VMEM((128, count), bf16)] + [pltpu.VMEM((count, 128), f32)] * 2,
        4 * 8 * count * count * pairs * 128,
        16 << 20,
        40,
    )(flag, q, k, v, out, d_out, probs)


def square_kernel(
    me_ref,
    core_ref,
    dq_one,
    dq_two,
    dk_one,
    dk_two,
    dv_one,
    dv_two,
    att_ref,
    hidden_ref,
    d_branch_ref,
    w_ref,
    x_ref,
    rms_ref,
    line_ref,
    d_hidden_ref,
    give_ref,
    *refs,
):
    grad_refs, turned = refs[:4], refs[4]
    pieces, wide = w_ref.shape[1], w_ref.shape[3]
    lefts = (dq_one, dq_two, dk_one, dk_two, dv_one, dv_two)
    start = 0
    for ref in (*lefts, att_ref):
        stop = start + ref.shape[1]
        turned[start:stop, :] = ref[...].T
        start = stop
    half = att_ref.shape[1]
    for step in range(BLOCKS):
        columns = pl.ds(pl.multiple_of((me_ref[0] ^ step) * wide, wide), wide)
        for part in range(4):
            right = d_branch_ref if part == 3 else hidden_ref
            grad = dot_nn(turned[part * half : (part + 1) * half, :], right[:, columns])
            grad = grad.astype(bf16).reshape(pieces, 128, wide)
            store_grad(grad_refs, step, grad, part * 128)
        total = None
        for index, ref in enumerate(lefts):
            part, side = index // 2, index % 2 * pieces // 2
            rows = slice(part * 128, (part + 1) * 128)
            weight = w_ref[step, side : side + pieces // 2, rows, :].reshape(half // 2, wide)
            piece = dot_nn(ref[...], weight)
            total = piece if total is None else total + piece
        d_hidden_ref[:, columns] = total.astype(bf16)
        scaled = x_ref[:, columns].astype(f32) * rms_ref[:, :1]
        attn = jnp.sum(total * scaled, axis=0, keepdims=True)
        lines = jnp.concatenate(
            [attn, line_ref[:, columns], jnp.zeros((14, wide), f32)], axis=0
        ).astype(bf16)
        store_grad(grad_refs, step, jnp.broadcast_to(lines[None], (pieces, 16, wide)), 4 * 128)
    give_rows(core_ref, d_hidden_ref, give_ref)


def square_call(me, core, lefts, attended, hidden, d_branch, weights, x_rows, rms, line):
    count, half = attended.shape
    width = hidden.shape[1]
    pieces, depth, wide = weights.shape[1:]
    whole = pl.BlockSpec(memory_space=pltpu.VMEM)
    return call(
        square_kernel,
        (),
        2,
        [whole] * (len(lefts) + 7),
        [whole] * 6,
        [shaped(hidden.shape, bf16), shaped((pieces, count // pieces // 2, width), bf16)]
        + grad_shapes(pieces, depth, wide),
        [pltpu.VMEM((4 * half, count), bf16)],
        14 * count * width * half,
        24 << 20,
        52,
    )(me, core, *lefts, attended, hidden, d_branch, weights, x_rows, rms, line)


def input_kernel(core_ref, x_ref, d_middle_ref, own_ref, other_ref, gain_ref, out_ref):
    rows = x_ref[0, 0].astype(f32)
    rms = rms_of(rows)
    scaled = rows * rms
    d_hidden = own_ref[0, 0].astype(f32) + other_ref[0].astype(f32)
    pulled = d_hidden * gain_ref[:1, :]
    out_ref[0] = (
        d_middle_ref[0]
        + rms * (pulled - scaled * jnp.mean(pulled * scaled, axis=-1, keepdims=True))
    ).astype(bf16)


def input_call(core, rows, d_middle, own, other, gains):
    slots, halves, tile, width = own.shape
    mine = pl.BlockSpec((1, 1, tile, width), lambda i, core: (i, core[0], 0, 0))
    plain = pl.BlockSpec((1, tile, width), lambda i, core: (i, 0, 0))
    return call(
        input_kernel,
        (slots,),
        1,
        [mine, plain, mine, plain, pl.BlockSpec((8, width), lambda i, core: (0, 0))],
        plain,
        shaped((slots, tile, width), bf16),
        [],
        0,
        8 << 20,
        16,
    )(core, rows.reshape(own.shape), d_middle, own, other, gains)


def per_device(
    inputs,
    bucket,
    attn_gain,
    w_query,
    w_key,
    w_value,
    w_out,
    ffn_gain,
    w_gate,
    w_up,
    w_down,
    cotangent,
):
    dp, narrow = lax.axis_size("dp"), lax.axis_size("narrow")
    chips = dp // 2
    core, chip = lax.axis_index("dp") % 2, lax.axis_index("dp") // 2
    place = lax.axis_index("narrow")
    same_core = [[2 * m + c for m in range(chips)] for c in range(2)]
    by_core = core == 0
    bundle, row_count, width = inputs.shape
    tile = row_count // 2
    own_width = w_query.shape[0]
    wide = width // BLOCKS

    def to_core(value):
        return lax.ppermute(value, "dp", [(i, i ^ 1) for i in range(dp)])

    def to_chip(value, flip):
        return lax.ppermute(value, "dp", [(i, i ^ (2 * flip)) for i in range(dp)])

    def along(value, shift):
        return lax.ppermute(
            value, "narrow", [(i, (i + shift) % narrow) for i in range(narrow)]
        )

    def stage(values, *done):
        return lax.optimization_barrier((values, done))[0]

    def ordered(mine, theirs, axis):
        join = functools.partial(jnp.concatenate, axis=axis)
        return jnp.where(by_core, join([mine, theirs]), join([theirs, mine]))

    def pick(value, index, axis):
        return lax.dynamic_index_in_dim(value, index, axis, keepdims=False)

    def mine_of(value, axis):
        low, high = (lax.index_in_dim(value, i, axis, keepdims=False) for i in range(2))
        return jnp.where(by_core, low, high), jnp.where(by_core, high, low)

    def turn(k):
        return lax.rem(place + (k + narrow), narrow)

    def blocks_for(value):
        return [pick(value, turn(k), 0) for k in range(narrow)]

    far_place = narrow // 2

    def across(blocks, near_late=(), far_late=(), sign=1):
        moved = [blocks[0]]
        for k in range(1, narrow):
            late = far_late if k == far_place else near_late
            moved.append(along(stage(blocks[k], *late) if late else blocks[k], sign * k))
        return moved

    def across_near(blocks, sign=1):
        return [along(blocks[k], sign * k) for k in range(1, narrow) if k != far_place]

    def across_far(block, sign=1):
        return along(block, sign * far_place)

    def joined(own, near, far):
        return [own] + near[: far_place - 1] + [far] + near[far_place - 1 :]

    def near_of(moved):
        return [moved[k] for k in range(1, narrow) if k != far_place]

    def in_order(moved):
        stacked = jnp.stack(moved)
        return jnp.stack([pick(stacked, turn(-i), 0) for i in range(narrow)])

    def group_start(value):
        keep, give = mine_of(value.reshape(bundle, 2, tile, width), 1)
        return ordered(keep, to_core(give), 0)

    def group_back(moved):
        mine, give = mine_of(in_order(moved).reshape(2, bundle, tile, width), 0)
        theirs = to_core(give)
        return ordered(mine[:, None], theirs[:, None], 1).reshape(bundle, row_count, width)

    def split_far(*parts):
        return mine_of(jnp.concatenate(parts, axis=1), 0)

    def two(part):
        return part.reshape(2, part.shape[0] // 2, own_width)

    def canonical(value):
        if chips == BLOCKS:
            return value
        parts = value.reshape((BLOCKS, chips // BLOCKS) + value.shape[1:])
        return jnp.moveaxis(parts, 1, -2).reshape((BLOCKS,) + value.shape[1:-1] + (wide,))

    def scattered(value):
        if chips == BLOCKS:
            return value
        parts = value.reshape(value.shape[:-1] + (chips // BLOCKS, width // chips))
        return jnp.moveaxis(parts, -2, 1).reshape(
            (chips,) + value.shape[1:-1] + (width // chips,)
        )

    def spread(value, *late):
        return across([value] * narrow, (), late)

    near = chips == BLOCKS

    def chips_first(value):
        return (to_chip(value, 1), to_chip(value, 2)) if near else ()

    def chips_second(first, second):
        return to_chip(first[: narrow // 2], 2), to_chip(second[narrow // 2 :], 1)

    def chips_full(value, firsts, seconds):
        if near:
            return jnp.stack([value, *firsts, jnp.concatenate(seconds)])
        return canonical(lax.all_gather(value, "dp", axis_index_groups=same_core))

    def chips_pieces(value, firsts, seconds):
        if near:
            return (value, *firsts, *seconds)
        full = chips_full(value, firsts, seconds)
        return full[0], full[1], full[2], full[3, : narrow // 2], full[3, narrow // 2 :]

    def sum_first(grads):
        x_keep, x_send, y_keep, y_send = grads
        return to_chip(x_send, 1), to_chip(y_send, 2)

    def sum_ready(grads, got):
        x_keep, _, y_keep, _ = grads
        return (
            (x_keep[1].astype(f32) + got[0][1].astype(f32)).astype(bf16),
            (y_keep[1].astype(f32) + got[1][1].astype(f32)).astype(bf16),
        )

    def sum_second(ready):
        return to_chip(ready[0], 2), to_chip(ready[1], 1)

    def sum_done(grads, got, last):
        x_keep, _, y_keep, _ = grads
        x_sum = x_keep[0].astype(f32) + got[0][0].astype(f32) + last[0].astype(f32)
        y_sum = y_keep[0].astype(f32) + got[1][0].astype(f32) + last[1].astype(f32)
        sent = [x_sum[k] for k in range(1, narrow // 2)] + [y_sum[k] for k in range(narrow // 2)]
        return x_sum[0], [None] + [block.astype(bf16) for block in sent]

    def sum_far(grads):
        x_keep, x_send, y_keep, y_send = grads
        x_all = jnp.stack([x_keep, x_send], axis=1).reshape((BLOCKS,) + x_keep.shape[1:])
        y_all = jnp.concatenate([y_keep, y_send])
        value = scattered(
            jnp.concatenate([x_all, y_all], axis=1).reshape(BLOCKS, narrow, -1, wide)
        )
        got = lax.psum_scatter(
            value.reshape(-1, value.shape[-1]),
            "dp",
            scatter_dimension=0,
            tiled=True,
            axis_index_groups=same_core,
        ).reshape(value.shape[1:])
        return got[0].astype(f32), [None] + [got[k] for k in range(1, narrow)]

    def swap_ready(own, got):
        total = own
        for piece in got[1:]:
            total = total + piece.astype(f32)
        low, high = total[:, :own_width], total[:, own_width:]
        return jnp.where(by_core, low, high), jnp.where(by_core, high, low).astype(bf16)

    def finish(keep, theirs, parts, size):
        theirs = theirs.astype(f32)
        both = jnp.where(by_core, jnp.stack([keep, theirs]), jnp.stack([theirs, keep]))
        return [both[:, i * size : (i + 1) * size] for i in range(parts)]

    me = (chip if near else 0 * chip).astype(jnp.int32)[None]
    core_index, place_index = core.astype(jnp.int32)[None], place.astype(jnp.int32)[None]
    kinds = [w_gate.T, w_up.T, w_down]
    depth = w_down.shape[0] // 2
    cut = -(-depth // 32 // 2) * 32
    if near:
        keep, give = square_split_call(
            core_index, bucket, w_query, w_key, w_value, w_out, attn_gain, ffn_gain
        )
    else:
        extra = jnp.concatenate(
            [
                attn_gain[None],
                ffn_gain[None],
                jnp.pad(bucket.astype(bf16), (0, own_width - bundle))[None],
                jnp.zeros((13, own_width), bf16),
            ]
        )
        keep, give = split_far(
            two(w_query.T), two(w_key.T), two(w_value.T), two(w_out), jnp.stack([extra, extra])
        )
        halves = [two(kind) for kind in kinds]
        ffn_keep, ffn_give = split_far(
            *[half[:, :cut] for half in halves], *[half[:, cut:] for half in halves]
        )
    square = ordered(keep, to_core(give), 1)

    square_z = spread(square)
    own_inputs, own_cotangent, kinds, square = stage((inputs, cotangent, kinds, square))
    if near:
        ffn_keep, ffn_give = ffn_split_call(core_index, cut, *kinds)
    x_blocks = blocks_for(group_start(own_inputs))
    cot_blocks = blocks_for(group_start(own_cotangent))
    ffn_theirs = to_core(ffn_give)
    ffn_one = ordered(ffn_keep[: 3 * cut], ffn_theirs[: 3 * cut], 1)
    ffn_two = ordered(ffn_keep[3 * cut :], ffn_theirs[3 * cut :], 1)
    flags = square[4 * 128 + 2].reshape(2, own_width)[:, :bundle].reshape(-1)
    flag = pick(flags.astype(jnp.int32), place, 0)[None]

    square_z, x_blocks, cot_blocks, ffn_one, ffn_two, flag = stage(
        (square_z, x_blocks, cot_blocks, ffn_one, ffn_two, flag)
    )
    square_z = jnp.stack(square_z)
    square_first = chips_first(square_z)
    x_moved = across(x_blocks)

    square_first, x_moved, ffn_one = stage((square_first, x_moved, ffn_one))
    x_own = jnp.stack(x_moved)
    x_other = to_core(x_own)
    square_second = chips_second(*square_first) if near else ()
    one_z = spread(ffn_one, x_other)
    x_rows, hidden, rms, gains, square_full, q, k, v = qkv_call(
        me,
        core_index,
        place_index,
        x_own,
        x_other,
        chips_pieces(square_z, square_first, square_second),
    )

    q, one_z, cot_blocks = stage((q, one_z, cot_blocks))
    one_z = jnp.stack(one_z)
    one_first = chips_first(one_z)
    cot_moved = across(cot_blocks)
    attended, probs = attend_call(flag, q, k, v)

    attended, one_first, cot_moved, ffn_two = stage((attended, one_first, cot_moved, ffn_two))
    one_second = chips_second(*one_first) if near else ()
    branch = branch_call(me, attended, square_full)
    cot_own = jnp.stack(cot_moved)
    two_z = spread(ffn_two, branch)
    middle_place = narrow // 2
    branch, cot_own, one_second, two_near = stage(
        (branch, cot_own, one_second, two_z[:middle_place] + two_z[middle_place + 1 :])
    )
    two_z = two_near[:middle_place] + [two_z[middle_place]] + two_near[middle_place:]
    branch_other, cot_other = to_core(branch), to_core(cot_own)
    middle, normed, cot_rows = middle_call(
        core_index, place_index, x_rows, branch, branch_other, gains, cot_own, cot_other
    )

    normed, two_z = stage((normed, two_z))
    two_z = jnp.stack(two_z)
    two_first = chips_first(two_z)
    part_result, part_d_normed, *one_grads = ffn_call(
        me, core_index, narrow, normed, cot_rows, chips_pieces(one_z, one_first, one_second)
    )

    part_result, part_d_normed, one_grads, two_first = stage(
        (part_result, part_d_normed, one_grads, two_first)
    )
    two_second = chips_second(*two_first) if near else ()

    part_result, part_d_normed, one_grads, two_second = stage(
        (part_result, part_d_normed, one_grads, two_second)
    )
    one_got = sum_first(one_grads) if near else ()
    result, d_normed, *two_grads, result_give = ffn_call(
        me,
        core_index,
        narrow,
        normed,
        cot_rows,
        chips_pieces(two_z, two_first, two_second),
        part_result,
        part_d_normed,
    )

    result_give, d_normed, one_got, two_grads = stage((result_give, d_normed, one_got, two_grads))
    by_rows = (narrow, 2, tile, width)
    d_normed_other, result_other = to_core(d_normed), to_core(result_give)
    one_last = sum_second(sum_ready(one_grads, one_got)) if near else ()
    d_middle, d_branch, d_att, ffn_gain_grad, out_rows = turn_call(
        me,
        core_index,
        middle,
        d_normed,
        d_normed_other,
        cot_rows,
        gains,
        square_full,
        result.reshape(by_rows),
        result_other,
    )
    out_moved = across(blocks_for(out_rows))

    d_att, one_last, two_grads = stage((d_att, one_last, two_grads))
    two_got = sum_first(two_grads) if near else ()
    pairs = d_att.shape[1] // 256
    lefts_one = attend_back_call(0, pairs, flag, q, k, v, attended, d_att, probs)

    lefts_one, d_att, one_grads, one_got, one_last, two_grads, two_got = stage(
        (lefts_one, d_att, one_grads, one_got, one_last, two_grads, two_got), near_of(out_moved)
    )
    two_last = sum_second(sum_ready(two_grads, two_got)) if near else ()
    one_own, one_sent = sum_done(one_grads, one_got, one_last) if near else sum_far(one_grads)
    lefts_two = attend_back_call(pairs, pairs, flag, q, k, v, attended, d_att, probs)
    one_near = across_near(one_sent, -1)

    lefts_two, two_last, out_moved, one_near, one_far = stage(
        (lefts_two, two_last, out_moved, one_near, one_sent[far_place])
    )
    one_places = joined(None, one_near, across_far(one_far, -1))
    two_own, two_sent = sum_done(two_grads, two_got, two_last) if near else sum_far(two_grads)
    two_sent[0] = two_own
    two_places = across(two_sent, (), (), -1)
    lefts = [left for both in zip(lefts_one, lefts_two) for left in both]
    d_hidden, d_hidden_give, *square_grads = square_call(
        me, core_index, lefts, attended, hidden, d_branch, square_full, x_rows, rms, 0.5 * ffn_gain_grad
    )

    d_hidden_give, square_grads, out_moved = stage(
        (d_hidden_give, square_grads, out_moved), near_of(two_places), one_places[far_place]
    )
    square_got = sum_first(square_grads) if near else ()
    d_hidden_other = to_core(d_hidden_give)
    input_blocks = blocks_for(
        input_call(
            core_index, x_rows, d_middle, d_hidden.reshape(by_rows), d_hidden_other, gains
        )
    )
    input_near = across_near(input_blocks)
    outputs = group_back(out_moved)
    one_keep, one_swap = swap_ready(one_own, one_places)

    square_got, one_swap, input_near, input_far, two_places = stage(
        (square_got, one_swap, input_near, input_blocks[far_place], two_places)
    )
    input_moved = joined(input_blocks[0], input_near, across_far(input_far))
    square_last = sum_second(sum_ready(square_grads, square_got)) if near else ()
    one_theirs = to_core(one_swap)
    two_keep, two_swap = swap_ready(two_own, two_places)

    square_last, input_moved, two_swap = stage((square_last, input_moved, two_swap))
    square_own, square_sent = (
        sum_done(square_grads, square_got, square_last) if near else sum_far(square_grads)
    )
    square_places = across(square_sent, (), (), -1)
    two_theirs = to_core(two_swap)
    input_grad = group_back(input_moved).astype(f32)
    one_parts = finish(one_keep, one_theirs, 3, cut)
    two_parts = finish(two_keep, two_theirs, 3, depth - cut)
    g_gate, g_up, g_down = [
        jnp.concatenate(parts, axis=1).reshape(2 * depth, own_width)
        for parts in zip(one_parts, two_parts)
    ]
    g_gate, g_up = g_gate.T, g_up.T
    square_places, outputs, input_grad, g_gate, g_up, g_down = stage(
        (square_places, outputs, input_grad, g_gate, g_up, g_down)
    )
    square_keep, square_swap = swap_ready(square_own, square_places)
    square_theirs = to_core(square_swap)
    g_query, g_key, g_value, g_out = [
        part.reshape(-1, own_width) for part in finish(square_keep, square_theirs, 4, 128)
    ]
    gain_own = square_keep[4 * 128 :] + square_theirs[4 * 128 :].astype(f32)
    return (
        outputs,
        input_grad,
        gain_own[0],
        g_query.T,
        g_key.T,
        g_value.T,
        g_out,
        gain_own[1],
        g_gate,
        g_up,
        g_down,
    )


def solution(mesh):
    rows = P("dp", "narrow", None)
    tall, flat = P("dp", "narrow"), P("narrow", "dp")
    return jax.shard_map(
        per_device,
        mesh=mesh,
        in_specs=(rows, P("dp"), P("dp"), tall, tall, tall, flat, P("dp"), tall, tall, flat, rows),
        out_specs=(rows, rows, P("dp"), tall, tall, tall, flat, P("dp"), tall, tall, flat),
        check_vma=False,
    )
```

```python
import functools

import jax
import jax.numpy as jnp
from jax import lax
from jax.experimental import pallas as pl
from jax.experimental.pallas import tpu as pltpu
from jax.sharding import PartitionSpec as P

HEAD = 64
SHORT = 384
EPS = 1e-06
BLOCKS = 4
f32 = jnp.float32
bf16 = jnp.bfloat16


def dot_nn(left, right):
    return jnp.dot(left, right, preferred_element_type=f32)


def dot_nt(left, right):
    return lax.dot_general(left, right, (((1,), (1,)), ((), ())), preferred_element_type=f32)


def call(kernel, grid, prefetch, in_specs, out_specs, out_shape, scratch, flops, moved, vmem):
    return pl.pallas_call(
        kernel,
        grid_spec=pltpu.PrefetchScalarGridSpec(
            num_scalar_prefetch=prefetch,
            grid=grid,
            in_specs=in_specs,
            out_specs=out_specs,
            scratch_shapes=scratch,
        ),
        out_shape=out_shape,
        compiler_params=pltpu.CompilerParams(vmem_limit_bytes=vmem << 20),
        cost_estimate=pl.CostEstimate(flops=flops, bytes_accessed=moved, transcendentals=0),
    )


def shaped(shape, dtype):
    return jax.ShapeDtypeStruct(shape, dtype)


def rms_of(rows):
    return lax.rsqrt(jnp.mean(rows * rows, axis=-1, keepdims=True) + EPS)


def store_grad(refs, step, grad, first):
    x_keep, x_send, y_keep, y_send = refs
    half, rows = grad.shape[0] // 2, slice(first, first + grad.shape[1])
    (x_send if step % 2 else x_keep)[step // 2, :, rows] = grad[:half]
    (y_send if step // 2 else y_keep)[step % 2, :, rows] = grad[half:]


def grad_shapes(pieces, rows, wide):
    return [shaped((2, pieces // 2, rows, wide), bf16)] * 4


def square_split_kernel(
    core_ref, bucket_ref, q_ref, k_ref, v_ref, o_ref, attn_ref, ffn_ref, keep_ref, give_ref
):
    halves = [ref[...].T for ref in (q_ref, k_ref, v_ref)] + [o_ref[...]]
    shape = (16, keep_ref.shape[1])
    row, lane = (lax.broadcasted_iota(jnp.int32, shape, axis) for axis in range(2))
    flags = jnp.zeros(shape, f32)
    for i in range(bucket_ref.shape[0]):
        flags = jnp.where(lane == i, bucket_ref[i].astype(f32), flags)
    flags = jnp.where(row == 2, flags, 0.0)
    flags = jnp.where(row == 1, ffn_ref[...].astype(f32), flags)
    extra = jnp.where(row == 0, attn_ref[...].astype(f32), flags).astype(bf16)

    def store(low_ref, high_ref):
        start = 0
        for half in halves:
            count = half.shape[0] // 2
            low_ref[start : start + count] = half[:count]
            high_ref[start : start + count] = half[count:]
            start += count
        low_ref[start:] = extra
        high_ref[start:] = extra

    @pl.when(core_ref[0] == 0)
    def _():
        store(keep_ref, give_ref)

    @pl.when(core_ref[0] != 0)
    def _():
        store(give_ref, keep_ref)


def square_split_call(core, bucket, q, k, v, o, attn, ffn):
    rows, cols = q.shape[1] // 2 * 4 + 16, o.shape[1]
    whole = pl.BlockSpec(memory_space=pltpu.VMEM)
    return call(
        square_split_kernel,
        (),
        2,
        [whole] * 6,
        [whole] * 2,
        [shaped((rows, cols), bf16)] * 2,
        [],
        0,
        1 << 20,
        16,
    )(core, bucket, q, k, v, o, attn[None], ffn[None])


def ffn_split_kernel(cut, core_ref, *refs):
    parts, (keep_ref, give_ref) = refs[:3], refs[3:]

    def store(low_ref, high_ref):
        start = 0
        half = parts[0].shape[0] // 2
        for first, last in ((0, cut), (cut, half)):
            for part in parts:
                count = last - first
                low_ref[start : start + count] = part[first:last]
                high_ref[start : start + count] = part[half + first : half + last]
                start += count

    @pl.when(core_ref[0] == 0)
    def _():
        store(keep_ref, give_ref)

    @pl.when(core_ref[0] != 0)
    def _():
        store(give_ref, keep_ref)


def ffn_split_call(core, cut, gate, up, down):
    rows, cols = gate.shape[0] // 2 * 3, gate.shape[1]
    whole = pl.BlockSpec(memory_space=pltpu.VMEM)
    return call(
        functools.partial(ffn_split_kernel, cut),
        (),
        1,
        [whole] * 3,
        [whole] * 2,
        [shaped((rows, cols), bf16)] * 2,
        [],
        0,
        1 << 20,
        16,
    )(core, gate, up, down)


def join_rows(core_ref, own_ref, other_ref, out_ref):
    count = own_ref.shape[1]

    @pl.when(core_ref[0] == 0)
    def _():
        out_ref[:count] = own_ref[0]
        out_ref[count:] = other_ref[0]

    @pl.when(core_ref[0] != 0)
    def _():
        out_ref[:count] = other_ref[0]
        out_ref[count:] = own_ref[0]


def qkv_kernel(
    me_ref, core_ref, place_ref, own_ref, other_ref, w0, w1, w2, w3, w4, x_ref, hidden_ref, rms_ref, gains_ref, w_ref, q_ref, k_ref, v_ref
):
    @pl.when(pl.program_id(0) == 0)
    def _():
        for step, piece in enumerate((w0, w1, w2)):
            w_ref[step] = piece[...]
        w_ref[3, : w3.shape[0]] = w3[...]
        w_ref[3, w3.shape[0] :] = w4[...]

    join_rows(core_ref, own_ref, other_ref, x_ref)
    rows = x_ref[...].astype(f32)
    rms = rms_of(rows)
    rms_ref[...] = jnp.broadcast_to(rms, rms_ref.shape)
    wide = w_ref.shape[3]
    half = w_ref.shape[1] * 128
    for step in range(BLOCKS):
        columns = pl.ds(pl.multiple_of((me_ref[0] ^ step) * wide, wide), wide)
        gains = w_ref[step, 0, 4 * 128 :, :].astype(f32)
        gains_ref[:, columns] = gains[:8]
        hidden_ref[:, columns] = (x_ref[:, columns].astype(f32) * rms * gains[:1]).astype(bf16)
    for part, ref in enumerate((q_ref, k_ref, v_ref)):
        total = None
        for step in range(BLOCKS):
            start = pl.multiple_of((me_ref[0] ^ step) * wide, wide)
            weight = w_ref[step, :, part * 128 : (part + 1) * 128, :].reshape(half, wide)
            piece = dot_nt(hidden_ref[:, pl.ds(start, wide)], weight)
            total = piece if total is None else total + piece
        if part == 0:
            total = total * (HEAD**-0.5)
        ref[...] = total.astype(bf16)


def qkv_call(me, core, place, own, other, weights):
    places, half_tile, width = own.shape
    half = weights[0].shape[0] * 128
    tile, count = 2 * half_tile, 2 * half_tile * places
    all_shape = (BLOCKS,) + weights[0].shape
    row_spec = pl.BlockSpec((tile, width), lambda i, me, core, place: (i, 0))
    half_spec = pl.BlockSpec((tile, half), lambda i, me, core, place: (i, 0))
    part_spec = pl.BlockSpec(
        (1, half_tile, width), lambda i, me, core, place: ((place[0] + places - i) % places, 0, 0)
    )
    return call(
        qkv_kernel,
        (places,),
        3,
        [
            part_spec,
            part_spec,
        ]
        + [pl.BlockSpec(w.shape, lambda i, me, core, place: (0, 0, 0)) for w in weights],
        [
            row_spec,
            row_spec,
            pl.BlockSpec((tile, 128), lambda i, me, core, place: (i, 0)),
            pl.BlockSpec((8, width), lambda i, me, core, place: (0, 0)),
            pl.BlockSpec(all_shape, lambda i, me, core, place: (0, 0, 0, 0)),
            half_spec,
            half_spec,
            half_spec,
        ],
        [shaped((count, width), bf16)] * 2
        + [shaped((count, 128), f32), shaped((8, width), f32), shaped(all_shape, bf16)]
        + [shaped((count, half), bf16)] * 3,
        [],
        2 * count * width * half * 3,
        12 << 20,
        40,
    )(me, core, place, own, other, *weights)


def two_heads(rows):
    low = lax.broadcasted_iota(jnp.int32, rows.shape, 1) < HEAD
    zero = jnp.zeros_like(rows)
    return jnp.concatenate([jnp.where(low, rows, zero), jnp.where(low, zero, rows)], axis=0)


def one_pair(both):
    half = both.shape[1] // 2
    return jnp.concatenate([both[:HEAD, :half], both[HEAD:, half:]], axis=0)


def attend_kernel(flag_ref, q_ref, k_ref, v_ref, out_ref, probs_ref, v_turned):
    block = pl.program_id(1)

    @pl.when(block == 0)
    def _():
        v_turned[...] = v_ref[...].T

    queries = two_heads(q_ref[...])

    def attend(keys, values):
        scores = dot_nt(keys, queries)
        expo = jnp.exp(scores - jnp.max(scores, axis=0, keepdims=True))
        probs = (expo * (1.0 / jnp.sum(expo, axis=0, keepdims=True))).astype(bf16)
        probs_ref[0, 0, : keys.shape[0], :] = probs
        out_ref[...] = one_pair(dot_nn(values, probs)).T.astype(bf16)

    @pl.when(flag_ref[0] == 1)
    def _():
        attend(k_ref[...], v_turned[...])

    @pl.when(flag_ref[0] != 1)
    def _():
        start = pl.multiple_of(block * SHORT, SHORT)
        attend(k_ref[pl.ds(start, SHORT), :], v_turned[:, pl.ds(start, SHORT)])


def attend_call(flag, q, k, v):
    count, half = q.shape
    pairs, blocks = half // 128, count // SHORT
    some = pl.BlockSpec((SHORT, 128), lambda j, i, flag: (i, j))
    every = pl.BlockSpec((count, 128), lambda j, i, flag: (0, j))
    return call(
        attend_kernel,
        (pairs, blocks),
        1,
        [some, every, every],
        [some, pl.BlockSpec((1, 1, count, 2 * SHORT), lambda j, i, flag: (j, i, 0, 0))],
        [shaped(q.shape, bf16), shaped((pairs, blocks, count, 2 * SHORT), bf16)],
        [pltpu.VMEM((128, count), bf16)],
        4 * 4 * count * count * half,
        28 << 20,
        32,
    )(flag, q, k, v)


def branch_kernel(me_ref, att_ref, w_ref, out_ref):
    wide = w_ref.shape[3]
    for step in range(BLOCKS):
        start = pl.multiple_of((me_ref[0] ^ step) * wide, wide)
        weight = w_ref[step].reshape(att_ref.shape[1], wide)
        out_ref[:, pl.ds(start, wide)] = dot_nn(att_ref[...], weight).astype(bf16)


def branch_call(me, attended, weights):
    count, half = attended.shape
    width = weights.shape[0] * weights.shape[3]
    tile = count // 4
    block = weights.shape[:2] + (128,) + weights.shape[3:]
    return call(
        branch_kernel,
        (count // tile,),
        1,
        [
            pl.BlockSpec((tile, half), lambda i, me: (i, 0)),
            pl.BlockSpec(block, lambda i, me: (0, 0, 3, 0)),
        ],
        pl.BlockSpec((tile, width), lambda i, me: (i, 0)),
        shaped((count, width), bf16),
        [],
        2 * count * width * half,
        5 << 20,
        24,
    )(me, attended, weights)


def middle_kernel(
    core_ref, place_ref, x_ref, one_ref, two_ref, gain_ref, own_ref, other_ref, middle_ref, normed_ref, cot_ref
):
    middle = x_ref[...].astype(f32) + (one_ref[...].astype(f32) + two_ref[...].astype(f32))
    middle_ref[...] = middle
    normed_ref[...] = (middle * rms_of(middle) * gain_ref[1:2, :]).astype(bf16)
    join_rows(core_ref, own_ref, other_ref, cot_ref)


def middle_call(core, place, rows, one, two, gain, own, other):
    count, width = rows.shape
    places, half_tile = own.shape[:2]
    spec = pl.BlockSpec((2 * half_tile, width), lambda i, core, place: (i, 0))
    part_spec = pl.BlockSpec(
        (1, half_tile, width), lambda i, core, place: ((place[0] + places - i) % places, 0, 0)
    )
    return call(
        middle_kernel,
        (places,),
        2,
        [spec] * 3
        + [pl.BlockSpec((8, width), lambda i, core, place: (0, 0)), part_spec, part_spec],
        [spec] * 3,
        [shaped(rows.shape, f32), shaped(rows.shape, bf16), shaped(rows.shape, bf16)],
        [],
        0,
        14 << 20,
        32,
    )(core, place, rows, one, two, gain, own, other)


def ffn_kernel(given, prior, me_ref, core_ref, normed_ref, d_out_ref, *refs):
    pieces_of, refs = refs[:given], refs[given:]
    before = refs[:2] if prior else None
    refs = refs[2 if prior else 0 :]
    result_ref, d_normed_ref = refs[:2]
    grad_refs, refs = refs[2:6], refs[6:]
    give_ref = refs[0] if prior else None
    weights, inner_t, gate_t, up_t = refs[1 if prior else 0 :]
    pieces, rows_all, wide = pieces_of[0].shape
    parts, kinds, depth = BLOCKS, 3, rows_all // 3
    units = pieces * depth
    tile = SHORT

    def columns(step):
        return pl.ds(pl.multiple_of((me_ref[0] ^ step) * wide, wide), wide)

    for kind in range(kinds):
        rows = slice(kind * depth, (kind + 1) * depth)
        for step in range(parts):
            start = 0
            for piece in pieces_of[step:] if step == parts - 1 else pieces_of[step : step + 1]:
                count = piece.shape[0] * depth
                value = piece[:, rows, :].reshape(count, wide)
                weights[kind, start : start + count, columns(step)] = value
                start += count

    def rows_step(index, carry):
        rows = pl.ds(pl.multiple_of(index * tile, tile), tile)
        normed = normed_ref[rows, :]
        gate, up = dot_nt(normed, weights[0]), dot_nt(normed, weights[1])
        d_inner = dot_nt(d_out_ref[rows, :], weights[2])
        square = gate * gate
        bent = jnp.tanh(gate * (0.7978845608 + 0.7978845608 * 0.044715 * square))
        half = 0.5 + 0.5 * bent
        gelu = gate * half
        slope = half + gate * (0.5 - 0.5 * bent * bent) * (
            0.7978845608 + 0.7978845608 * 3 * 0.044715 * square
        )
        inner = (gelu * up).astype(bf16)
        d_gate = (d_inner * up * slope).astype(bf16)
        d_up = (d_inner * gelu).astype(bf16)
        inner_t[:, rows] = inner.T
        gate_t[:, rows] = d_gate.T
        up_t[:, rows] = d_up.T
        forward = dot_nn(inner, weights[2])
        backward = dot_nn(d_gate, weights[0]) + dot_nn(d_up, weights[1])
        if prior:
            forward += before[0][rows, :].astype(f32)
            backward += before[1][rows, :].astype(f32)
        result_ref[rows, :] = forward.astype(bf16)
        d_normed_ref[rows, :] = backward.astype(bf16)
        return carry

    lax.fori_loop(0, normed_ref.shape[0] // tile, rows_step, 0)
    for step in range(parts):
        here, there = normed_ref[:, columns(step)], d_out_ref[:, columns(step)]
        for kind, (left, right) in enumerate(((gate_t, here), (up_t, here), (inner_t, there))):
            grad = dot_nn(left[...], right).astype(bf16)
            store_grad(grad_refs, step, grad.reshape(pieces, depth, wide), kind * depth)
    if prior:
        give_rows(core_ref, result_ref, give_ref)


def give_rows(core_ref, all_ref, give_ref):
    places, count = give_ref.shape[:2]
    for place in range(places):
        start = (2 * place + 1 - core_ref[0]) * count
        give_ref[place] = all_ref[pl.ds(pl.multiple_of(start, count), count), :]


def ffn_call(me, core, places, normed, d_out, weights, *before):
    count, width = normed.shape
    pieces, rows_all, wide = weights[0].shape
    units = pieces * rows_all // 3
    whole = pl.BlockSpec(memory_space=pltpu.VMEM)
    return call(
        functools.partial(ffn_kernel, len(weights), bool(before)),
        (),
        2,
        [whole] * (2 + len(weights) + len(before)),
        [whole] * (7 if before else 6),
        [shaped(normed.shape, bf16)] * 2
        + grad_shapes(pieces, rows_all, wide)
        + ([shaped((places, count // places // 2, width), bf16)] if before else []),
        [pltpu.VMEM((3, units, width), bf16)] + [pltpu.VMEM((units, count), bf16)] * 3,
        18 * count * width * units,
        20 << 20,
        48,
    )(me, core, normed, d_out, *weights, *before)


def turn_kernel(
    me_ref,
    core_ref,
    middle_ref,
    one_ref,
    two_ref,
    cot_ref,
    gain_ref,
    w_ref,
    own_ref,
    other_ref,
    d_middle_ref,
    d_branch_ref,
    d_att_ref,
    gain_grad_ref,
    out_ref,
):
    middle = middle_ref[...]
    rms = rms_of(middle)
    scaled = middle * rms
    d_normed = one_ref[...].astype(f32) + two_ref[...].astype(f32)
    pulled = d_normed * gain_ref[1:2, :]
    d_middle = cot_ref[...].astype(f32) + rms * (
        pulled - scaled * jnp.mean(pulled * scaled, axis=-1, keepdims=True)
    )
    d_branch_ref[...] = d_middle.astype(bf16)
    count = out_ref.shape[1]

    @pl.when(core_ref[0] == 0)
    def _():
        d_middle_ref[0] = d_middle[:count]

    @pl.when(core_ref[0] != 0)
    def _():
        d_middle_ref[0] = d_middle[count:]

    rows = pl.ds(pl.multiple_of(core_ref[0] * count, count), count)
    out_ref[0] = (
        middle_ref[rows, :] + (own_ref[0, 0].astype(f32) + other_ref[0].astype(f32))
    ).astype(bf16)

    @pl.when(pl.program_id(0) == 0)
    def _():
        gain_grad_ref[...] = jnp.zeros_like(gain_grad_ref)

    gain_grad_ref[...] += jnp.sum(d_normed * scaled, axis=0, keepdims=True)
    wide = w_ref.shape[3]
    total = None
    for step in range(BLOCKS):
        start = pl.multiple_of((me_ref[0] ^ step) * wide, wide)
        piece = dot_nt(d_branch_ref[:, pl.ds(start, wide)], w_ref[step].reshape(d_att_ref.shape[1], wide))
        total = piece if total is None else total + piece
    d_att_ref[...] = total.astype(bf16)


def turn_call(me, core, middle, one, two, cot, gain, weights, own, other):
    count, width = middle.shape
    half = weights.shape[1] * 128
    places, _, half_tile, _ = own.shape
    tile = 2 * half_tile
    spec = pl.BlockSpec((tile, width), lambda i, me, core: (i, 0))
    line = pl.BlockSpec((1, width), lambda i, me, core: (0, 0))
    gain_spec = pl.BlockSpec((8, width), lambda i, me, core: (0, 0))
    plain = pl.BlockSpec((1, half_tile, width), lambda i, me, core: (i, 0, 0))
    block = weights.shape[:2] + (128,) + weights.shape[3:]
    return call(
        turn_kernel,
        (places,),
        2,
        [spec, spec, spec, spec, gain_spec]
        + [pl.BlockSpec(block, lambda i, me, core: (0, 0, 3, 0))]
        + [pl.BlockSpec((1, 1, half_tile, width), lambda i, me, core: (i, core[0], 0, 0)), plain],
        [plain, spec, pl.BlockSpec((tile, half), lambda i, me, core: (i, 0)), line, plain],
        [
            shaped((places, half_tile, width), f32),
            shaped(middle.shape, bf16),
            shaped((count, half), bf16),
            shaped((1, width), f32),
            shaped((places, half_tile, width), bf16),
        ],
        [],
        2 * count * width * half,
        22 << 20,
        40,
    )(me, core, middle, one, two, cot, gain, weights, own, other)


def attend_back_kernel(
    flag_ref, q_ref, k_ref, v_ref, out_ref, d_out_ref, probs_ref, dq_ref, dk_ref, dv_ref, k_turned, dk_sum, dv_sum
):
    block, blocks = pl.program_id(1), pl.num_programs(1)

    @pl.when(block == 0)
    def _():
        k_turned[...] = k_ref[...].T

    queries, grads = two_heads(q_ref[...]), two_heads(d_out_ref[...])
    turned = (d_out_ref[...].astype(f32) * out_ref[...].astype(f32)).T
    delta = jnp.concatenate(
        [
            jnp.sum(turned[:HEAD], axis=0, keepdims=True),
            jnp.sum(turned[HEAD:], axis=0, keepdims=True),
        ],
        axis=1,
    )

    def back(values, keys_turned):
        probs = probs_ref[0, 0, : values.shape[0], :]
        d_probs = dot_nt(values, grads)
        d_scores = (probs.astype(f32) * (d_probs - delta)).astype(bf16)
        d_query = one_pair(dot_nn(keys_turned, d_scores)).T * (HEAD**-0.5)
        dq_ref[...] = d_query.astype(bf16)
        return dot_nn(d_scores, queries), dot_nn(probs, grads)

    @pl.when(flag_ref[0] == 1)
    def _():
        d_key, d_value = back(v_ref[...], k_turned[...])

        @pl.when(block == 0)
        def _():
            dk_sum[...] = d_key
            dv_sum[...] = d_value

        @pl.when(block > 0)
        def _():
            dk_sum[...] += d_key
            dv_sum[...] += d_value

    @pl.when(flag_ref[0] != 1)
    def _():
        rows = pl.ds(pl.multiple_of(block * SHORT, SHORT), SHORT)
        d_key, d_value = back(v_ref[rows, :], k_turned[:, rows])
        dk_sum[rows, :] = d_key
        dv_sum[rows, :] = d_value

    @pl.when(block == blocks - 1)
    def _():
        dk_ref[...] = dk_sum[...].astype(bf16)
        dv_ref[...] = dv_sum[...].astype(bf16)


def attend_back_call(first, pairs, flag, q, k, v, out, d_out, probs):
    count, half = q.shape
    blocks = count // SHORT
    some = pl.BlockSpec((SHORT, 128), lambda j, i, flag: (i, j + first))
    every = pl.BlockSpec((count, 128), lambda j, i, flag: (0, j + first))
    some_out = pl.BlockSpec((SHORT, 128), lambda j, i, flag: (i, j))
    every_out = pl.BlockSpec((count, 128), lambda j, i, flag: (0, j))
    return call(
        attend_back_kernel,
        (pairs, blocks),
        1,
        [
            some,
            every,
            every,
            some,
            some,
            pl.BlockSpec((1, 1, count, 2 * SHORT), lambda j, i, flag: (j + first, i, 0, 0)),
        ],
        [some_out, every_out, every_out],
        [shaped((count, pairs * 128), bf16)] * 3,
        [pltpu.VMEM((128, count), bf16)] + [pltpu.VMEM((count, 128), f32)] * 2,
        4 * 8 * count * count * pairs * 128,
        16 << 20,
        32,
    )(flag, q, k, v, out, d_out, probs)


def square_kernel(
    me_ref,
    core_ref,
    dq_one,
    dq_two,
    dk_one,
    dk_two,
    dv_one,
    dv_two,
    att_ref,
    hidden_ref,
    d_branch_ref,
    w_ref,
    x_ref,
    rms_ref,
    line_ref,
    d_hidden_ref,
    give_ref,
    *refs,
):
    grad_refs, turned = refs[:4], refs[4]
    pieces, wide = w_ref.shape[1], w_ref.shape[3]
    lefts = (dq_one, dq_two, dk_one, dk_two, dv_one, dv_two)
    start = 0
    for ref in (*lefts, att_ref):
        stop = start + ref.shape[1]
        turned[start:stop, :] = ref[...].T
        start = stop
    half = att_ref.shape[1]
    for step in range(BLOCKS):
        columns = pl.ds(pl.multiple_of((me_ref[0] ^ step) * wide, wide), wide)
        for part in range(4):
            right = d_branch_ref if part == 3 else hidden_ref
            grad = dot_nn(turned[part * half : (part + 1) * half, :], right[:, columns])
            grad = grad.astype(bf16).reshape(pieces, 128, wide)
            store_grad(grad_refs, step, grad, part * 128)
        total = None
        for index, ref in enumerate(lefts):
            part, side = index // 2, index % 2 * pieces // 2
            rows = slice(part * 128, (part + 1) * 128)
            weight = w_ref[step, side : side + pieces // 2, rows, :].reshape(half // 2, wide)
            piece = dot_nn(ref[...], weight)
            total = piece if total is None else total + piece
        d_hidden_ref[:, columns] = total.astype(bf16)
        scaled = x_ref[:, columns].astype(f32) * rms_ref[:, :1]
        attn = jnp.sum(total * scaled, axis=0, keepdims=True)
        lines = jnp.concatenate(
            [attn, line_ref[:, columns], jnp.zeros((14, wide), f32)], axis=0
        ).astype(bf16)
        store_grad(grad_refs, step, jnp.broadcast_to(lines[None], (pieces, 16, wide)), 4 * 128)
    give_rows(core_ref, d_hidden_ref, give_ref)


def square_call(me, core, lefts, attended, hidden, d_branch, weights, x_rows, rms, line):
    count, half = attended.shape
    width = hidden.shape[1]
    pieces, depth, wide = weights.shape[1:]
    whole = pl.BlockSpec(memory_space=pltpu.VMEM)
    return call(
        square_kernel,
        (),
        2,
        [whole] * (len(lefts) + 7),
        [whole] * 6,
        [shaped(hidden.shape, bf16), shaped((pieces, count // pieces // 2, width), bf16)]
        + grad_shapes(pieces, depth, wide),
        [pltpu.VMEM((4 * half, count), bf16)],
        14 * count * width * half,
        24 << 20,
        52,
    )(me, core, *lefts, attended, hidden, d_branch, weights, x_rows, rms, line)


def input_kernel(core_ref, x_ref, d_middle_ref, own_ref, other_ref, gain_ref, out_ref):
    rows = x_ref[0, 0].astype(f32)
    rms = rms_of(rows)
    scaled = rows * rms
    d_hidden = own_ref[0, 0].astype(f32) + other_ref[0].astype(f32)
    pulled = d_hidden * gain_ref[:1, :]
    out_ref[0] = (
        d_middle_ref[0]
        + rms * (pulled - scaled * jnp.mean(pulled * scaled, axis=-1, keepdims=True))
    ).astype(bf16)


def input_call(core, rows, d_middle, own, other, gains):
    slots, halves, tile, width = own.shape
    mine = pl.BlockSpec((1, 1, tile, width), lambda i, core: (i, core[0], 0, 0))
    plain = pl.BlockSpec((1, tile, width), lambda i, core: (i, 0, 0))
    return call(
        input_kernel,
        (slots,),
        1,
        [mine, plain, mine, plain, pl.BlockSpec((8, width), lambda i, core: (0, 0))],
        plain,
        shaped((slots, tile, width), bf16),
        [],
        0,
        8 << 20,
        16,
    )(core, rows.reshape(own.shape), d_middle, own, other, gains)


def per_device(
    inputs,
    bucket,
    attn_gain,
    w_query,
    w_key,
    w_value,
    w_out,
    ffn_gain,
    w_gate,
    w_up,
    w_down,
    cotangent,
):
    dp, narrow = lax.axis_size("dp"), lax.axis_size("narrow")
    chips = dp // 2
    core, chip = lax.axis_index("dp") % 2, lax.axis_index("dp") // 2
    place = lax.axis_index("narrow")
    same_core = [[2 * m + c for m in range(chips)] for c in range(2)]
    by_core = core == 0
    bundle, row_count, width = inputs.shape
    tile = row_count // 2
    own_width = w_query.shape[0]
    wide = width // BLOCKS

    def to_core(value):
        return lax.ppermute(value, "dp", [(i, i ^ 1) for i in range(dp)])

    def to_chip(value, flip):
        return lax.ppermute(value, "dp", [(i, i ^ (2 * flip)) for i in range(dp)])

    def along(value, shift):
        return lax.ppermute(
            value, "narrow", [(i, (i + shift) % narrow) for i in range(narrow)]
        )

    def stage(values, *done):
        return lax.optimization_barrier((values, done))[0]

    def ordered(mine, theirs, axis):
        join = functools.partial(jnp.concatenate, axis=axis)
        return jnp.where(by_core, join([mine, theirs]), join([theirs, mine]))

    def pick(value, index, axis):
        return lax.dynamic_index_in_dim(value, index, axis, keepdims=False)

    def mine_of(value, axis):
        low, high = (lax.index_in_dim(value, i, axis, keepdims=False) for i in range(2))
        return jnp.where(by_core, low, high), jnp.where(by_core, high, low)

    def turn(k):
        return lax.rem(place + (k + narrow), narrow)

    def blocks_for(value):
        return [pick(value, turn(k), 0) for k in range(narrow)]

    far_place = narrow // 2

    def across(blocks, near_late=(), far_late=(), sign=1):
        moved = [blocks[0]]
        for k in range(1, narrow):
            late = far_late if k == far_place else near_late
            moved.append(along(stage(blocks[k], *late) if late else blocks[k], sign * k))
        return moved

    def across_near(blocks, sign=1):
        return [along(blocks[k], sign * k) for k in range(1, narrow) if k != far_place]

    def across_far(block, sign=1):
        return along(block, sign * far_place)

    def joined(own, near, far):
        return [own] + near[: far_place - 1] + [far] + near[far_place - 1 :]

    def near_of(moved):
        return [moved[k] for k in range(1, narrow) if k != far_place]

    def in_order(moved):
        stacked = jnp.stack(moved)
        return jnp.stack([pick(stacked, turn(-i), 0) for i in range(narrow)])

    def group_start(value):
        keep, give = mine_of(value.reshape(bundle, 2, tile, width), 1)
        return ordered(keep, to_core(give), 0)

    def group_back(moved):
        mine, give = mine_of(in_order(moved).reshape(2, bundle, tile, width), 0)
        theirs = to_core(give)
        return ordered(mine[:, None], theirs[:, None], 1).reshape(bundle, row_count, width)

    def split_far(*parts):
        return mine_of(jnp.concatenate(parts, axis=1), 0)

    def two(part):
        return part.reshape(2, part.shape[0] // 2, own_width)

    def canonical(value):
        if chips == BLOCKS:
            return value
        parts = value.reshape((BLOCKS, chips // BLOCKS) + value.shape[1:])
        return jnp.moveaxis(parts, 1, -2).reshape((BLOCKS,) + value.shape[1:-1] + (wide,))

    def scattered(value):
        if chips == BLOCKS:
            return value
        parts = value.reshape(value.shape[:-1] + (chips // BLOCKS, width // chips))
        return jnp.moveaxis(parts, -2, 1).reshape(
            (chips,) + value.shape[1:-1] + (width // chips,)
        )

    def spread(value, *late):
        return across([value] * narrow, (), late)

    near = chips == BLOCKS

    def chips_first(value):
        return (to_chip(value, 1), to_chip(value, 2)) if near else ()

    def chips_second(first, second):
        return to_chip(first[: narrow // 2], 2), to_chip(second[narrow // 2 :], 1)

    def chips_full(value, firsts, seconds):
        if near:
            return jnp.stack([value, *firsts, jnp.concatenate(seconds)])
        return canonical(lax.all_gather(value, "dp", axis_index_groups=same_core))

    def chips_pieces(value, firsts, seconds):
        if near:
            return (value, *firsts, *seconds)
        full = chips_full(value, firsts, seconds)
        return full[0], full[1], full[2], full[3, : narrow // 2], full[3, narrow // 2 :]

    def sum_first(grads):
        x_keep, x_send, y_keep, y_send = grads
        return to_chip(x_send, 1), to_chip(y_send, 2)

    def sum_ready(grads, got):
        x_keep, _, y_keep, _ = grads
        return (
            (x_keep[1].astype(f32) + got[0][1].astype(f32)).astype(bf16),
            (y_keep[1].astype(f32) + got[1][1].astype(f32)).astype(bf16),
        )

    def sum_second(ready):
        return to_chip(ready[0], 2), to_chip(ready[1], 1)

    def sum_done(grads, got, last):
        x_keep, _, y_keep, _ = grads
        x_sum = x_keep[0].astype(f32) + got[0][0].astype(f32) + last[0].astype(f32)
        y_sum = y_keep[0].astype(f32) + got[1][0].astype(f32) + last[1].astype(f32)
        sent = [x_sum[k] for k in range(1, narrow // 2)] + [y_sum[k] for k in range(narrow // 2)]
        return x_sum[0], [None] + [block.astype(bf16) for block in sent]

    def sum_far(grads):
        x_keep, x_send, y_keep, y_send = grads
        x_all = jnp.stack([x_keep, x_send], axis=1).reshape((BLOCKS,) + x_keep.shape[1:])
        y_all = jnp.concatenate([y_keep, y_send])
        value = scattered(
            jnp.concatenate([x_all, y_all], axis=1).reshape(BLOCKS, narrow, -1, wide)
        )
        got = lax.psum_scatter(
            value.reshape(-1, value.shape[-1]),
            "dp",
            scatter_dimension=0,
            tiled=True,
            axis_index_groups=same_core,
        ).reshape(value.shape[1:])
        return got[0].astype(f32), [None] + [got[k] for k in range(1, narrow)]

    def swap_ready(own, got):
        total = own
        for piece in got[1:]:
            total = total + piece.astype(f32)
        low, high = total[:, :own_width], total[:, own_width:]
        return jnp.where(by_core, low, high), jnp.where(by_core, high, low).astype(bf16)

    def finish(keep, theirs, parts, size):
        theirs = theirs.astype(f32)
        both = jnp.where(by_core, jnp.stack([keep, theirs]), jnp.stack([theirs, keep]))
        return [both[:, i * size : (i + 1) * size] for i in range(parts)]

    me = (chip if near else 0 * chip).astype(jnp.int32)[None]
    core_index, place_index = core.astype(jnp.int32)[None], place.astype(jnp.int32)[None]
    kinds = [w_gate.T, w_up.T, w_down]
    depth = w_down.shape[0] // 2
    cut = -(-depth // 32 // 2) * 32
    if near:
        keep, give = square_split_call(
            core_index, bucket, w_query, w_key, w_value, w_out, attn_gain, ffn_gain
        )
    else:
        extra = jnp.concatenate(
            [
                attn_gain[None],
                ffn_gain[None],
                jnp.pad(bucket.astype(bf16), (0, own_width - bundle))[None],
                jnp.zeros((13, own_width), bf16),
            ]
        )
        keep, give = split_far(
            two(w_query.T), two(w_key.T), two(w_value.T), two(w_out), jnp.stack([extra, extra])
        )
        halves = [two(kind) for kind in kinds]
        ffn_keep, ffn_give = split_far(
            *[half[:, :cut] for half in halves], *[half[:, cut:] for half in halves]
        )
    square = ordered(keep, to_core(give), 1)

    square_z = spread(square)
    own_inputs, own_cotangent, kinds, square = stage((inputs, cotangent, kinds, square))
    if near:
        ffn_keep, ffn_give = ffn_split_call(core_index, cut, *kinds)
    x_blocks = blocks_for(group_start(own_inputs))
    cot_blocks = blocks_for(group_start(own_cotangent))
    ffn_theirs = to_core(ffn_give)
    ffn_one = ordered(ffn_keep[: 3 * cut], ffn_theirs[: 3 * cut], 1)
    ffn_two = ordered(ffn_keep[3 * cut :], ffn_theirs[3 * cut :], 1)
    flags = square[4 * 128 + 2].reshape(2, own_width)[:, :bundle].reshape(-1)
    flag = pick(flags.astype(jnp.int32), place, 0)[None]

    square_z, x_blocks, cot_blocks, ffn_one, ffn_two, flag = stage(
        (square_z, x_blocks, cot_blocks, ffn_one, ffn_two, flag)
    )
    square_z = jnp.stack(square_z)
    square_first = chips_first(square_z)
    x_moved = across(x_blocks)

    square_first, x_moved, ffn_one = stage((square_first, x_moved, ffn_one))
    x_own = jnp.stack(x_moved)
    x_other = to_core(x_own)
    square_second = chips_second(*square_first) if near else ()
    one_z = spread(ffn_one, x_other)
    x_rows, hidden, rms, gains, square_full, q, k, v = qkv_call(
        me,
        core_index,
        place_index,
        x_own,
        x_other,
        chips_pieces(square_z, square_first, square_second),
    )

    q, one_z, cot_blocks = stage((q, one_z, cot_blocks))
    one_z = jnp.stack(one_z)
    one_first = chips_first(one_z)
    cot_moved = across(cot_blocks)
    attended, probs = attend_call(flag, q, k, v)

    attended, one_first, cot_moved, ffn_two = stage((attended, one_first, cot_moved, ffn_two))
    one_second = chips_second(*one_first) if near else ()
    branch = branch_call(me, attended, square_full)
    cot_own = jnp.stack(cot_moved)
    two_z = spread(ffn_two, branch)
    middle_place = narrow // 2
    branch, cot_own, one_second, two_near = stage(
        (branch, cot_own, one_second, two_z[:middle_place] + two_z[middle_place + 1 :])
    )
    two_z = two_near[:middle_place] + [two_z[middle_place]] + two_near[middle_place:]
    branch_other, cot_other = to_core(branch), to_core(cot_own)
    middle, normed, cot_rows = middle_call(
        core_index, place_index, x_rows, branch, branch_other, gains, cot_own, cot_other
    )

    normed, two_z = stage((normed, two_z))
    two_z = jnp.stack(two_z)
    two_first = chips_first(two_z)
    part_result, part_d_normed, *one_grads = ffn_call(
        me, core_index, narrow, normed, cot_rows, chips_pieces(one_z, one_first, one_second)
    )

    part_result, part_d_normed, one_grads, two_first = stage(
        (part_result, part_d_normed, one_grads, two_first)
    )
    two_second = chips_second(*two_first) if near else ()

    part_result, part_d_normed, one_grads, two_second = stage(
        (part_result, part_d_normed, one_grads, two_second)
    )
    one_got = sum_first(one_grads) if near else ()
    result, d_normed, *two_grads, result_give = ffn_call(
        me,
        core_index,
        narrow,
        normed,
        cot_rows,
        chips_pieces(two_z, two_first, two_second),
        part_result,
        part_d_normed,
    )

    result_give, d_normed, one_got, two_grads = stage((result_give, d_normed, one_got, two_grads))
    by_rows = (narrow, 2, tile, width)
    d_normed_other, result_other = to_core(d_normed), to_core(result_give)
    one_last = sum_second(sum_ready(one_grads, one_got)) if near else ()
    d_middle, d_branch, d_att, ffn_gain_grad, out_rows = turn_call(
        me,
        core_index,
        middle,
        d_normed,
        d_normed_other,
        cot_rows,
        gains,
        square_full,
        result.reshape(by_rows),
        result_other,
    )
    out_moved = across(blocks_for(out_rows))

    d_att, one_last, two_grads = stage((d_att, one_last, two_grads))
    two_got = sum_first(two_grads) if near else ()
    pairs = d_att.shape[1] // 256
    lefts_one = attend_back_call(0, pairs, flag, q, k, v, attended, d_att, probs)

    lefts_one, d_att, one_grads, one_got, one_last, two_grads, two_got = stage(
        (lefts_one, d_att, one_grads, one_got, one_last, two_grads, two_got), near_of(out_moved)
    )
    two_last = sum_second(sum_ready(two_grads, two_got)) if near else ()
    one_own, one_sent = sum_done(one_grads, one_got, one_last) if near else sum_far(one_grads)
    lefts_two = attend_back_call(pairs, pairs, flag, q, k, v, attended, d_att, probs)
    one_near = across_near(one_sent, -1)

    lefts_two, two_last, out_moved, one_near, one_far = stage(
        (lefts_two, two_last, out_moved, one_near, one_sent[far_place])
    )
    one_places = joined(None, one_near, across_far(one_far, -1))
    two_own, two_sent = sum_done(two_grads, two_got, two_last) if near else sum_far(two_grads)
    two_sent[0] = two_own
    two_places = across(two_sent, (), (), -1)
    lefts = [left for both in zip(lefts_one, lefts_two) for left in both]
    d_hidden, d_hidden_give, *square_grads = square_call(
        me, core_index, lefts, attended, hidden, d_branch, square_full, x_rows, rms, 0.5 * ffn_gain_grad
    )

    d_hidden_give, square_grads, out_moved = stage(
        (d_hidden_give, square_grads, out_moved), near_of(two_places), one_places[far_place]
    )
    square_got = sum_first(square_grads) if near else ()
    d_hidden_other = to_core(d_hidden_give)
    input_blocks = blocks_for(
        input_call(
            core_index, x_rows, d_middle, d_hidden.reshape(by_rows), d_hidden_other, gains
        )
    )
    input_near = across_near(input_blocks)
    outputs = group_back(out_moved)
    one_keep, one_swap = swap_ready(one_own, one_places)

    square_got, one_swap, input_near, input_far, two_places = stage(
        (square_got, one_swap, input_near, input_blocks[far_place], two_places)
    )
    input_moved = joined(input_blocks[0], input_near, across_far(input_far))
    square_last = sum_second(sum_ready(square_grads, square_got)) if near else ()
    one_theirs = to_core(one_swap)
    two_keep, two_swap = swap_ready(two_own, two_places)

    square_last, input_moved, two_swap = stage((square_last, input_moved, two_swap))
    square_own, square_sent = (
        sum_done(square_grads, square_got, square_last) if near else sum_far(square_grads)
    )
    square_places = across(square_sent, (), (), -1)
    two_theirs = to_core(two_swap)
    input_grad = group_back(input_moved).astype(f32)
    one_parts = finish(one_keep, one_theirs, 3, cut)
    two_parts = finish(two_keep, two_theirs, 3, depth - cut)
    g_gate, g_up, g_down = [
        jnp.concatenate(parts, axis=1).reshape(2 * depth, own_width)
        for parts in zip(one_parts, two_parts)
    ]
    g_gate, g_up = g_gate.T, g_up.T
    square_places, outputs, input_grad, g_gate, g_up, g_down = stage(
        (square_places, outputs, input_grad, g_gate, g_up, g_down)
    )
    square_keep, square_swap = swap_ready(square_own, square_places)
    square_theirs = to_core(square_swap)
    g_query, g_key, g_value, g_out = [
        part.reshape(-1, own_width) for part in finish(square_keep, square_theirs, 4, 128)
    ]
    gain_own = square_keep[4 * 128 :] + square_theirs[4 * 128 :].astype(f32)
    return (
        outputs,
        input_grad,
        gain_own[0],
        g_query.T,
        g_key.T,
        g_value.T,
        g_out,
        gain_own[1],
        g_gate,
        g_up,
        g_down,
    )


def solution(mesh):
    rows = P("dp", "narrow", None)
    tall, flat = P("dp", "narrow"), P("narrow", "dp")
    return jax.shard_map(
        per_device,
        mesh=mesh,
        in_specs=(rows, P("dp"), P("dp"), tall, tall, tall, flat, P("dp"), tall, tall, flat, rows),
        out_specs=(rows, rows, P("dp"), tall, tall, tall, flat, P("dp"), tall, tall, flat),
        check_vma=False,
    )
```
